32 devices in a mesh: expert: 8 (over y, x, core), replica: 4 (over z).
Axes of the slice: x: 2, y: 2, z: 4, core: 2. Of those that a mesh axis runs over, the one named last changes fastest.
Arguments:
- tokens: bfloat16 [4096, 2048], P(('replica', 'expert')), parts along dimension 0, may hold values from -6 to 6
- expert_ids: int32 [4096, 8], P(('replica', 'expert')), parts along dimension 0, may hold values from 0 to 127, all different within a row; in each aligned block of 128 rows (0 to 127, 128 to 255, ...) at most 12 rows name the same one
- combine: float32 [4096, 8], P(('replica', 'expert')), parts along dimension 0, may hold values from 0.25 to 1
- old_gate: bfloat16 [1536, 2048], P('expert'), may hold values from -0.125 to 0.125
- old_up: bfloat16 [1536, 2048], P('expert'), may hold values from -0.125 to 0.125
- old_down: bfloat16 [1536, 2048], P('expert'), may hold values from -0.21875 to 0.21875
- move_plan: int32 [2, 3, 96], replicated, may hold values from -1 to 191, as said below
Outputs:
- mixed: bfloat16 [4096, 2048], P(('replica', 'expert')), parts along dimension 0
- arrived: bfloat16 [12, 768, 2048], P('replica', 'expert'), parts along dimension 0
The draws below stay inside these ranges and needn't reach their ends.
There are 4 independent parts, one for each index of `replica`. The reference program is written for one: setup_inputs(seed, part) draws one part's arguments, and reference() takes and returns one part's arrays. A program takes and returns all parts, laid end to end along the dimension named above; an argument that names none is the same for every part. Nothing has to cross between parts.
Inputs may be any that keep to these rules, and one draw needn't show every extreme that they name: `expert_ids`: each row names 8 different experts; among the 128 rows of one device no expert is named more than 12 times, a bound that some block reaches. `move_plan`: in each group the non-negative entries over the three survivors name every one of the leaving device's 192 rows exactly once; each survivor's entries fill its slots from the first, -1 after them; every survivor receives at least 24 rows; in every draw some survivor receives 96 rows.
All inputs are finite; a program needn't handle non-finite values.
Results may differ from the reference program's by a relative error of at most 0.0058.
Values may be sent and summed in bfloat16 or wider, within the bound.
No kernel may reach another device: no remote copies, remote signals or barrier semaphores. Data moves between devices by JAX's collectives and lax.ppermute only.
A program may use at most 128 MiB of HBM per device.

```python
import math
import jax
import jax.numpy as jnp
import numpy as np
from jax import lax

D = 2048
HIDDEN_UNITS = 768
EXPERTS_ALL = 128
TOPK = 8
TOK_DEV = 128
TOKENS = 1024
EXPERTS_WIN = 2
OLD_ROWS = 192
MOVE_MAX = 96
CAP = 12
N_EXPERT = 8


def draw_move_plan(key, part):
    key = jax.random.fold_in(key, 7)
    key_perm, key_first, key_second, key_full = jax.random.split(key, 4)
    group_keys = jax.random.split(key_perm, EXPERTS_WIN)
    permutations = jax.vmap(lambda one_key: jax.random.permutation(one_key, OLD_ROWS))(group_keys)
    least_rows = max(1, MOVE_MAX // 4)
    leading_count = jax.random.randint(key_first, (EXPERTS_WIN,), least_rows, MOVE_MAX + 1)
    full_group = jax.random.randint(key_full, (), 0, EXPERTS_WIN)
    leading_count = jnp.where(jnp.arange(EXPERTS_WIN) == full_group, MOVE_MAX, leading_count)
    second_low = jnp.maximum(MOVE_MAX - leading_count, least_rows)
    second_high = jnp.minimum(MOVE_MAX, OLD_ROWS - leading_count - least_rows)
    second_count = jax.random.randint(key_second, (EXPERTS_WIN,), second_low, second_high + 1)
    trailing_count = OLD_ROWS - leading_count - second_count
    counts = jnp.stack([leading_count, second_count, trailing_count], axis=1)
    starts = jnp.stack([jnp.zeros_like(leading_count), leading_count, leading_count + second_count], axis=1)
    slot_range = jnp.arange(MOVE_MAX)
    take_index = jnp.minimum(starts[:, :, None] + slot_range[None, None, :], OLD_ROWS - 1)
    spread = jnp.broadcast_to(permutations[:, None, :], (EXPERTS_WIN, 3, OLD_ROWS))
    chosen = jnp.take_along_axis(spread, take_index, axis=2)
    return jnp.where(slot_range[None, None, :] < counts[:, :, None], chosen, -1).astype(jnp.int32)


def shard_levels(stream_key, extent, pieces, low, largest):
    gain = 1.0
    for dim, blocks in pieces:
        draws = jax.random.uniform(jax.random.fold_in(jax.random.fold_in(stream_key, 6), dim), (blocks,), jnp.float32, low / len(pieces), largest / len(pieces))
        gain = gain * jnp.repeat(jnp.exp(draws), extent[dim] // blocks).reshape((-1,) + (1,) * (len(extent) - 1 - dim))
    return gain


def shared_out(rng, own, number, rows, count, top, most, slope):
    ranking = jax.random.permutation(rng, count)
    crowded, common = shares(count, rows * top, most, slope, True), shares(count, rows * top, most, slope, False)
    places = jnp.arange(count)

    def named(lengths, offset_by):
        used = int((lengths > 0).sum())
        fixed = max(1, used // 4)
        moved = fixed + (places - fixed + offset_by * (used - fixed)) % max(1, count - fixed)
        return jnp.zeros((count,), jnp.int32).at[ranking[jnp.where(places < fixed, places, moved)]].set(jnp.asarray(lengths, jnp.int32))

    lengths = jnp.where(number % 4 == 0, named(crowded, number // 4), named(common, number - number // 4 - 1))
    mixed = jax.random.permutation(jax.random.fold_in(own, 3), count)
    giver, sink = mixed[0:count // 2 * 2:2], mixed[1:count // 2 * 2:2]
    room = jnp.minimum(lengths[giver] - 1, most - lengths[sink]) // 2
    room = jnp.where((giver == ranking[0]) | (sink == ranking[0]) | (lengths[sink] == 0), 0, jnp.maximum(room, 0))
    moved = jax.random.randint(jax.random.fold_in(own, 4), (count // 2,), 0, 1 << 20) % (room + 1)
    lengths = lengths.at[giver].add(-moved).at[sink].add(moved)
    labels = jnp.searchsorted(jnp.cumsum(lengths), jnp.arange(rows * top), side="right").astype(jnp.int32)
    table = labels.reshape(top, rows).T
    table = table[jax.random.permutation(jax.random.fold_in(own, 1), rows)]
    offset_by = jax.random.randint(jax.random.fold_in(own, 2), (rows, 1), 0, top)
    return jnp.take_along_axis(table, (jnp.arange(top)[None, :] + offset_by) % top, axis=1)


def shares(count, total, most, lean, full):
    portions = [(1 << 20) // math.isqrt(standing ** lean) + 1 for standing in range(1, count + 1)]
    largest = most if full else min(most, max(-(-total // count), total * portions[0] // sum(portions)))
    least = 1 if total - largest >= count - 1 else 0
    given, rest = [largest] + [least] * (count - 1), total - largest - least * (count - 1)
    while rest > 0:
        candidates = [i for i in range(1, count) if given[i] < largest] or [i for i in range(1, count) if given[i] < most]
        mass, budget = sum([portions[i] for i in candidates]), rest
        for i in candidates:
            more = min(most - given[i], max(1, budget * portions[i] // mass), rest)
            given[i] = given[i] + more
            rest = rest - more
    return np.array(given)


def gaussian(stream_key, dims, scale, bound, shards=(), held_as=jnp.bfloat16):
    gain = shard_levels(stream_key, dims, shards, -0.22, 0.18) if shards else 1.0
    array = jax.random.normal(stream_key, dims, jnp.float32) * scale * gain
    return jnp.minimum(jnp.maximum(array, -bound), bound).astype(held_as)


def setup_inputs(seed: int = 0, part: int = 0) -> dict:
    splits = jax.random.split(jax.random.key(seed), 8)
    part_splits = jax.random.split(jax.random.fold_in(splits[7], part), 8)
    tokens = gaussian(part_splits[0], (TOKENS, D), 1.0, 6.0, ((0, 8),))
    expert_ids_keys = jax.random.split(jax.random.fold_in(part_splits[1], 1), TOKENS // TOK_DEV)
    expert_ids_turns = jax.random.permutation(jax.random.fold_in(part_splits[1], 3), TOKENS // TOK_DEV)
    expert_ids = jax.vmap(lambda own, number: shared_out(jax.random.fold_in(part_splits[1], 2), own, number, TOK_DEV, EXPERTS_ALL, TOPK, CAP, 2))(expert_ids_keys, expert_ids_turns).reshape((TOKENS, TOPK))
    combine = jnp.clip(0.25 + 0.75 * jax.random.uniform(part_splits[2], (TOKENS, TOPK), jnp.float32) ** shard_levels(part_splits[2], (TOKENS, TOPK), ((0, 8),), -0.2, 0.2), 0.25, 1.0)
    old_gate = gaussian(splits[3], (N_EXPERT * OLD_ROWS, D), D ** -0.5, 0.125, ((0, 8),))
    old_up = gaussian(splits[4], (N_EXPERT * OLD_ROWS, D), D ** -0.5, 0.125, ((0, 8),))
    old_down = gaussian(splits[5], (N_EXPERT * OLD_ROWS, D), HIDDEN_UNITS ** -0.5, 0.21875, ((0, 8),))
    move_plan = draw_move_plan(jax.random.fold_in(splits[7], 71), part)
    return {"tokens": tokens, "expert_ids": expert_ids, "combine": combine, "old_gate": old_gate, "old_up": old_up, "old_down": old_down, "move_plan": move_plan}


def reference(tokens, expert_ids, combine, old_gate, old_up, old_down, move_plan):
    old_all = jnp.stack([old_gate, old_up, old_down], axis=0)
    model_width = tokens.shape[1]
    leaver_base = (jnp.arange(EXPERTS_WIN, dtype=jnp.int32) * 4 + 3) * OLD_ROWS
    plan_rows = (leaver_base[:, None, None] + jnp.maximum(move_plan, 0)).astype(jnp.int32)
    gathered = jnp.take(old_all, plan_rows.reshape(-1), axis=1).reshape(3, EXPERTS_WIN, 3, MOVE_MAX, model_width)
    gathered = jnp.where((move_plan >= 0)[None, :, :, :, None], gathered, jnp.zeros((), old_all.dtype))
    padded = jnp.concatenate([gathered, jnp.zeros((3, EXPERTS_WIN, 1, MOVE_MAX, model_width), old_all.dtype)], axis=2)
    arrived = padded.reshape(3, EXPERTS_WIN * 4 * MOVE_MAX, model_width)

    flat_ids = expert_ids.reshape(-1)
    flat_weights = combine.reshape(-1)
    limit = N_EXPERT * CAP
    numbers = (((1,), (1,)), ((), ()))

    def one_expert(accumulated, expert_number):
        chosen_mask = flat_ids == expert_number
        positions = jnp.nonzero(chosen_mask, size=limit, fill_value=0)[0].astype(jnp.int32)
        live_slot = jnp.arange(limit) < jnp.sum(chosen_mask.astype(jnp.int32))
        token_rows = (positions // TOPK).astype(jnp.int32)
        inputs = jnp.take(tokens, token_rows, axis=0)
        expert_sum = jnp.zeros((limit, model_width), jnp.float32)
        for remaining_device in range(3):
            owning_device = (4 * expert_number + remaining_device).astype(jnp.int32)
            resident = lax.dynamic_slice_in_dim(old_all, (owning_device * OLD_ROWS).astype(jnp.int32), OLD_ROWS, 1)
            extra_rows = lax.dynamic_slice_in_dim(arrived, (owning_device * MOVE_MAX).astype(jnp.int32), MOVE_MAX, 1)
            held_rows = jnp.concatenate([resident, extra_rows], axis=1)
            gate_value = lax.dot_general(inputs, held_rows[0], numbers, preferred_element_type=jnp.float32)
            up_value = lax.dot_general(inputs, held_rows[1], numbers, preferred_element_type=jnp.float32)
            hidden = (jax.nn.silu(gate_value) * up_value).astype(jnp.bfloat16)
            partial_value = jnp.dot(hidden, held_rows[2], preferred_element_type=jnp.float32).astype(jnp.bfloat16)
            partial_value = lax.optimization_barrier(partial_value)
            expert_sum = expert_sum + partial_value.astype(jnp.float32)
        scales = jnp.where(live_slot, jnp.take(flat_weights, positions), jnp.zeros((), flat_weights.dtype))
        contribution = expert_sum * scales[:, None].astype(jnp.float32)
        accumulated = accumulated.at[token_rows].add(contribution)
        return accumulated, None

    start = jnp.zeros((tokens.shape[0], model_width), jnp.float32)
    accumulated, _ = lax.scan(one_expert, start, jnp.arange(EXPERTS_WIN, dtype=jnp.int32))
    return accumulated.astype(jnp.bfloat16), arrived
```

```python
import functools

import jax
import jax.numpy as jnp
from jax import lax
from jax.experimental import pallas as pl
from jax.experimental.pallas import tpu as pltpu
from jax.sharding import PartitionSpec as P

CAP = 12
SLOTS = 16
GROUP = 4
BF16 = jnp.bfloat16
F32 = jnp.float32
VMEM = pl.BlockSpec(memory_space=pltpu.VMEM)
SMEM = pl.BlockSpec(memory_space=pltpu.SMEM)
HBM = pl.BlockSpec(memory_space=pl.ANY)


def params():
    return pltpu.CompilerParams(vmem_limit_bytes=40 * 1024 * 1024)


def slot_matrix(ids, group, experts):
    tok = ids.shape[1]
    member = []
    for j in range(experts):
        expert = lax.rem(group + j, experts)
        named = jnp.where(ids == expert, 1.0, 0.0)
        member.append(jnp.sum(named, axis=0, keepdims=True))
    member = jnp.concatenate(member, axis=0)
    row = lax.broadcasted_iota(jnp.int32, (tok, tok), 0)
    col = lax.broadcasted_iota(jnp.int32, (tok, tok), 1)
    upto = jnp.where(row <= col, 1.0, 0.0).astype(BF16)
    rank = jnp.dot(member.astype(BF16), upto, preferred_element_type=F32)
    place = jnp.where(member > 0, rank - 1.0, -1.0).astype(jnp.int32)
    slot = lax.broadcasted_iota(jnp.int32, (SLOTS, tok), 0)
    blocks = [jnp.where(slot == place[j : j + 1, :], 1.0, 0.0) for j in range(experts)]
    return jnp.concatenate(blocks, axis=0)


def dispatch_kernel(experts, where_ref, ids_ref, tok_ref, own_ref, other_ref):
    chosen = slot_matrix(ids_ref[...], where_ref[0], experts).astype(BF16)
    rows = jnp.dot(chosen, tok_ref[...], preferred_element_type=F32).astype(BF16)
    own_ref[...] = rows[:SLOTS]
    other_ref[...] = rows[SLOTS:].reshape(other_ref.shape)


def select_kernel(where_ref, plan_ref, gate_ref, up_ref, down_ref, *out_refs):
    group = where_ref[0]
    rows = gate_ref.shape[0]
    most = plan_ref.shape[2]

    @pl.when(where_ref[1] == GROUP - 1)
    def _():
        number = lax.broadcasted_iota(jnp.int32, (rows, most), 0)
        for p in range(GROUP - 1):
            plan = plan_ref[p, pl.ds(group, 1), :]
            pick = jnp.where(number == plan, 1.0, 0.0).astype(BF16)
            for m, ref in enumerate((gate_ref, up_ref, down_ref)):
                out_refs[p][m] = lax.dot_general(
                    pick, ref[...], (((0,), (0,)), ((), ())), preferred_element_type=F32
                ).astype(BF16)


def merge_kernel(where_ref, first_ref, second_ref, third_ref, out_ref, sems):
    position = where_ref[1]
    for p, ref in ((1, second_ref), (2, third_ref)):

        @pl.when(position == p)
        def _():
            copies = [
                pltpu.make_async_copy(ref.at[m], out_ref.at[m], sems.at[m]) for m in range(3)
            ]
            for copy in copies:
                copy.start()
            for copy in copies:
                copy.wait()


def expert_kernel(*refs):
    x_refs, (gate_ref, up_ref, down_ref), out_refs = refs[:4], refs[4:7], refs[7:]
    rows = x_refs[0].shape[0]
    x = jnp.concatenate([ref[...] for ref in x_refs], axis=0)
    numbers = (((1,), (1,)), ((), ()))
    gate_value = lax.dot_general(x, gate_ref[...], numbers, preferred_element_type=F32)
    up_value = lax.dot_general(x, up_ref[...], numbers, preferred_element_type=F32)
    hidden = (gate_value / (1.0 + jnp.exp(-gate_value)) * up_value).astype(BF16)
    partial = jnp.dot(hidden, down_ref[...], preferred_element_type=F32).astype(BF16)
    for k, ref in enumerate(out_refs):
        ref[...] = partial[k * rows : (k + 1) * rows]


def combine_kernel(experts, where_ref, ids_ref, weight_ref, own_ref, back_ref, out_ref):
    ids = ids_ref[...]
    group = where_ref[0]
    chosen = slot_matrix(ids, group, experts)
    scale = []
    for j in range(experts):
        expert = lax.rem(group + j, experts)
        weight = jnp.sum(
            jnp.where(ids == expert, weight_ref[...], 0.0), axis=0, keepdims=True
        )
        block = chosen[j * SLOTS : (j + 1) * SLOTS]
        scale.append(jnp.sum(block * weight, axis=1, keepdims=True))
    scale = jnp.concatenate(scale, axis=0)
    back = back_ref[...].reshape(-1, back_ref.shape[-1]).astype(F32)
    value = jnp.concatenate([own_ref[...], back], axis=0) * scale
    high = value.astype(BF16)
    rest = value - high.astype(F32)
    middle = rest.astype(BF16)
    low = (rest - middle.astype(F32)).astype(BF16)
    parts = jnp.concatenate([high, middle, low], axis=0)
    chosen = chosen.astype(BF16)
    chosen = jnp.concatenate([chosen] * 3, axis=0)
    out_ref[...] = lax.dot_general(
        chosen, parts, (((0,), (0,)), ((), ())), preferred_element_type=F32
    ).astype(BF16)


def on_device(tokens, expert_ids, combine, old_gate, old_up, old_down, move_plan):
    devices = lax.axis_size("expert")
    experts = move_plan.shape[0]
    most = move_plan.shape[2]
    width = tokens.shape[1]
    device = lax.axis_index("expert")
    group, position = device // GROUP, device % GROUP
    where = jnp.stack([group, position]).astype(jnp.int32)
    ids = expert_ids.T
    weights = combine.T
    plan = jnp.transpose(move_plan, (1, 0, 2))

    def shape(*dims, dtype=BF16):
        return jax.ShapeDtypeStruct(dims, dtype)

    def permute(block, target):
        return lax.ppermute(block, "expert", [(i, target(i)) for i in range(devices)])

    own, others = pl.pallas_call(
        functools.partial(dispatch_kernel, experts),
        out_shape=(shape(SLOTS, width), shape(experts - 1, SLOTS, width)),
        in_specs=[SMEM, VMEM, VMEM],
        out_specs=(VMEM, VMEM),
        compiler_params=params(),
        name="dispatch",
    )(where, ids, tokens)

    chosen = pl.pallas_call(
        select_kernel,
        out_shape=[shape(3, most, width)] * 3,
        in_specs=[SMEM, VMEM, VMEM, VMEM, VMEM],
        out_specs=[VMEM] * 3,
        compiler_params=params(),
        name="select",
    )(where, plan, old_gate, old_up, old_down)

    across = [
        permute(others[j - 1], lambda i: (i + GROUP * j) % devices) for j in range(1, experts)
    ]
    here = jnp.concatenate([own] + across, axis=0)
    rows = [here] + [permute(here, lambda i: i ^ k) for k in (1, 2, 3)]

    landed = [
        lax.ppermute(
            chosen[p],
            "expert",
            [(GROUP * e + GROUP - 1, GROUP * e + p) for e in range(experts)],
        )
        for p in range(GROUP - 1)
    ]

    step = min(experts * SLOTS, 32)
    row_spec = pl.BlockSpec((step, width), lambda i: (i, 0))
    whole_spec = pl.BlockSpec(old_gate.shape, lambda i: (0, 0))
    partial = pl.pallas_call(
        expert_kernel,
        grid=(experts * SLOTS // step,),
        out_shape=[shape(experts * SLOTS, width)] * 4,
        in_specs=[row_spec] * 4 + [whole_spec] * 3,
        out_specs=[row_spec] * 4,
        compiler_params=params(),
        name="expert",
    )(*rows, old_gate, old_up, old_down)
    total = partial[0].astype(F32)
    for k in (1, 2, 3):
        total = total + permute(partial[k], lambda i: i ^ k).astype(F32)
    total = total.reshape(experts, SLOTS, width)
    back = jnp.stack(
        [
            permute(total[j].astype(BF16), lambda i: (i - GROUP * j) % devices)
            for j in range(1, experts)
        ]
    )
    mixed = pl.pallas_call(
        functools.partial(combine_kernel, experts),
        out_shape=shape(tokens.shape[0], width),
        in_specs=[SMEM, VMEM, VMEM, VMEM, VMEM],
        out_specs=VMEM,
        compiler_params=params(),
        name="combine",
    )(where, ids, weights, total[0], back)

    arrived = pl.pallas_call(
        merge_kernel,
        out_shape=shape(3, most, width),
        in_specs=[SMEM, HBM, HBM, HBM],
        out_specs=HBM,
        input_output_aliases={1: 0},
        scratch_shapes=[pltpu.SemaphoreType.DMA((3,))],
        compiler_params=params(),
        name="merge",
    )(where, *landed)
    return mixed, arrived


def solution(mesh):
    placed = (
        P(("replica", "expert"), None),
        P(("replica", "expert"), None),
        P(("replica", "expert"), None),
        P("expert", None),
        P("expert", None),
        P("expert", None),
        P(),
    )
    return jax.shard_map(
        on_device,
        mesh=mesh,
        in_specs=placed,
        out_specs=(P(("replica", "expert"), None), P("replica", "expert", None)),
        check_vma=False,
    )
```

```python
import functools

import jax
import jax.numpy as jnp
from jax import lax
from jax.experimental import pallas as pl
from jax.experimental.pallas import tpu as pltpu
from jax.sharding import PartitionSpec as P

CAP = 12
SLOTS = 16
GROUP = 4
BF16 = jnp.bfloat16
F32 = jnp.float32
VMEM = pl.BlockSpec(memory_space=pltpu.VMEM)
SMEM = pl.BlockSpec(memory_space=pltpu.SMEM)
HBM = pl.BlockSpec(memory_space=pl.ANY)


def params(megabytes=40):
    return pltpu.CompilerParams(vmem_limit_bytes=megabytes * 1024 * 1024)


def slot_matrix(ids, group, experts):
    tok = ids.shape[1]
    member = []
    for j in range(experts):
        expert = lax.rem(group + j, experts)
        named = jnp.where(ids == expert, 1.0, 0.0)
        member.append(jnp.sum(named, axis=0, keepdims=True))
    member = jnp.concatenate(member, axis=0)
    row = lax.broadcasted_iota(jnp.int32, (tok, tok), 0)
    col = lax.broadcasted_iota(jnp.int32, (tok, tok), 1)
    upto = jnp.where(row <= col, 1.0, 0.0).astype(BF16)
    rank = jnp.dot(member.astype(BF16), upto, preferred_element_type=F32)
    place = jnp.where(member > 0, rank - 1.0, -1.0).astype(jnp.int32)
    slot = lax.broadcasted_iota(jnp.int32, (SLOTS, tok), 0)
    blocks = [jnp.where(slot == place[j : j + 1, :], 1.0, 0.0) for j in range(experts)]
    return jnp.concatenate(blocks, axis=0)


def dispatch_kernel(experts, where_ref, ids_ref, tok_hbm, *refs):
    out_refs, (tok_ref, sem) = refs[:experts], refs[experts:]
    copy = pltpu.make_async_copy(tok_hbm, tok_ref, sem)
    copy.start()
    chosen = slot_matrix(ids_ref[...], where_ref[0], experts).astype(BF16)
    copy.wait()
    rows = jnp.dot(chosen, tok_ref[...], preferred_element_type=F32).astype(BF16)
    for j, ref in enumerate(out_refs):
        ref[...] = rows[j * SLOTS : (j + 1) * SLOTS]


def pick_rows(number, plan, held_ref):
    pick = jnp.where(number == plan, 1.0, 0.0).astype(BF16)
    return lax.dot_general(
        pick, held_ref[...], (((0,), (0,)), ((), ())), preferred_element_type=F32
    ).astype(BF16)


def select_kernel(wanted, where_ref, plan_ref, gate_hbm, up_hbm, down_hbm, after_ref, *refs):
    out_refs, (held_ref, sems) = refs[: len(wanted)], refs[len(wanted) :]
    group = where_ref[0]
    rows = held_ref.shape[1]
    parity = where_ref[2]

    @pl.when(where_ref[1] == GROUP - 1)
    def _():
        copies = [
            pltpu.make_async_copy(ref, held_ref.at[m], sems.at[m])
            for m, ref in enumerate((gate_hbm, up_hbm, down_hbm))
        ]
        for copy in copies:
            copy.start()
        plans = []
        for survivor, first, count in wanted:
            plan = plan_ref[survivor, pl.ds(group, 1), :]
            if first is None:
                plan = jnp.where(parity == 0, plan[:, :count], plan[:, count : 2 * count])
            else:
                plan = plan[:, first : first + count]
            plans.append(plan)
        width = sum(count for _, _, count in wanted)
        number = lax.broadcasted_iota(jnp.int32, (rows, width), 0)
        pick = jnp.where(number == jnp.concatenate(plans, axis=1), 1.0, 0.0).astype(BF16)
        for m, copy in enumerate(copies):
            copy.wait()
            found = lax.dot_general(
                pick, held_ref[m], (((0,), (0,)), ((), ())), preferred_element_type=F32
            ).astype(BF16)
            start = 0
            for (_, _, count), ref in zip(wanted, out_refs):
                ref[m] = found[start : start + count]
                start += count


def merge_kernel(part, where_ref, *refs):
    shared, swapped, straight, near = refs[0:2], refs[2:4], refs[4:6], refs[6]
    out_ref, sems = refs[7:]
    position, parity = where_ref[1], where_ref[2]

    def move(pieces):
        copies = []
        for ref, first, count in pieces:
            for m in range(3):
                copies.append(
                    pltpu.make_async_copy(
                        ref.at[m], out_ref.at[m, pl.ds(first, count)], sems.at[len(copies)]
                    )
                )
        for copy in copies:
            copy.start()
        for copy in copies:
            copy.wait()

    for p in range(2):
        for even in range(2):
            mine = position == 1 if p == 1 else jnp.logical_or(position == 0, position == 3)

            @pl.when(jnp.logical_and(mine, parity == even))
            def _():
                move(
                    [
                        (shared[p], part * even, part),
                        (swapped[p], part * (1 - even), part),
                        (straight[p], 2 * part, out_ref.shape[1] - 2 * part),
                    ]
                )

    @pl.when(position == 2)
    def _():
        move([(near, 0, out_ref.shape[1])])


def expert_kernel(pieces, *refs):
    x_refs, (gate_ref, up_ref, down_ref), out_refs = (
        refs[:pieces],
        refs[pieces : pieces + 3],
        refs[pieces + 3 :],
    )
    x = jnp.concatenate([ref[...] for ref in x_refs], axis=0)
    numbers = (((1,), (1,)), ((), ()))
    gate_value = lax.dot_general(x, gate_ref[...], numbers, preferred_element_type=F32)
    up_value = lax.dot_general(x, up_ref[...], numbers, preferred_element_type=F32)
    hidden = (gate_value / (1.0 + jnp.exp(-gate_value)) * up_value).astype(BF16)
    partial = jnp.dot(hidden, down_ref[...], preferred_element_type=F32).astype(BF16)
    for k, ref in enumerate(out_refs):
        ref[...] = partial[k * SLOTS : (k + 1) * SLOTS]


def combine_kernel(experts, where_ref, ids_ref, weight_ref, *refs):
    piece_refs, out_ref = refs[: experts * GROUP], refs[experts * GROUP]
    ids = ids_ref[...]
    group = where_ref[0]
    tok = ids.shape[0]
    row = lax.broadcasted_iota(jnp.int32, (tok, tok), 0)
    col = lax.broadcasted_iota(jnp.int32, (tok, tok), 1)
    upto = jnp.where(col <= row, 1.0, 0.0).astype(BF16)
    slot = lax.broadcasted_iota(jnp.int32, (tok, GROUP * SLOTS), 1) % SLOTS
    mixed = None
    for j in range(experts):
        named = ids == lax.rem(group + j, experts)
        member = jnp.sum(jnp.where(named, 1.0, 0.0), axis=1, keepdims=True)
        weight = jnp.sum(jnp.where(named, weight_ref[...], 0.0), axis=1, keepdims=True)
        rank = jnp.dot(upto, member.astype(BF16), preferred_element_type=F32)
        place = jnp.where(member > 0, rank - 1.0, -1.0).astype(jnp.int32)
        chosen = jnp.where(slot == place, 1.0, 0.0).astype(BF16)
        parts = [ref[...] for ref in piece_refs[j * GROUP : (j + 1) * GROUP]]
        found = jnp.dot(
            chosen, jnp.concatenate(parts, axis=0), preferred_element_type=F32
        )
        term = weight * found
        mixed = term if mixed is None else mixed + term
    out_ref[...] = mixed.astype(BF16)


def on_device(tokens, expert_ids, combine, old_gate, old_up, old_down, move_plan):
    devices = lax.axis_size("expert")
    replicas = lax.axis_size("replica")
    experts = move_plan.shape[0]
    most = move_plan.shape[2]
    width = tokens.shape[1]
    device = lax.axis_index("expert")
    group, position = device // GROUP, device % GROUP
    parity = lax.axis_index("replica") % 2
    where = jnp.stack([group, position, parity]).astype(jnp.int32)
    plan = jnp.transpose(move_plan, (1, 0, 2))
    weights = (old_gate, old_up, old_down)
    part = most // 3
    rest = most - 2 * part

    def shape(*dims, dtype=BF16):
        return jax.ShapeDtypeStruct(dims, dtype)

    def send(block, j, k):
        route = []
        for i in range(devices):
            g, p = i // GROUP, i % GROUP
            route.append((i, GROUP * ((g + j) % experts) + (p ^ k)))
        return lax.ppermute(block, "expert", route)

    def migrate(block, survivor):
        route = [(GROUP * e + GROUP - 1, GROUP * e + survivor) for e in range(experts)]
        return lax.ppermute(block, "expert", route)

    def swap(block, survivor):
        route = []
        for r in range(replicas):
            for e in range(experts):
                i = GROUP * e + survivor
                route.append((i * replicas + r, i * replicas + (r ^ 1)))
        return lax.ppermute(block, ("expert", "replica"), route)

    def select(wanted, after, name):
        return pl.pallas_call(
            functools.partial(select_kernel, wanted),
            out_shape=[shape(3, count, width) for _, _, count in wanted],
            in_specs=[SMEM, VMEM, HBM, HBM, HBM, HBM],
            out_specs=[VMEM] * len(wanted),
            scratch_shapes=[
                pltpu.VMEM((3,) + old_gate.shape, BF16),
                pltpu.SemaphoreType.DMA((3,)),
            ],
            compiler_params=params(60),
            name=name,
        )(where, plan, *weights, after)

    parcels = pl.pallas_call(
        functools.partial(dispatch_kernel, experts),
        out_shape=[shape(SLOTS, width)] * experts,
        in_specs=[SMEM, VMEM, HBM],
        out_specs=[VMEM] * experts,
        scratch_shapes=[pltpu.VMEM(tokens.shape, BF16), pltpu.SemaphoreType.DMA],
        compiler_params=params(60),
        name="dispatch",
    )(where, expert_ids.T, tokens)

    pairs = [(j, k) for j in range(experts) for k in range(GROUP)]
    rows = [parcels[0]] + [send(parcels[j], j, k) for j, k in pairs[1:]]

    first = select(
        [(0, None, part), (1, None, part), (2, 0, most)], parcels[0], "select_first"
    )
    shared = [migrate(first[p], p) for p in range(2)]
    near = migrate(first[2], 2)

    pieces = len(pairs)
    partial = pl.pallas_call(
        functools.partial(expert_kernel, pieces),
        out_shape=[shape(SLOTS, width)] * pieces,
        in_specs=[VMEM] * (pieces + 3),
        out_specs=[VMEM] * pieces,
        compiler_params=params(),
        name="expert",
    )(*rows, *weights)
    back = [partial[0]] + [
        send(block, -j, k) for (j, k), block in zip(pairs[1:], partial[1:])
    ]

    last = select([(0, 2 * part, rest), (1, 2 * part, rest)], back[1], "select_last")
    straight = [migrate(last[p], p) for p in range(2)]
    swapped = [swap(shared[p], p) for p in range(2)]

    mixed = pl.pallas_call(
        functools.partial(combine_kernel, experts),
        out_shape=shape(tokens.shape[0], width),
        in_specs=[SMEM, VMEM, VMEM] + [VMEM] * pieces,
        out_specs=VMEM,
        compiler_params=params(),
        name="combine",
    )(where, expert_ids, combine, *back)

    arrived = pl.pallas_call(
        functools.partial(merge_kernel, part),
        out_shape=shape(3, most, width),
        in_specs=[SMEM] + [HBM] * 7,
        out_specs=HBM,
        scratch_shapes=[pltpu.SemaphoreType.DMA((9,))],
        compiler_params=params(),
        name="merge",
    )(where, *shared, *swapped, *straight, near)
    return mixed, arrived


def solution(mesh):
    placed = (
        P(("replica", "expert"), None),
        P(("replica", "expert"), None),
        P(("replica", "expert"), None),
        P("expert", None),
        P("expert", None),
        P("expert", None),
        P(),
    )
    return jax.shard_map(
        on_device,
        mesh=mesh,
        in_specs=placed,
        out_specs=(P(("replica", "expert"), None), P("replica", "expert", None)),
        check_vma=False,
    )
```

```python
import functools

import jax
import jax.numpy as jnp
from jax import lax
from jax.experimental import pallas as pl
from jax.experimental.pallas import tpu as pltpu
from jax.sharding import PartitionSpec as P

CAP = 12
SLOTS = 16
GROUP = 4
BF16 = jnp.bfloat16
F32 = jnp.float32
VMEM = pl.BlockSpec(memory_space=pltpu.VMEM)
SMEM = pl.BlockSpec(memory_space=pltpu.SMEM)
HBM = pl.BlockSpec(memory_space=pl.ANY)


def params(megabytes=40):
    return pltpu.CompilerParams(vmem_limit_bytes=megabytes * 1024 * 1024)


def slot_matrix(ids, group, experts):
    tok = ids.shape[1]
    member = []
    for j in range(experts):
        expert = lax.rem(group + j, experts)
        named = jnp.where(ids == expert, 1.0, 0.0)
        member.append(jnp.sum(named, axis=0, keepdims=True))
    member = jnp.concatenate(member, axis=0)
    row = lax.broadcasted_iota(jnp.int32, (tok, tok), 0)
    col = lax.broadcasted_iota(jnp.int32, (tok, tok), 1)
    upto = jnp.where(row <= col, 1.0, 0.0).astype(BF16)
    rank = jnp.dot(member.astype(BF16), upto, preferred_element_type=F32)
    place = jnp.where(member > 0, rank - 1.0, -1.0).astype(jnp.int32)
    slot = lax.broadcasted_iota(jnp.int32, (SLOTS, tok), 0)
    blocks = [jnp.where(slot == place[j : j + 1, :], 1.0, 0.0) for j in range(experts)]
    return jnp.concatenate(blocks, axis=0)


def dispatch_kernel(experts, where_ref, ids_ref, tok_hbm, *refs):
    out_refs, (tok_ref, sem) = refs[:experts], refs[experts:]
    copy = pltpu.make_async_copy(tok_hbm, tok_ref, sem)
    copy.start()
    chosen = slot_matrix(ids_ref[...], where_ref[0], experts).astype(BF16)
    copy.wait()
    rows = jnp.dot(chosen, tok_ref[...], preferred_element_type=F32).astype(BF16)
    for j, ref in enumerate(out_refs):
        ref[...] = rows[j * SLOTS : (j + 1) * SLOTS]


def select_kernel(replicas, where_ref, plan_ref, gate_hbm, up_hbm, down_hbm, after_ref, *refs):
    out_refs, (held_ref, sems) = refs[: GROUP - 1], refs[GROUP - 1 :]
    rows = held_ref.shape[1]
    share = out_refs[0].shape[1]

    @pl.when(where_ref[1] == GROUP - 1)
    def _():
        copies = [
            pltpu.make_async_copy(ref, held_ref.at[m], sems.at[m])
            for m, ref in enumerate((gate_hbm, up_hbm, down_hbm))
        ]
        for copy in copies:
            copy.start()
        plans = []
        for survivor in range(GROUP - 1):
            whole = plan_ref[survivor, pl.ds(where_ref[0], 1), :]
            plan = whole[:, :share]
            for r in range(1, replicas):
                part = whole[:, r * share : (r + 1) * share]
                plan = jnp.where(where_ref[2] == r, part, plan)
            plans.append(plan)
        number = lax.broadcasted_iota(jnp.int32, (rows, share * len(plans)), 0)
        pick = jnp.where(number == jnp.concatenate(plans, axis=1), 1.0, 0.0).astype(BF16)
        for m, copy in enumerate(copies):
            copy.wait()
            found = lax.dot_general(
                pick, held_ref[m], (((0,), (0,)), ((), ())), preferred_element_type=F32
            )
            for p, ref in enumerate(out_refs):
                ref[m] = found[p * share : (p + 1) * share].astype(BF16)


def expert_kernel(*refs):
    x_refs, (gate_ref, up_ref, down_ref), out_refs = refs[:4], refs[4:7], refs[7:]
    rows = x_refs[0].shape[0]
    x = jnp.concatenate([ref[...] for ref in x_refs], axis=0)
    numbers = (((1,), (1,)), ((), ()))
    gate_value = lax.dot_general(x, gate_ref[...], numbers, preferred_element_type=F32)
    up_value = lax.dot_general(x, up_ref[...], numbers, preferred_element_type=F32)
    hidden = (gate_value / (1.0 + jnp.exp(-gate_value)) * up_value).astype(BF16)
    partial = jnp.dot(hidden, down_ref[...], preferred_element_type=F32).astype(BF16)
    for k, ref in enumerate(out_refs):
        ref[...] = partial[k * rows : (k + 1) * rows]


def combine_kernel(experts, where_ref, ids_ref, weight_ref, *refs):
    near_refs, back_refs, out_ref = refs[:GROUP], refs[GROUP:-1], refs[-1]
    ids = ids_ref[...]
    group = where_ref[0]
    tok = ids.shape[0]
    row = lax.broadcasted_iota(jnp.int32, (tok, tok), 0)
    col = lax.broadcasted_iota(jnp.int32, (tok, tok), 1)
    upto = jnp.where(col <= row, 1.0, 0.0).astype(BF16)
    mixed = None
    for j in range(experts):
        named = ids == lax.rem(group + j, experts)
        member = jnp.sum(jnp.where(named, 1.0, 0.0), axis=1, keepdims=True)
        weight = jnp.sum(jnp.where(named, weight_ref[...], 0.0), axis=1, keepdims=True)
        rank = jnp.dot(upto, member.astype(BF16), preferred_element_type=F32)
        place = jnp.where(member > 0, rank - 1.0, -1.0).astype(jnp.int32)
        if j == 0:
            rows = jnp.concatenate([ref[:SLOTS] for ref in near_refs], axis=0)
        else:
            rows = back_refs[j - 1][...]
        slot = lax.broadcasted_iota(jnp.int32, (tok, rows.shape[0]), 1) % SLOTS
        chosen = jnp.where(slot == place, 1.0, 0.0).astype(BF16)
        term = weight * jnp.dot(chosen, rows, preferred_element_type=F32)
        mixed = term if mixed is None else mixed + term
    out_ref[...] = mixed.astype(BF16)


def on_device(tokens, expert_ids, combine, old_gate, old_up, old_down, move_plan):
    devices = lax.axis_size("expert")
    replicas = lax.axis_size("replica")
    experts = move_plan.shape[0]
    most = move_plan.shape[2]
    share = most // replicas
    width = tokens.shape[1]
    device = lax.axis_index("expert")
    group, position = device // GROUP, device % GROUP
    where = jnp.stack([group, position, lax.axis_index("replica")]).astype(jnp.int32)
    plan = jnp.transpose(move_plan, (1, 0, 2))
    weights = (old_gate, old_up, old_down)

    def shape(*dims, dtype=BF16):
        return jax.ShapeDtypeStruct(dims, dtype)

    def permute(block, target):
        return lax.ppermute(block, "expert", [(i, target(i)) for i in range(devices)])

    def migrate(block, survivor):
        route = [(GROUP * e + GROUP - 1, GROUP * e + survivor) for e in range(experts)]
        return lax.ppermute(block, "expert", route)

    parcels = pl.pallas_call(
        functools.partial(dispatch_kernel, experts),
        out_shape=[shape(SLOTS, width)] * experts,
        in_specs=[SMEM, VMEM, HBM],
        out_specs=[VMEM] * experts,
        scratch_shapes=[pltpu.VMEM(tokens.shape, BF16), pltpu.SemaphoreType.DMA],
        compiler_params=params(60),
        name="dispatch",
    )(where, expert_ids.T, tokens)

    chosen = pl.pallas_call(
        functools.partial(select_kernel, replicas),
        out_shape=[shape(3, share, width)] * (GROUP - 1),
        in_specs=[SMEM, VMEM, HBM, HBM, HBM, HBM],
        out_specs=[VMEM] * (GROUP - 1),
        scratch_shapes=[
            pltpu.VMEM((3,) + old_gate.shape, BF16),
            pltpu.SemaphoreType.DMA((3,)),
        ],
        compiler_params=params(60),
        cost_estimate=pl.CostEstimate(
            flops=4 * 10**9, bytes_accessed=8 * 10**6, transcendentals=0
        ),
        name="select",
    )(where, plan, *weights, parcels[0])

    across = [
        permute(parcels[j], lambda i: (i + GROUP * j) % devices) for j in range(1, experts)
    ]
    here = jnp.concatenate([parcels[0]] + across, axis=0)
    rows = [here] + [permute(here, lambda i: i ^ k) for k in (1, 2, 3)]

    landed = [migrate(chosen[p], p) for p in range(GROUP - 1)]
    arrived = lax.all_gather(landed[0] + landed[1] + landed[2], "replica", axis=1, tiled=True)

    step = min(experts * SLOTS, 32)
    row_spec = pl.BlockSpec((step, width), lambda i: (i, 0))
    whole_spec = pl.BlockSpec(old_gate.shape, lambda i: (0, 0))
    partial = pl.pallas_call(
        expert_kernel,
        grid=(experts * SLOTS // step,),
        out_shape=[shape(experts * SLOTS, width)] * GROUP,
        in_specs=[row_spec] * GROUP + [whole_spec] * 3,
        out_specs=[row_spec] * GROUP,
        compiler_params=params(),
        name="expert",
    )(*rows, *weights)
    near = [partial[0]] + [permute(partial[k], lambda i: i ^ k) for k in (1, 2, 3)]
    total = sum(block[SLOTS:].astype(F32) for block in near).astype(BF16)
    back = [
        permute(
            total[(j - 1) * SLOTS : j * SLOTS], lambda i: (i - GROUP * j) % devices
        )
        for j in range(1, experts)
    ]
    mixed = pl.pallas_call(
        functools.partial(combine_kernel, experts),
        out_shape=shape(tokens.shape[0], width),
        in_specs=[SMEM, VMEM, VMEM] + [VMEM] * (GROUP + experts - 1),
        out_specs=VMEM,
        compiler_params=params(),
        name="combine",
    )(where, expert_ids, combine, *near, *back)
    return mixed, arrived


def solution(mesh):
    placed = (
        P(("replica", "expert"), None),
        P(("replica", "expert"), None),
        P(("replica", "expert"), None),
        P("expert", None),
        P("expert", None),
        P("expert", None),
        P(),
    )
    return jax.shard_map(
        on_device,
        mesh=mesh,
        in_specs=placed,
        out_specs=(P(("replica", "expert"), None), P("replica", "expert", None)),
        check_vma=False,
    )
```

```python
import functools

import jax
import jax.numpy as jnp
from jax import lax
from jax.experimental import pallas as pl
from jax.experimental.pallas import tpu as pltpu
from jax.sharding import PartitionSpec as P

CAP = 12
SLOTS = 16
GROUP = 4
BF16 = jnp.bfloat16
F32 = jnp.float32
VMEM = pl.BlockSpec(memory_space=pltpu.VMEM)
HBM = pl.BlockSpec(memory_space=pl.ANY)


def params():
    return pltpu.CompilerParams(vmem_limit_bytes=40 * 1024 * 1024)


def cost(microseconds):
    return pl.CostEstimate(
        flops=microseconds * 10**9, bytes_accessed=10**6, transcendentals=0
    )


def slot_matrix(ids, group, experts):
    tok = ids.shape[1]
    member = []
    for j in range(experts):
        expert = lax.rem(group + j, experts)
        named = jnp.where(ids == expert, 1.0, 0.0)
        member.append(jnp.sum(named, axis=0, keepdims=True))
    member = jnp.concatenate(member, axis=0)
    row = lax.broadcasted_iota(jnp.int32, (tok, tok), 0)
    col = lax.broadcasted_iota(jnp.int32, (tok, tok), 1)
    upto = jnp.where(row <= col, 1.0, 0.0).astype(BF16)
    rank = jnp.dot(member.astype(BF16), upto, preferred_element_type=F32)
    place = jnp.where(member > 0, rank - 1.0, -1.0).astype(jnp.int32)
    slot = lax.broadcasted_iota(jnp.int32, (SLOTS, tok), 0)
    blocks = [jnp.where(slot == place[j : j + 1, :], 1.0, 0.0) for j in range(experts)]
    return jnp.concatenate(blocks, axis=0)


def dispatch_kernel(experts, ids_ref, tok_ref, *out_refs):
    group = lax.axis_index("expert") // GROUP
    chosen = slot_matrix(ids_ref[...], group, experts).astype(BF16)
    rows = jnp.dot(chosen, tok_ref[...], preferred_element_type=F32).astype(BF16)
    for j, ref in enumerate(out_refs):
        ref[...] = rows[j * SLOTS : (j + 1) * SLOTS]


def select_kernel(wanted, plan_ref, gate_ref, up_ref, down_ref, *out_refs):
    device = lax.axis_index("expert")
    even = lax.axis_index("replica") % 2 == 0
    rows = gate_ref.shape[0]

    @pl.when(device % GROUP == GROUP - 1)
    def _():
        plans = []
        for survivor, first, count in wanted:
            plan = plan_ref[survivor, pl.ds(device // GROUP, 1), :]
            if first is None:
                plan = jnp.where(even, plan[:, :count], plan[:, count : 2 * count])
            else:
                plan = plan[:, first : first + count]
            plans.append(plan)
        total = sum(count for _, _, count in wanted)
        number = lax.broadcasted_iota(jnp.int32, (rows, total), 0)
        pick = jnp.where(number == jnp.concatenate(plans, axis=1), 1.0, 0.0).astype(BF16)
        for m, held_ref in enumerate((gate_ref, up_ref, down_ref)):
            found = lax.dot_general(
                pick, held_ref[...], (((0,), (0,)), ((), ())), preferred_element_type=F32
            ).astype(BF16)
            start = 0
            for (_, _, count), ref in zip(wanted, out_refs):
                ref[m] = found[start : start + count]
                start += count


def merge_kernel(part, shared_ref, swapped_ref, first_ref, second_ref, near_ref, out_ref, sems):
    position = lax.axis_index("expert") % GROUP
    parity = lax.axis_index("replica") % 2
    most = out_ref.shape[1]

    def move(pieces):
        copies = []
        for ref, first, count in pieces:
            for m in range(3):
                copies.append(
                    pltpu.make_async_copy(
                        ref.at[m], out_ref.at[m, pl.ds(first, count)], sems.at[len(copies)]
                    )
                )
        for copy in copies:
            copy.start()
        for copy in copies:
            copy.wait()

    for p, ref in ((0, first_ref), (1, second_ref)):
        for even in range(2):
            mine = position == 1 if p == 1 else jnp.logical_or(position == 0, position == 3)

            @pl.when(jnp.logical_and(mine, parity == even))
            def _():
                move(
                    [
                        (shared_ref, part * even, part),
                        (swapped_ref, part * (1 - even), part),
                        (ref, 2 * part, most - 2 * part),
                    ]
                )

    @pl.when(position == 2)
    def _():
        move([(near_ref, 0, most)])


def expert_kernel(mine_ref, other_ref, gate_ref, up_ref, down_ref, keep_ref, send_ref):
    rows = mine_ref.shape[0]
    x = jnp.concatenate([mine_ref[...], other_ref[...]], axis=0)
    numbers = (((1,), (1,)), ((), ()))
    gate_value = lax.dot_general(x, gate_ref[...], numbers, preferred_element_type=F32)
    up_value = lax.dot_general(x, up_ref[...], numbers, preferred_element_type=F32)
    hidden = (gate_value / (1.0 + jnp.exp(-gate_value)) * up_value).astype(BF16)
    partial = jnp.dot(hidden, down_ref[...], preferred_element_type=F32)
    keep_ref[...] = partial[:rows]
    send_ref[...] = partial[rows:].astype(BF16)


def combine_kernel(experts, ids_ref, weight_ref, *refs):
    piece_refs, out_ref = refs[:-1], refs[-1]
    ids = ids_ref[...]
    group = lax.axis_index("expert") // GROUP
    tok = ids.shape[0]
    each = len(piece_refs) // experts
    row = lax.broadcasted_iota(jnp.int32, (tok, tok), 0)
    col = lax.broadcasted_iota(jnp.int32, (tok, tok), 1)
    upto = jnp.where(col <= row, 1.0, 0.0).astype(BF16)
    slot = lax.broadcasted_iota(jnp.int32, (tok, each * SLOTS), 1) % SLOTS
    mixed = None
    for j in range(experts):
        named = ids == lax.rem(group + j, experts)
        member = jnp.sum(jnp.where(named, 1.0, 0.0), axis=1, keepdims=True)
        weight = jnp.sum(jnp.where(named, weight_ref[...], 0.0), axis=1, keepdims=True)
        rank = jnp.dot(upto, member.astype(BF16), preferred_element_type=F32)
        place = jnp.where(member > 0, rank - 1.0, -1.0).astype(jnp.int32)
        chosen = jnp.where(slot == place, 1.0, 0.0).astype(BF16)
        rows = [ref[...] for ref in piece_refs[j * each : (j + 1) * each]]
        found = jnp.dot(chosen, jnp.concatenate(rows, axis=0), preferred_element_type=F32)
        term = weight * found
        mixed = term if mixed is None else mixed + term
    out_ref[...] = mixed.astype(BF16)


def on_device(tokens, expert_ids, combine, old_gate, old_up, old_down, move_plan):
    devices = lax.axis_size("expert")
    replicas = lax.axis_size("replica")
    experts = move_plan.shape[0]
    most = move_plan.shape[2]
    width = tokens.shape[1]
    plan = jnp.transpose(move_plan, (1, 0, 2))
    weights = (old_gate, old_up, old_down)
    part = most // 3
    rest = most - 2 * part

    def shape(*dims, dtype=BF16):
        return jax.ShapeDtypeStruct(dims, dtype)

    def send(block, j, k):
        route = []
        for i in range(devices):
            g, p = i // GROUP, i % GROUP
            route.append((i, GROUP * ((g + j) % experts) + (p ^ k)))
        return lax.ppermute(block, "expert", route)

    def migrate(block, survivor):
        route = [(GROUP * e + GROUP - 1, GROUP * e + survivor) for e in range(experts)]
        return lax.ppermute(block, "expert", route)

    def swap(block):
        route = []
        for r in range(replicas):
            for i in range(devices):
                if i % GROUP < 2:
                    route.append((i * replicas + r, i * replicas + (r ^ 1)))
        return lax.ppermute(block, ("expert", "replica"), route)

    def select(wanted, held, name):
        return pl.pallas_call(
            functools.partial(select_kernel, wanted),
            out_shape=[shape(3, count, width) for _, _, count in wanted],
            in_specs=[VMEM] * 4,
            out_specs=[VMEM] * len(wanted),
            compiler_params=params(),
            cost_estimate=cost(2),
            name=name,
        )(plan, *held)

    parcels = pl.pallas_call(
        functools.partial(dispatch_kernel, experts),
        out_shape=[shape(SLOTS, width)] * experts,
        in_specs=[VMEM, VMEM],
        out_specs=[VMEM] * experts,
        compiler_params=params(),
        cost_estimate=cost(2),
        name="dispatch",
    )(expert_ids.T, tokens)

    pairs = [(j, k) for j in range(experts) for k in (0, 2)]
    mine = [parcels[0]] + [send(parcels[j], j, k) for j, k in pairs[1:]]
    mine = jnp.concatenate(mine, axis=0)
    other = send(mine, 0, 1)

    held, mine = lax.optimization_barrier((weights, mine))
    first = select([(0, None, part), (1, None, part)], held, "select_first")
    shared = [migrate(first[p], p) for p in range(2)]
    other, _ = lax.optimization_barrier((other, first))

    total = mine.shape[0]
    step = min(total, 64)
    row_spec = pl.BlockSpec((step, width), lambda i: (i, 0))
    whole_spec = pl.BlockSpec(old_gate.shape, lambda i: (0, 0))
    keep, give = pl.pallas_call(
        expert_kernel,
        grid=(total // step,),
        out_shape=[shape(total, width, dtype=F32), shape(total, width)],
        in_specs=[row_spec] * 2 + [whole_spec] * 3,
        out_specs=[row_spec] * 2,
        compiler_params=params(),
        cost_estimate=cost(4),
        name="expert",
    )(mine, other, *weights)
    taken = send(give, 0, 1)
    summed = (keep + taken.astype(F32)).astype(BF16)
    pieces = [summed[n * SLOTS : (n + 1) * SLOTS] for n in range(len(pairs))]
    back = [pieces[0]] + [
        send(block, -j, k) for (j, k), block in zip(pairs[1:], pieces[1:])
    ]

    held, shared, back = lax.optimization_barrier((weights, shared, back))
    shared = shared[0] + shared[1]
    swapped = swap(shared)
    last = select(
        [(0, 2 * part, rest), (1, 2 * part, rest), (2, 0, most)], held, "select_last"
    )
    straight = [migrate(last[p], p) for p in range(GROUP - 1)]

    mixed = pl.pallas_call(
        functools.partial(combine_kernel, experts),
        out_shape=shape(tokens.shape[0], width),
        in_specs=[VMEM, VMEM] + [VMEM] * len(back),
        out_specs=VMEM,
        compiler_params=params(),
        cost_estimate=cost(2),
        name="combine",
    )(expert_ids, combine, *back)

    arrived = pl.pallas_call(
        functools.partial(merge_kernel, part),
        out_shape=shape(3, most, width),
        in_specs=[HBM] * 5,
        out_specs=HBM,
        scratch_shapes=[pltpu.SemaphoreType.DMA((9,))],
        compiler_params=params(),
        name="merge",
    )(shared, swapped, *straight)
    return mixed, arrived


def solution(mesh):
    placed = (
        P(("replica", "expert"), None),
        P(("replica", "expert"), None),
        P(("replica", "expert"), None),
        P("expert", None),
        P("expert", None),
        P("expert", None),
        P(),
    )
    return jax.shard_map(
        on_device,
        mesh=mesh,
        in_specs=placed,
        out_specs=(P(("replica", "expert"), None), P("replica", "expert", None)),
        check_vma=False,
    )
```

```python
import functools

import jax
import jax.numpy as jnp
from jax import lax
from jax.experimental import pallas as pl
from jax.experimental.pallas import tpu as pltpu
from jax.sharding import PartitionSpec as P

CAP = 12
SLOTS = 16
GROUP = 4
BF16 = jnp.bfloat16
F32 = jnp.float32
VMEM = pl.BlockSpec(memory_space=pltpu.VMEM)
HBM = pl.BlockSpec(memory_space=pl.ANY)


def params():
    return pltpu.CompilerParams(vmem_limit_bytes=40 * 1024 * 1024)


def cost(microseconds):
    return pl.CostEstimate(
        flops=microseconds * 10**9, bytes_accessed=10**4, transcendentals=0
    )


def slot_matrix(ids, group, experts):
    tok = ids.shape[1]
    member = []
    for j in range(experts):
        expert = lax.rem(group + j, experts)
        named = jnp.where(ids == expert, 1.0, 0.0)
        member.append(jnp.sum(named, axis=0, keepdims=True))
    member = jnp.concatenate(member, axis=0)
    row = lax.broadcasted_iota(jnp.int32, (tok, tok), 0)
    col = lax.broadcasted_iota(jnp.int32, (tok, tok), 1)
    upto = jnp.where(row <= col, 1.0, 0.0).astype(BF16)
    rank = jnp.dot(member.astype(BF16), upto, preferred_element_type=F32)
    place = jnp.where(member > 0, rank - 1.0, -1.0).astype(jnp.int32)
    slot = lax.broadcasted_iota(jnp.int32, (SLOTS, tok), 0)
    blocks = [jnp.where(slot == place[j : j + 1, :], 1.0, 0.0) for j in range(experts)]
    return jnp.concatenate(blocks, axis=0)


def dispatch_kernel(experts, ids_ref, tok_ref, *out_refs):
    group = lax.axis_index("expert") // GROUP
    chosen = slot_matrix(ids_ref[...], group, experts).astype(BF16)
    rows = jnp.dot(chosen, tok_ref[...], preferred_element_type=F32).astype(BF16)
    for j, ref in enumerate(out_refs):
        ref[...] = rows[j * SLOTS : (j + 1) * SLOTS]


def select_kernel(wanted, plan_ref, gate_ref, up_ref, down_ref, *out_refs):
    device = lax.axis_index("expert")
    even = lax.axis_index("replica") % 2 == 0
    rows = gate_ref.shape[0]

    @pl.when(device % GROUP == GROUP - 1)
    def _():
        plans = []
        for survivor, first, count in wanted:
            plan = plan_ref[survivor, pl.ds(device // GROUP, 1), :]
            if first is None:
                plan = jnp.where(even, plan[:, :count], plan[:, count : 2 * count])
            else:
                plan = plan[:, first : first + count]
            plans.append(plan)
        total = sum(count for _, _, count in wanted)
        number = lax.broadcasted_iota(jnp.int32, (rows, total), 0)
        pick = jnp.where(number == jnp.concatenate(plans, axis=1), 1.0, 0.0).astype(BF16)
        for m, held_ref in enumerate((gate_ref, up_ref, down_ref)):
            found = lax.dot_general(
                pick, held_ref[...], (((0,), (0,)), ((), ())), preferred_element_type=F32
            ).astype(BF16)
            start = 0
            for (_, _, count), ref in zip(wanted, out_refs):
                ref[m] = found[start : start + count]
                start += count


def merge_kernel(part, shared_ref, swapped_ref, first_ref, second_ref, near_ref, out_ref, sems):
    position = lax.axis_index("expert") % GROUP
    parity = lax.axis_index("replica") % 2
    most = out_ref.shape[1]

    def move(pieces):
        copies = []
        for ref, first, count in pieces:
            for m in range(3):
                copies.append(
                    pltpu.make_async_copy(
                        ref.at[m], out_ref.at[m, pl.ds(first, count)], sems.at[len(copies)]
                    )
                )
        for copy in copies:
            copy.start()
        for copy in copies:
            copy.wait()

    for p, ref in ((0, first_ref), (1, second_ref)):
        for even in range(2):
            mine = position == 1 if p == 1 else jnp.logical_or(position == 0, position == 3)

            @pl.when(jnp.logical_and(mine, parity == even))
            def _():
                move(
                    [
                        (shared_ref, part * even, part),
                        (swapped_ref, part * (1 - even), part),
                        (ref, 2 * part, most - 2 * part),
                    ]
                )

    @pl.when(position == 2)
    def _():
        move([(near_ref, 0, most)])


def expert_kernel(mine_ref, other_ref, gate_ref, up_ref, down_ref, keep_ref, send_ref):
    rows = mine_ref.shape[0]
    x = jnp.concatenate([mine_ref[...], other_ref[...]], axis=0)
    numbers = (((1,), (1,)), ((), ()))
    gate_value = lax.dot_general(x, gate_ref[...], numbers, preferred_element_type=F32)
    up_value = lax.dot_general(x, up_ref[...], numbers, preferred_element_type=F32)
    hidden = (gate_value / (1.0 + jnp.exp(-gate_value)) * up_value).astype(BF16)
    partial = jnp.dot(hidden, down_ref[...], preferred_element_type=F32)
    keep_ref[...] = partial[:rows]
    send_ref[...] = partial[rows:].astype(BF16)


def combine_kernel(experts, ids_ref, weight_ref, *refs):
    piece_refs, out_ref = refs[:-1], refs[-1]
    ids = ids_ref[...]
    group = lax.axis_index("expert") // GROUP
    tok = ids.shape[0]
    each = len(piece_refs) // experts
    row = lax.broadcasted_iota(jnp.int32, (tok, tok), 0)
    col = lax.broadcasted_iota(jnp.int32, (tok, tok), 1)
    upto = jnp.where(col <= row, 1.0, 0.0).astype(BF16)
    slot = lax.broadcasted_iota(jnp.int32, (tok, each * SLOTS), 1) % SLOTS
    mixed = None
    for j in range(experts):
        named = ids == lax.rem(group + j, experts)
        member = jnp.sum(jnp.where(named, 1.0, 0.0), axis=1, keepdims=True)
        weight = jnp.sum(jnp.where(named, weight_ref[...], 0.0), axis=1, keepdims=True)
        rank = jnp.dot(upto, member.astype(BF16), preferred_element_type=F32)
        place = jnp.where(member > 0, rank - 1.0, -1.0).astype(jnp.int32)
        chosen = jnp.where(slot == place, 1.0, 0.0).astype(BF16)
        rows = [ref[...] for ref in piece_refs[j * each : (j + 1) * each]]
        found = jnp.dot(chosen, jnp.concatenate(rows, axis=0), preferred_element_type=F32)
        term = weight * found
        mixed = term if mixed is None else mixed + term
    out_ref[...] = mixed.astype(BF16)


def on_device(tokens, expert_ids, combine, old_gate, old_up, old_down, move_plan):
    devices = lax.axis_size("expert")
    replicas = lax.axis_size("replica")
    experts = move_plan.shape[0]
    most = move_plan.shape[2]
    width = tokens.shape[1]
    plan = jnp.transpose(move_plan, (1, 0, 2))
    weights = (old_gate, old_up, old_down)
    part = most // 3
    rest = most - 2 * part

    def shape(*dims, dtype=BF16):
        return jax.ShapeDtypeStruct(dims, dtype)

    def send(block, j, k):
        route = []
        for i in range(devices):
            g, p = i // GROUP, i % GROUP
            route.append((i, GROUP * ((g + j) % experts) + (p ^ k)))
        return lax.ppermute(block, "expert", route)

    def migrate(block, survivor):
        route = [(GROUP * e + GROUP - 1, GROUP * e + survivor) for e in range(experts)]
        return lax.ppermute(block, "expert", route)

    def swap(block):
        route = []
        for r in range(replicas):
            for i in range(devices):
                if i % GROUP < 2:
                    route.append((i * replicas + r, i * replicas + (r ^ 1)))
        return lax.ppermute(block, ("expert", "replica"), route)

    def select(wanted, held):
        return pl.pallas_call(
            functools.partial(select_kernel, wanted),
            out_shape=[shape(3, count, width) for _, _, count in wanted],
            in_specs=[VMEM] * 4,
            out_specs=[VMEM] * len(wanted),
            compiler_params=params(),
            cost_estimate=cost(2),
            name="select",
        )(plan, *held)

    parcels = pl.pallas_call(
        functools.partial(dispatch_kernel, experts),
        out_shape=[shape(SLOTS, width)] * experts,
        in_specs=[VMEM, VMEM],
        out_specs=[VMEM] * experts,
        compiler_params=params(),
        cost_estimate=cost(2),
        name="dispatch",
    )(expert_ids.T, tokens)

    pairs = [(j, k) for j in range(experts) for k in (0, 2)]
    mine = [parcels[0]] + [send(parcels[j], j, k) for j, k in pairs[1:]]
    held, parcels = lax.optimization_barrier((weights, parcels))
    chosen = select(
        [(0, None, part), (1, None, part)]
        + [(0, 2 * part, rest), (1, 2 * part, rest), (2, 0, most)],
        held,
    )
    mine, chosen = lax.optimization_barrier((mine, chosen))
    mine = jnp.concatenate(mine, axis=0)
    other = send(mine, 0, 1)

    shared = [migrate(chosen[p], p) for p in range(2)]

    total = mine.shape[0]
    step = min(total, 64)
    row_spec = pl.BlockSpec((step, width), lambda i: (i, 0))
    whole_spec = pl.BlockSpec(old_gate.shape, lambda i: (0, 0))
    keep, give = pl.pallas_call(
        expert_kernel,
        grid=(total // step,),
        out_shape=[shape(total, width, dtype=F32), shape(total, width)],
        in_specs=[row_spec] * 2 + [whole_spec] * 3,
        out_specs=[row_spec] * 2,
        compiler_params=params(),
        cost_estimate=cost(4),
        name="expert",
    )(mine, other, *weights)
    shared = shared[0] + shared[1]
    taken, shared = lax.optimization_barrier((send(give, 0, 1), shared))
    summed = (keep + taken.astype(F32)).astype(BF16)
    pieces = [summed[n * SLOTS : (n + 1) * SLOTS] for n in range(len(pairs))]
    back = [pieces[0]] + [
        send(block, -j, k) for (j, k), block in zip(pairs[1:], pieces[1:])
    ]

    swapped = swap(shared)
    last, _ = lax.optimization_barrier((chosen[2:], summed))
    straight = [migrate(last[p], p) for p in range(GROUP - 1)]

    mixed = pl.pallas_call(
        functools.partial(combine_kernel, experts),
        out_shape=shape(tokens.shape[0], width),
        in_specs=[VMEM, VMEM] + [VMEM] * len(back),
        out_specs=VMEM,
        compiler_params=params(),
        cost_estimate=cost(12),
        name="combine",
    )(expert_ids, combine, *back)

    arrived = pl.pallas_call(
        functools.partial(merge_kernel, part),
        out_shape=shape(3, most, width),
        in_specs=[HBM] * 5,
        out_specs=HBM,
        scratch_shapes=[pltpu.SemaphoreType.DMA((9,))],
        compiler_params=params(),
        name="merge",
    )(shared, swapped, *straight)
    return mixed, arrived


def solution(mesh):
    placed = (
        P(("replica", "expert"), None),
        P(("replica", "expert"), None),
        P(("replica", "expert"), None),
        P("expert", None),
        P("expert", None),
        P("expert", None),
        P(),
    )
    return jax.shard_map(
        on_device,
        mesh=mesh,
        in_specs=placed,
        out_specs=(P(("replica", "expert"), None), P("replica", "expert", None)),
        check_vma=False,
    )
```

```python
import functools

import jax
import jax.numpy as jnp
from jax import lax
from jax.experimental import pallas as pl
from jax.experimental.pallas import tpu as pltpu
from jax.sharding import PartitionSpec as P

CAP = 12
SLOTS = 16
GROUP = 4
BF16 = jnp.bfloat16
F32 = jnp.float32
VMEM = pl.BlockSpec(memory_space=pltpu.VMEM)
HBM = pl.BlockSpec(memory_space=pl.ANY)


def params():
    return pltpu.CompilerParams(vmem_limit_bytes=40 * 1024 * 1024)


def cost(microseconds):
    return pl.CostEstimate(
        flops=microseconds * 10**9, bytes_accessed=10**4, transcendentals=0
    )


def slot_matrix(ids, group, experts):
    tok = ids.shape[1]
    member = []
    for j in range(experts):
        expert = lax.rem(group + j, experts)
        named = jnp.where(ids == expert, 1.0, 0.0)
        member.append(jnp.sum(named, axis=0, keepdims=True))
    member = jnp.concatenate(member, axis=0)
    row = lax.broadcasted_iota(jnp.int32, (tok, tok), 0)
    col = lax.broadcasted_iota(jnp.int32, (tok, tok), 1)
    upto = jnp.where(row <= col, 1.0, 0.0).astype(BF16)
    rank = jnp.dot(member.astype(BF16), upto, preferred_element_type=F32)
    place = jnp.where(member > 0, rank - 1.0, -1.0).astype(jnp.int32)
    slot = lax.broadcasted_iota(jnp.int32, (SLOTS, tok), 0)
    blocks = [jnp.where(slot == place[j : j + 1, :], 1.0, 0.0) for j in range(experts)]
    return jnp.concatenate(blocks, axis=0)


def dispatch_kernel(experts, ids_ref, tok_ref, *out_refs):
    group = lax.axis_index("expert") // GROUP
    chosen = slot_matrix(ids_ref[...], group, experts).astype(BF16)
    rows = jnp.dot(chosen, tok_ref[...], preferred_element_type=F32).astype(BF16)
    for j, ref in enumerate(out_refs):
        ref[...] = rows[j * SLOTS : (j + 1) * SLOTS]


def select_kernel(wanted, plan_ref, gate_ref, up_ref, down_ref, *out_refs):
    device = lax.axis_index("expert")
    even = lax.axis_index("replica") % 2 == 0
    rows = gate_ref.shape[0]

    @pl.when(device % GROUP == GROUP - 1)
    def _():
        plans = []
        for survivor, first, count in wanted:
            plan = plan_ref[survivor, pl.ds(device // GROUP, 1), :]
            if first is None:
                plan = jnp.where(even, plan[:, :count], plan[:, count : 2 * count])
            else:
                plan = plan[:, first : first + count]
            plans.append(plan)
        total = sum(count for _, _, count in wanted)
        number = lax.broadcasted_iota(jnp.int32, (rows, total), 0)
        pick = jnp.where(number == jnp.concatenate(plans, axis=1), 1.0, 0.0).astype(BF16)
        for m, held_ref in enumerate((gate_ref, up_ref, down_ref)):
            found = lax.dot_general(
                pick, held_ref[...], (((0,), (0,)), ((), ())), preferred_element_type=F32
            ).astype(BF16)
            start = 0
            for (_, _, count), ref in zip(wanted, out_refs):
                ref[m] = found[start : start + count]
                start += count


def merge_kernel(shared_ref, swapped_ref, straight_ref, near_ref, out_ref, sems):
    position = lax.axis_index("expert") % GROUP
    parity = lax.axis_index("replica") % 2
    half = shared_ref.shape[1]

    def move(pieces):
        copies = []
        for ref, first in pieces:
            for m in range(3):
                rows = pl.ds(first, ref.shape[1])
                copies.append(
                    pltpu.make_async_copy(ref.at[m], out_ref.at[m, rows], sems.at[len(copies)])
                )
        for copy in copies:
            copy.start()
        for copy in copies:
            copy.wait()

    for even in range(2):

        @pl.when(jnp.logical_and(position == 0, parity == even))
        def _():
            move([(shared_ref, half * even), (swapped_ref, half * (1 - even))])

    @pl.when(jnp.logical_or(position == 1, position == 3))
    def _():
        move([(straight_ref, 0)])

    @pl.when(position == 2)
    def _():
        move([(near_ref, 0)])


def expert_kernel(mine_ref, other_ref, gate_ref, up_ref, down_ref, keep_ref, send_ref):
    rows = mine_ref.shape[0]
    x = jnp.concatenate([mine_ref[...], other_ref[...]], axis=0)
    numbers = (((1,), (1,)), ((), ()))
    gate_value = lax.dot_general(x, gate_ref[...], numbers, preferred_element_type=F32)
    up_value = lax.dot_general(x, up_ref[...], numbers, preferred_element_type=F32)
    hidden = (gate_value / (1.0 + jnp.exp(-gate_value)) * up_value).astype(BF16)
    partial = jnp.dot(hidden, down_ref[...], preferred_element_type=F32)
    keep_ref[...] = partial[:rows]
    send_ref[...] = partial[rows:].astype(BF16)


def combine_kernel(experts, ids_ref, weight_ref, *refs):
    piece_refs, out_ref = refs[:-1], refs[-1]
    ids = ids_ref[...]
    group = lax.axis_index("expert") // GROUP
    tok = ids.shape[0]
    each = len(piece_refs) // experts
    row = lax.broadcasted_iota(jnp.int32, (tok, tok), 0)
    col = lax.broadcasted_iota(jnp.int32, (tok, tok), 1)
    upto = jnp.where(col <= row, 1.0, 0.0).astype(BF16)
    slot = lax.broadcasted_iota(jnp.int32, (tok, each * SLOTS), 1) % SLOTS
    mixed = None
    for j in range(experts):
        named = ids == lax.rem(group + j, experts)
        member = jnp.sum(jnp.where(named, 1.0, 0.0), axis=1, keepdims=True)
        weight = jnp.sum(jnp.where(named, weight_ref[...], 0.0), axis=1, keepdims=True)
        rank = jnp.dot(upto, member.astype(BF16), preferred_element_type=F32)
        place = jnp.where(member > 0, rank - 1.0, -1.0).astype(jnp.int32)
        chosen = jnp.where(slot == place, 1.0, 0.0).astype(BF16)
        rows = [ref[...] for ref in piece_refs[j * each : (j + 1) * each]]
        found = jnp.dot(chosen, jnp.concatenate(rows, axis=0), preferred_element_type=F32)
        term = weight * found
        mixed = term if mixed is None else mixed + term
    out_ref[...] = mixed.astype(BF16)


def on_device(tokens, expert_ids, combine, old_gate, old_up, old_down, move_plan):
    devices = lax.axis_size("expert")
    replicas = lax.axis_size("replica")
    experts = move_plan.shape[0]
    most = move_plan.shape[2]
    width = tokens.shape[1]
    plan = jnp.transpose(move_plan, (1, 0, 2))
    weights = (old_gate, old_up, old_down)
    half = most // 2

    def shape(*dims, dtype=BF16):
        return jax.ShapeDtypeStruct(dims, dtype)

    def send(block, j, k):
        route = []
        for i in range(devices):
            g, p = i // GROUP, i % GROUP
            route.append((i, GROUP * ((g + j) % experts) + (p ^ k)))
        return lax.ppermute(block, "expert", route)

    def migrate(block, survivor):
        route = [(GROUP * e + GROUP - 1, GROUP * e + survivor) for e in range(experts)]
        return lax.ppermute(block, "expert", route)

    def swap(block):
        route = []
        for r in range(replicas):
            for i in range(devices):
                if i % GROUP == 0:
                    route.append((i * replicas + r, i * replicas + (r ^ 1)))
        return lax.ppermute(block, ("expert", "replica"), route)

    def select(wanted, held):
        return pl.pallas_call(
            functools.partial(select_kernel, wanted),
            out_shape=[shape(3, count, width) for _, _, count in wanted],
            in_specs=[VMEM] * 4,
            out_specs=[VMEM] * len(wanted),
            compiler_params=params(),
            cost_estimate=cost(2),
            name="select",
        )(plan, *held)

    parcels = pl.pallas_call(
        functools.partial(dispatch_kernel, experts),
        out_shape=[shape(SLOTS, width)] * experts,
        in_specs=[VMEM, VMEM],
        out_specs=[VMEM] * experts,
        compiler_params=params(),
        cost_estimate=cost(2),
        name="dispatch",
    )(expert_ids.T, tokens)

    pairs = [(j, k) for j in range(experts) for k in (0, 2)]
    mine = [parcels[0]] + [send(parcels[j], j, k) for j, k in pairs[1:]]
    held, parcels = lax.optimization_barrier((weights, parcels))
    chosen = select([(0, None, half), (1, 0, most), (2, 0, most)], held)
    mine, chosen = lax.optimization_barrier((mine, chosen))
    mine = jnp.concatenate(mine, axis=0)
    other = send(mine, 0, 1)

    shared = migrate(chosen[0], 0)
    straight = migrate(chosen[1], 1)
    total = mine.shape[0]
    step = min(total, 64)
    row_spec = pl.BlockSpec((step, width), lambda i: (i, 0))
    whole_spec = pl.BlockSpec(old_gate.shape, lambda i: (0, 0))
    keep, give = pl.pallas_call(
        expert_kernel,
        grid=(total // step,),
        out_shape=[shape(total, width, dtype=F32), shape(total, width)],
        in_specs=[row_spec] * 2 + [whole_spec] * 3,
        out_specs=[row_spec] * 2,
        compiler_params=params(),
        cost_estimate=cost(0),
        name="expert",
    )(mine, other, *weights)
    taken, shared = lax.optimization_barrier((send(give, 0, 1), shared))
    summed = (keep + taken.astype(F32)).astype(BF16)
    pieces = [summed[n * SLOTS : (n + 1) * SLOTS] for n in range(len(pairs))]
    back = [pieces[0]] + [
        send(block, -j, k) for (j, k), block in zip(pairs[1:], pieces[1:])
    ]

    near, _ = lax.optimization_barrier((chosen[2], back[len(pairs) // 2]))
    near = migrate(near, 2)
    swapped = swap(shared)
    straight, back = lax.optimization_barrier((straight, back))

    mixed = pl.pallas_call(
        functools.partial(combine_kernel, experts),
        out_shape=shape(tokens.shape[0], width),
        in_specs=[VMEM, VMEM] + [VMEM] * len(back),
        out_specs=VMEM,
        compiler_params=params(),
        cost_estimate=cost(12),
        name="combine",
    )(expert_ids, combine, *back)

    arrived = pl.pallas_call(
        merge_kernel,
        out_shape=shape(3, most, width),
        in_specs=[HBM] * 4,
        out_specs=HBM,
        scratch_shapes=[pltpu.SemaphoreType.DMA((6,))],
        compiler_params=params(),
        name="merge",
    )(shared, swapped, straight, near)
    return mixed, arrived


def solution(mesh):
    placed = (
        P(("replica", "expert"), None),
        P(("replica", "expert"), None),
        P(("replica", "expert"), None),
        P("expert", None),
        P("expert", None),
        P("expert", None),
        P(),
    )
    return jax.shard_map(
        on_device,
        mesh=mesh,
        in_specs=placed,
        out_specs=(P(("replica", "expert"), None), P("replica", "expert", None)),
        check_vma=False,
    )
```

```python
import functools

import jax
import jax.numpy as jnp
from jax import lax
from jax.experimental import pallas as pl
from jax.experimental.pallas import tpu as pltpu
from jax.sharding import PartitionSpec as P

CAP = 12
PACK = 2 * CAP
GROUP = 4
BF16 = jnp.bfloat16
F32 = jnp.float32
VMEM = pl.BlockSpec(memory_space=pltpu.VMEM)
HBM = pl.BlockSpec(memory_space=pl.ANY)


def params():
    return pltpu.CompilerParams(vmem_limit_bytes=40 * 1024 * 1024)


def cost(microseconds):
    return pl.CostEstimate(
        flops=microseconds * 10**9, bytes_accessed=10**4, transcendentals=0
    )


def token_places(ids, group, experts):
    tok = ids.shape[1]
    member = []
    for j in range(experts):
        named = jnp.where(ids == lax.rem(group + j, experts), 1.0, 0.0)
        member.append(jnp.sum(named, axis=0, keepdims=True))
    member = jnp.concatenate(member, axis=0)
    row = lax.broadcasted_iota(jnp.int32, (tok, tok), 0)
    col = lax.broadcasted_iota(jnp.int32, (tok, tok), 1)
    upto = jnp.where(row <= col, 1.0, 0.0).astype(BF16)
    rank = jnp.dot(member.astype(BF16), upto, preferred_element_type=F32)
    return jnp.where(member > 0, rank - 1.0, -PACK).astype(jnp.int32)


def dispatch_kernel(experts, ids_ref, tok_ref, *out_refs):
    group = lax.axis_index("expert") // GROUP
    place = token_places(ids_ref[...], group, experts)
    tok, half = tok_ref.shape[0], tok_ref.shape[1] // 2
    slot = lax.broadcasted_iota(jnp.int32, (PACK, tok), 0)
    for j, ref in enumerate(out_refs):
        spot = place[j : j + 1, :]
        left = jnp.where(jnp.logical_and(slot == spot, spot >= 0), 1.0, 0.0).astype(BF16)
        right = jnp.where(slot == spot + CAP, 1.0, 0.0).astype(BF16)
        rows = jnp.dot(left, tok_ref[:, :half], preferred_element_type=F32)
        rows = rows + jnp.dot(right, tok_ref[:, half:], preferred_element_type=F32)
        ref[...] = rows.astype(BF16)


def select_kernel(wanted, plan_ref, gate_ref, up_ref, down_ref, *out_refs):
    device = lax.axis_index("expert")
    even = lax.axis_index("replica") % 2 == 0
    rows = gate_ref.shape[0]

    @pl.when(device % GROUP == GROUP - 1)
    def _():
        plans = []
        for survivor, first, count in wanted:
            plan = plan_ref[survivor, pl.ds(device // GROUP, 1), :]
            if first is None:
                plan = jnp.where(even, plan[:, :count], plan[:, count : 2 * count])
            else:
                plan = plan[:, first : first + count]
            plans.append(plan)
        total = sum(count for _, _, count in wanted)
        number = lax.broadcasted_iota(jnp.int32, (rows, total), 0)
        pick = jnp.where(number == jnp.concatenate(plans, axis=1), 1.0, 0.0).astype(BF16)
        for m, held_ref in enumerate((gate_ref, up_ref, down_ref)):
            found = lax.dot_general(
                pick, held_ref[...], (((0,), (0,)), ((), ())), preferred_element_type=F32
            ).astype(BF16)
            start = 0
            for (_, _, count), ref in zip(wanted, out_refs):
                ref[m] = found[start : start + count]
                start += count


def merge_kernel(shared_ref, swapped_ref, first_ref, second_ref, near_ref, out_ref, sems):
    position = lax.axis_index("expert") % GROUP
    parity = lax.axis_index("replica") % 2
    half = shared_ref.shape[1]

    def move(pieces):
        copies = []
        for ref, first in pieces:
            for m in range(3):
                rows = pl.ds(first, ref.shape[1])
                copies.append(
                    pltpu.make_async_copy(ref.at[m], out_ref.at[m, rows], sems.at[len(copies)])
                )
        for copy in copies:
            copy.start()
        for copy in copies:
            copy.wait()

    for even in range(2):

        @pl.when(jnp.logical_and(position == 0, parity == even))
        def _():
            move([(shared_ref, half * even), (swapped_ref, half * (1 - even))])

    @pl.when(jnp.logical_or(position == 1, position == 3))
    def _():
        move([(first_ref, 0), (second_ref, first_ref.shape[1])])

    @pl.when(position == 2)
    def _():
        move([(near_ref, 0)])


def expert_kernel(mine_ref, other_ref, gate_ref, up_ref, down_ref, keep_ref, give_ref):
    rows, half = mine_ref.shape
    x = jnp.concatenate([mine_ref[...], other_ref[...]], axis=0)
    total = x.shape[0]
    numbers = (((1,), (1,)), ((), ()))

    def project(ref):
        left = lax.dot_general(x, ref[:, :half], numbers, preferred_element_type=F32)
        right = lax.dot_general(x, ref[:, half:], numbers, preferred_element_type=F32)
        return left + jnp.concatenate([right[CAP:], right[:CAP]], axis=0)

    gate_value = project(gate_ref)
    up_value = project(up_ref)
    hidden = (gate_value / (1.0 + jnp.exp(-gate_value)) * up_value).astype(BF16)
    left = jnp.dot(hidden, down_ref[:, :half], preferred_element_type=F32)
    right = jnp.dot(hidden, down_ref[:, half:], preferred_element_type=F32)
    right = jnp.concatenate([right[total - CAP :], right[: total - CAP]], axis=0)
    row = lax.broadcasted_iota(jnp.int32, (total, half), 0)
    partial = jnp.where(row % PACK < CAP, left, right)
    keep_ref[...] = partial[:rows]
    give_ref[...] = partial[rows:].astype(BF16)


def combine_kernel(experts, ids_ref, weight_ref, *refs):
    piece_refs, out_ref = refs[:-1], refs[-1]
    ids = ids_ref[...]
    group = lax.axis_index("expert") // GROUP
    tok = ids.shape[0]
    half = out_ref.shape[1] // 2
    row = lax.broadcasted_iota(jnp.int32, (tok, tok), 0)
    col = lax.broadcasted_iota(jnp.int32, (tok, tok), 1)
    upto = jnp.where(col <= row, 1.0, 0.0).astype(BF16)
    slot = lax.broadcasted_iota(jnp.int32, (tok, PACK), 1)
    mixed = [None, None]
    for j in range(experts):
        named = ids == lax.rem(group + j, experts)
        member = jnp.sum(jnp.where(named, 1.0, 0.0), axis=1, keepdims=True)
        weight = jnp.sum(jnp.where(named, weight_ref[...], 0.0), axis=1, keepdims=True)
        rank = jnp.dot(upto, member.astype(BF16), preferred_element_type=F32)
        place = jnp.where(member > 0, rank - 1.0, -PACK).astype(jnp.int32)
        for side in range(2):
            chosen = jnp.where(slot == place + side * CAP, 1.0, 0.0).astype(BF16)
            found = jnp.dot(chosen, piece_refs[j][...], preferred_element_type=F32)
            term = weight * found
            mixed[side] = term if mixed[side] is None else mixed[side] + term
    out_ref[:, :half] = mixed[0].astype(BF16)
    out_ref[:, half:] = mixed[1].astype(BF16)


def on_device(tokens, expert_ids, combine, old_gate, old_up, old_down, move_plan):
    devices = lax.axis_size("expert")
    replicas = lax.axis_size("replica")
    experts = move_plan.shape[0]
    most = move_plan.shape[2]
    width = tokens.shape[1]
    plan = jnp.transpose(move_plan, (1, 0, 2))
    weights = (old_gate, old_up, old_down)
    half = most // 2

    def shape(*dims, dtype=BF16):
        return jax.ShapeDtypeStruct(dims, dtype)

    def send(block, j, k):
        route = []
        for i in range(devices):
            g, p = i // GROUP, i % GROUP
            route.append((i, GROUP * ((g + j) % experts) + (p ^ k)))
        return lax.ppermute(block, "expert", route)

    def migrate(block, survivor):
        route = [(GROUP * e + GROUP - 1, GROUP * e + survivor) for e in range(experts)]
        return lax.ppermute(block, "expert", route)

    def swap(block):
        route = []
        for r in range(replicas):
            for i in range(devices):
                if i % GROUP == 0:
                    route.append((i * replicas + r, i * replicas + (r ^ 1)))
        return lax.ppermute(block, ("expert", "replica"), route)

    def select(wanted, held):
        return pl.pallas_call(
            functools.partial(select_kernel, wanted),
            out_shape=[shape(3, count, width) for _, _, count in wanted],
            in_specs=[VMEM] * 4,
            out_specs=[VMEM] * len(wanted),
            compiler_params=params(),
            cost_estimate=cost(2),
            name="select",
        )(plan, *held)

    parcels = pl.pallas_call(
        functools.partial(dispatch_kernel, experts),
        out_shape=[shape(PACK, width // 2)] * experts,
        in_specs=[VMEM, VMEM],
        out_specs=[VMEM] * experts,
        compiler_params=params(),
        cost_estimate=cost(2),
        name="dispatch",
    )(expert_ids.T, tokens)

    held, across = lax.optimization_barrier((weights, parcels[1]))
    parcels = [parcels[0], across] + list(parcels[2:])
    across = [send(parcels[j], j, 0) for j in range(1, experts)]
    here = jnp.concatenate([parcels[0]] + across, axis=0)
    chosen = select([(0, None, half), (1, 0, half), (1, half, most - half), (2, 0, most)], held)
    here, chosen = lax.optimization_barrier((here, chosen))
    mine = jnp.concatenate([here, send(here, 0, 2)], axis=0)
    other = send(mine, 0, 1)

    shared = migrate(chosen[0], 0)
    first = migrate(chosen[1], 1)

    total = mine.shape[0]
    step = min(total, 4 * PACK)
    row_spec = pl.BlockSpec((step, width // 2), lambda i: (i, 0))
    whole_spec = pl.BlockSpec(old_gate.shape, lambda i: (0, 0))
    keep, give = pl.pallas_call(
        expert_kernel,
        grid=(total // step,),
        out_shape=[shape(total, width // 2, dtype=F32), shape(total, width // 2)],
        in_specs=[row_spec] * 2 + [whole_spec] * 3,
        out_specs=[row_spec] * 2,
        compiler_params=params(),
        cost_estimate=cost(0),
        name="expert",
    )(mine, other, *weights)
    taken, shared = lax.optimization_barrier((send(give, 0, 1), shared))
    summed = keep + taken.astype(F32)
    far = send(summed[total // 2 :].astype(BF16), 0, 2)

    far, first = lax.optimization_barrier((far, first))
    swapped = swap(shared)
    second = migrate(lax.optimization_barrier((chosen[2], summed))[0], 1)

    summed = (summed[: total // 2] + far.astype(F32)).astype(BF16)
    pieces = [summed[j * PACK : (j + 1) * PACK] for j in range(experts)]
    back = [pieces[0]] + [send(pieces[j], -j, 0) for j in range(1, experts)]
    near = migrate(lax.optimization_barrier((chosen[3], back))[0], 2)
    back, swapped, second = lax.optimization_barrier((back, swapped, second))

    mixed = pl.pallas_call(
        functools.partial(combine_kernel, experts),
        out_shape=shape(tokens.shape[0], width),
        in_specs=[VMEM, VMEM] + [VMEM] * len(back),
        out_specs=VMEM,
        compiler_params=params(),
        cost_estimate=cost(12),
        name="combine",
    )(expert_ids, combine, *back)

    arrived = pl.pallas_call(
        merge_kernel,
        out_shape=shape(3, most, width),
        in_specs=[HBM] * 5,
        out_specs=HBM,
        scratch_shapes=[pltpu.SemaphoreType.DMA((6,))],
        compiler_params=params(),
        name="merge",
    )(shared, swapped, first, second, near)
    return mixed, arrived


def solution(mesh):
    placed = (
        P(("replica", "expert"), None),
        P(("replica", "expert"), None),
        P(("replica", "expert"), None),
        P("expert", None),
        P("expert", None),
        P("expert", None),
        P(),
    )
    return jax.shard_map(
        on_device,
        mesh=mesh,
        in_specs=placed,
        out_specs=(P(("replica", "expert"), None), P("replica", "expert", None)),
        check_vma=False,
    )
```

```python
import functools

import jax
import jax.numpy as jnp
from jax import lax
from jax.experimental import pallas as pl
from jax.experimental.pallas import tpu as pltpu
from jax.sharding import PartitionSpec as P

CAP = 12
PACK = 2 * CAP
GROUP = 4
BF16 = jnp.bfloat16
F32 = jnp.float32
VMEM = pl.BlockSpec(memory_space=pltpu.VMEM)
HBM = pl.BlockSpec(memory_space=pl.ANY)


def params(megabytes=16):
    return pltpu.CompilerParams(vmem_limit_bytes=megabytes * 1024 * 1024)


def cost(microseconds):
    return pl.CostEstimate(
        flops=microseconds * 10**9, bytes_accessed=10**4, transcendentals=0
    )


def token_places(ids, group, experts):
    tok = ids.shape[1]
    member = []
    for j in range(experts):
        named = jnp.where(ids == lax.rem(group + j, experts), 1.0, 0.0)
        member.append(jnp.sum(named, axis=0, keepdims=True))
    member = jnp.concatenate(member, axis=0)
    row = lax.broadcasted_iota(jnp.int32, (tok, tok), 0)
    col = lax.broadcasted_iota(jnp.int32, (tok, tok), 1)
    upto = jnp.where(row <= col, 1.0, 0.0).astype(BF16)
    rank = jnp.dot(member.astype(BF16), upto, preferred_element_type=F32)
    return jnp.where(member > 0, rank - 1.0, -PACK).astype(jnp.int32)


def dispatch_kernel(experts, ids_ref, tok_ref, *out_refs):
    group = lax.axis_index("expert") // GROUP
    place = token_places(ids_ref[...], group, experts)
    tok, half = tok_ref.shape[0], tok_ref.shape[1] // 2
    slot = lax.broadcasted_iota(jnp.int32, (PACK, tok), 0)
    for j, ref in enumerate(out_refs):
        spot = place[j : j + 1, :]
        left = jnp.where(jnp.logical_and(slot == spot, spot >= 0), 1.0, 0.0).astype(BF16)
        right = jnp.where(slot == spot + CAP, 1.0, 0.0).astype(BF16)
        rows = jnp.dot(left, tok_ref[:, :half], preferred_element_type=F32)
        rows = rows + jnp.dot(right, tok_ref[:, half:], preferred_element_type=F32)
        ref[...] = rows.astype(BF16)


def select_kernel(wanted, plan_ref, gate_ref, up_ref, down_ref, *out_refs):
    device = lax.axis_index("expert")
    even = lax.axis_index("replica") % 2 == 0
    rows = gate_ref.shape[0]

    @pl.when(device % GROUP == GROUP - 1)
    def _():
        plans = []
        for survivor, first, count in wanted:
            plan = plan_ref[survivor, pl.ds(device // GROUP, 1), :]
            if first is None:
                plan = jnp.where(even, plan[:, :count], plan[:, count : 2 * count])
            else:
                plan = plan[:, first : first + count]
            plans.append(plan)
        total = sum(count for _, _, count in wanted)
        number = lax.broadcasted_iota(jnp.int32, (rows, total), 0)
        pick = jnp.where(number == jnp.concatenate(plans, axis=1), 1.0, 0.0).astype(BF16)
        for m, held_ref in enumerate((gate_ref, up_ref, down_ref)):
            found = lax.dot_general(
                pick, held_ref[...], (((0,), (0,)), ((), ())), preferred_element_type=F32
            ).astype(BF16)
            start = 0
            for (_, _, count), ref in zip(wanted, out_refs):
                ref[m] = found[start : start + count]
                start += count


def merge_kernel(shared_ref, swapped_ref, first_ref, second_ref, near_ref, out_ref, sems):
    position = lax.axis_index("expert") % GROUP
    parity = lax.axis_index("replica") % 2
    half = shared_ref.shape[1]

    def move(pieces):
        copies = []
        for ref, first in pieces:
            for m in range(3):
                rows = pl.ds(first, ref.shape[1])
                copies.append(
                    pltpu.make_async_copy(ref.at[m], out_ref.at[m, rows], sems.at[len(copies)])
                )
        for copy in copies:
            copy.start()
        for copy in copies:
            copy.wait()

    for even in range(2):

        @pl.when(jnp.logical_and(position == 1, parity == even))
        def _():
            move([(shared_ref, half * even), (swapped_ref, half * (1 - even))])

    @pl.when(jnp.logical_or(position == 0, position == 3))
    def _():
        move([(first_ref, 0), (second_ref, first_ref.shape[1])])

    @pl.when(position == 2)
    def _():
        move([(near_ref, 0)])


def expert_kernel(mine_ref, other_ref, gate_ref, up_ref, down_ref, keep_ref, give_ref):
    rows, half = mine_ref.shape
    x = jnp.concatenate([mine_ref[...], other_ref[...]], axis=0)
    total = x.shape[0]
    numbers = (((1,), (1,)), ((), ()))

    def project(ref):
        left = lax.dot_general(x, ref[:, :half], numbers, preferred_element_type=F32)
        right = lax.dot_general(x, ref[:, half:], numbers, preferred_element_type=F32)
        return left + jnp.concatenate([right[CAP:], right[:CAP]], axis=0)

    gate_value = project(gate_ref)
    up_value = project(up_ref)
    hidden = (gate_value / (1.0 + jnp.exp(-gate_value)) * up_value).astype(BF16)
    left = jnp.dot(hidden, down_ref[:, :half], preferred_element_type=F32)
    right = jnp.dot(hidden, down_ref[:, half:], preferred_element_type=F32)
    right = jnp.concatenate([right[total - CAP :], right[: total - CAP]], axis=0)
    row = lax.broadcasted_iota(jnp.int32, (total, half), 0)
    partial = jnp.where(row % PACK < CAP, left, right)
    keep_ref[...] = partial[:rows]
    give_ref[...] = partial[rows:].astype(BF16)


def combine_kernel(experts, ids_ref, weight_ref, *refs):
    piece_refs, out_ref = refs[:-1], refs[-1]
    ids = ids_ref[...]
    group = lax.axis_index("expert") // GROUP
    tok = ids.shape[0]
    half = out_ref.shape[1] // 2
    row = lax.broadcasted_iota(jnp.int32, (tok, tok), 0)
    col = lax.broadcasted_iota(jnp.int32, (tok, tok), 1)
    upto = jnp.where(col <= row, 1.0, 0.0).astype(BF16)
    slot = lax.broadcasted_iota(jnp.int32, (tok, PACK), 1)
    mixed = [None, None]
    for j in range(experts):
        named = ids == lax.rem(group + j, experts)
        member = jnp.sum(jnp.where(named, 1.0, 0.0), axis=1, keepdims=True)
        weight = jnp.sum(jnp.where(named, weight_ref[...], 0.0), axis=1, keepdims=True)
        rank = jnp.dot(upto, member.astype(BF16), preferred_element_type=F32)
        place = jnp.where(member > 0, rank - 1.0, -PACK).astype(jnp.int32)
        for side in range(2):
            chosen = jnp.where(slot == place + side * CAP, 1.0, 0.0).astype(BF16)
            found = jnp.dot(chosen, piece_refs[j][...], preferred_element_type=F32)
            term = weight * found
            mixed[side] = term if mixed[side] is None else mixed[side] + term
    out_ref[:, :half] = mixed[0].astype(BF16)
    out_ref[:, half:] = mixed[1].astype(BF16)


def on_device(tokens, expert_ids, combine, old_gate, old_up, old_down, move_plan):
    devices = lax.axis_size("expert")
    replicas = lax.axis_size("replica")
    experts = move_plan.shape[0]
    most = move_plan.shape[2]
    width = tokens.shape[1]
    plan = jnp.transpose(move_plan, (1, 0, 2))
    weights = (old_gate, old_up, old_down)
    half = most // 2

    def shape(*dims, dtype=BF16):
        return jax.ShapeDtypeStruct(dims, dtype)

    def send(block, j, k):
        route = []
        for i in range(devices):
            g, p = i // GROUP, i % GROUP
            route.append((i, GROUP * ((g + j) % experts) + (p ^ k)))
        return lax.ppermute(block, "expert", route)

    def migrate(block, survivor):
        route = [(GROUP * e + GROUP - 1, GROUP * e + survivor) for e in range(experts)]
        return lax.ppermute(block, "expert", route)

    def swap(block):
        route = []
        for r in range(replicas):
            for i in range(devices):
                if i % GROUP == 1:
                    route.append((i * replicas + r, i * replicas + (r ^ 1)))
        return lax.ppermute(block, ("expert", "replica"), route)

    def select(wanted, held):
        return pl.pallas_call(
            functools.partial(select_kernel, wanted),
            out_shape=[shape(3, count, width) for _, _, count in wanted],
            in_specs=[VMEM] * 4,
            out_specs=[VMEM] * len(wanted),
            compiler_params=params(),
            cost_estimate=cost(2),
            name="select",
        )(plan, *held)

    parcels = pl.pallas_call(
        functools.partial(dispatch_kernel, experts),
        out_shape=[shape(PACK, width // 2)] * experts,
        in_specs=[VMEM, VMEM],
        out_specs=[VMEM] * experts,
        compiler_params=params(),
        cost_estimate=cost(2),
        name="dispatch",
    )(expert_ids.T, tokens)

    held, across = lax.optimization_barrier((weights, parcels[1]))
    parcels = [parcels[0], across] + list(parcels[2:])
    across = [send(parcels[j], j, 0) for j in range(1, experts)]
    here = jnp.concatenate([parcels[0]] + across, axis=0)
    chosen = select([(1, None, half), (0, 0, half), (0, half, most - half), (2, 0, most)], held)
    here, chosen = lax.optimization_barrier((here, chosen))
    mine = jnp.concatenate([here, send(here, 0, 2)], axis=0)
    other = send(mine, 0, 1)

    shared = migrate(chosen[0], 1)
    first = migrate(chosen[1], 0)

    total = mine.shape[0]
    step = min(total, 4 * PACK)
    row_spec = pl.BlockSpec((step, width // 2), lambda i: (i, 0))
    whole_spec = pl.BlockSpec(old_gate.shape, lambda i: (0, 0))
    keep, give = pl.pallas_call(
        expert_kernel,
        grid=(total // step,),
        out_shape=[shape(total, width // 2, dtype=F32), shape(total, width // 2)],
        in_specs=[row_spec] * 2 + [whole_spec] * 3,
        out_specs=[row_spec] * 2,
        compiler_params=params(),
        cost_estimate=cost(0),
        name="expert",
    )(mine, other, *weights)
    taken, shared = lax.optimization_barrier((send(give, 0, 1), shared))
    summed = keep + taken.astype(F32)
    far = send(summed[total // 2 :].astype(BF16), 0, 2)

    far, first = lax.optimization_barrier((far, first))
    swapped = swap(shared)
    second = migrate(lax.optimization_barrier((chosen[2], summed))[0], 0)

    summed = (summed[: total // 2] + far.astype(F32)).astype(BF16)
    pieces = [summed[j * PACK : (j + 1) * PACK] for j in range(experts)]
    back = [pieces[0]] + [send(pieces[j], -j, 0) for j in range(1, experts)]
    near = migrate(lax.optimization_barrier((chosen[3], back))[0], 2)
    back, swapped, second = lax.optimization_barrier((back, swapped, second))

    mixed = pl.pallas_call(
        functools.partial(combine_kernel, experts),
        out_shape=shape(tokens.shape[0], width),
        in_specs=[VMEM, VMEM] + [VMEM] * len(back),
        out_specs=VMEM,
        compiler_params=params(14 + experts),
        cost_estimate=cost(12),
        name="combine",
    )(expert_ids, combine, *back)

    arrived = pl.pallas_call(
        merge_kernel,
        out_shape=shape(3, most, width),
        in_specs=[HBM] * 5,
        out_specs=HBM,
        scratch_shapes=[pltpu.SemaphoreType.DMA((6,))],
        compiler_params=params(),
        name="merge",
    )(shared, swapped, first, second, near)
    return mixed, arrived


def solution(mesh):
    placed = (
        P(("replica", "expert"), None),
        P(("replica", "expert"), None),
        P(("replica", "expert"), None),
        P("expert", None),
        P("expert", None),
        P("expert", None),
        P(),
    )
    return jax.shard_map(
        on_device,
        mesh=mesh,
        in_specs=placed,
        out_specs=(P(("replica", "expert"), None), P("replica", "expert", None)),
        check_vma=False,
    )
```

```python
import functools

import jax
import jax.numpy as jnp
from jax import lax
from jax.experimental import pallas as pl
from jax.experimental.pallas import tpu as pltpu
from jax.sharding import PartitionSpec as P

CAP = 12
PACK = 2 * CAP
GROUP = 4
BF16 = jnp.bfloat16
F32 = jnp.float32
VMEM = pl.BlockSpec(memory_space=pltpu.VMEM)
HBM = pl.BlockSpec(memory_space=pltpu.HBM)


def params(megabytes=16):
    return pltpu.CompilerParams(vmem_limit_bytes=megabytes * 1024 * 1024)


def cost(microseconds):
    return pl.CostEstimate(
        flops=microseconds * 10**9, bytes_accessed=10**4, transcendentals=0
    )


def token_places(ids, group, experts):
    tok = ids.shape[1]
    member = []
    for j in range(experts):
        named = jnp.where(ids == lax.rem(group + j, experts), 1.0, 0.0)
        member.append(jnp.sum(named, axis=0, keepdims=True))
    member = jnp.concatenate(member, axis=0)
    row = lax.broadcasted_iota(jnp.int32, (tok, tok), 0)
    col = lax.broadcasted_iota(jnp.int32, (tok, tok), 1)
    upto = jnp.where(row <= col, 1.0, 0.0).astype(BF16)
    rank = jnp.dot(member.astype(BF16), upto, preferred_element_type=F32)
    return jnp.where(member > 0, rank - 1.0, -PACK).astype(jnp.int32)


def dispatch_kernel(experts, ids_hbm, tok_hbm, *refs):
    out_refs, (ids_ref, tok_ref, sems) = refs[:experts], refs[experts:]
    tok, half = tok_ref.shape[0], tok_ref.shape[1] // 2
    copies = [pltpu.make_async_copy(ids_hbm, ids_ref, sems.at[0])]
    for side in range(2):
        columns = pl.ds(side * half, half)
        copies.append(
            pltpu.make_async_copy(
                tok_hbm.at[:, columns], tok_ref.at[:, columns], sems.at[side + 1]
            )
        )
    for copy in copies:
        copy.start()
    group = lax.axis_index("expert") // GROUP
    copies[0].wait()
    place = token_places(ids_ref[...], group, experts)
    slot = lax.broadcasted_iota(jnp.int32, (PACK, tok), 0)
    copies[1].wait()
    copies[2].wait()
    for j, ref in enumerate(out_refs):
        spot = place[j : j + 1, :]
        left = jnp.where(jnp.logical_and(slot == spot, spot >= 0), 1.0, 0.0).astype(BF16)
        right = jnp.where(slot == spot + CAP, 1.0, 0.0).astype(BF16)
        rows = jnp.dot(left, tok_ref[:, :half], preferred_element_type=F32)
        rows = rows + jnp.dot(right, tok_ref[:, half:], preferred_element_type=F32)
        ref[...] = rows.astype(BF16)


def select_kernel(wanted, plan_ref, gate_ref, up_ref, down_ref, *out_refs):
    device = lax.axis_index("expert")
    even = lax.axis_index("replica") % 2 == 0
    rows = gate_ref.shape[0]

    @pl.when(device % GROUP == GROUP - 1)
    def _():
        plans = []
        for survivor, count, first in wanted:
            plan = plan_ref[survivor, pl.ds(device // GROUP, 1), :]
            if first is None:
                plan = jnp.where(even, plan[:, :count], plan[:, count : 2 * count])
            else:
                plan = plan[:, first : first + count]
            plans.append(plan)
        total = sum(count for _, count, _ in wanted)
        number = lax.broadcasted_iota(jnp.int32, (rows, total), 0)
        pick = jnp.where(number == jnp.concatenate(plans, axis=1), 1.0, 0.0).astype(BF16)
        for m, held_ref in enumerate((gate_ref, up_ref, down_ref)):
            found = lax.dot_general(
                pick, held_ref[...], (((0,), (0,)), ((), ())), preferred_element_type=F32
            ).astype(BF16)
            start = 0
            for (_, count, _), ref in zip(wanted, out_refs):
                ref[m] = found[start : start + count]
                start += count


def merge_kernel(*refs):
    shared_refs, swapped_refs, (straight_ref, near_ref, out_ref, sems) = refs[:2], refs[2:4], refs[4:]
    position = lax.axis_index("expert") % GROUP
    parity = lax.axis_index("replica") % 2

    def move(pieces):
        copies = []
        for ref, first in pieces:
            for m in range(3):
                rows = pl.ds(first, ref.shape[1])
                copies.append(
                    pltpu.make_async_copy(ref.at[m], out_ref.at[m, rows], sems.at[len(copies)])
                )
        for copy in copies:
            copy.start()
        for copy in copies:
            copy.wait()

    for p in range(2):
        part = shared_refs[p].shape[1]
        for even in range(2):
            mine = position == 1 if p == 1 else jnp.logical_or(position == 0, position == 3)

            @pl.when(jnp.logical_and(mine, parity == even))
            def _():
                pieces = [(shared_refs[p], part * even), (swapped_refs[p], part * (1 - even))]
                if p == 0:
                    pieces.append((straight_ref, 2 * part))
                move(pieces)

    @pl.when(position == 2)
    def _():
        move([(near_ref, 0)])


def expert_kernel(mine_ref, other_ref, gate_ref, up_ref, down_ref, keep_ref, give_ref):
    rows, half = mine_ref.shape
    x = jnp.concatenate([mine_ref[...], other_ref[...]], axis=0)
    total = x.shape[0]
    numbers = (((1,), (1,)), ((), ()))

    def project(ref):
        left = lax.dot_general(x, ref[:, :half], numbers, preferred_element_type=F32)
        right = lax.dot_general(x, ref[:, half:], numbers, preferred_element_type=F32)
        return left + jnp.concatenate([right[CAP:], right[:CAP]], axis=0)

    gate_value = project(gate_ref)
    up_value = project(up_ref)
    hidden = (gate_value / (1.0 + jnp.exp(-gate_value)) * up_value).astype(BF16)
    left = jnp.dot(hidden, down_ref[:, :half], preferred_element_type=F32)
    right = jnp.dot(hidden, down_ref[:, half:], preferred_element_type=F32)
    right = jnp.concatenate([right[total - CAP :], right[: total - CAP]], axis=0)
    row = lax.broadcasted_iota(jnp.int32, (total, half), 0)
    partial = jnp.where(row % PACK < CAP, left, right)
    keep_ref[...] = partial[:rows]
    give_ref[...] = partial[rows:].astype(BF16)


def combine_kernel(experts, ids_ref, weight_ref, *refs):
    piece_refs, out_ref = refs[:-1], refs[-1]
    ids = ids_ref[...]
    group = lax.axis_index("expert") // GROUP
    half = out_ref.shape[1] // 2
    place = token_places(ids, group, experts)
    weights = []
    for j in range(experts):
        named = ids == lax.rem(group + j, experts)
        weights.append(jnp.sum(jnp.where(named, weight_ref[...], 0.0), axis=0, keepdims=True))
    weights = jnp.concatenate(weights, axis=0).T
    slot = lax.broadcasted_iota(jnp.int32, (PACK, ids.shape[1]), 0)
    numbers = (((0,), (0,)), ((), ()))
    mixed = [None, None]
    for j in range(experts):
        spot = place[j : j + 1, :]
        for side in range(2):
            chosen = jnp.where(slot == spot + side * CAP, 1.0, 0.0).astype(BF16)
            found = lax.dot_general(
                chosen, piece_refs[j][...], numbers, preferred_element_type=F32
            )
            term = weights[:, j : j + 1] * found
            mixed[side] = term if mixed[side] is None else mixed[side] + term
    out_ref[:, :half] = mixed[0].astype(BF16)
    out_ref[:, half:] = mixed[1].astype(BF16)


def on_device(tokens, expert_ids, combine, old_gate, old_up, old_down, move_plan):
    devices = lax.axis_size("expert")
    replicas = lax.axis_size("replica")
    experts = move_plan.shape[0]
    most = move_plan.shape[2]
    width = tokens.shape[1]
    plan = jnp.transpose(move_plan, (1, 0, 2))
    weights = (old_gate, old_up, old_down)
    half = most // 2
    part = most // 3
    rest = most - 2 * part

    def shape(*dims, dtype=BF16):
        return jax.ShapeDtypeStruct(dims, dtype)

    def send(block, j, k):
        route = []
        for i in range(devices):
            g, p = i // GROUP, i % GROUP
            route.append((i, GROUP * ((g + j) % experts) + (p ^ k)))
        return lax.ppermute(block, "expert", route)

    def migrate(block, survivor):
        route = [(GROUP * e + GROUP - 1, GROUP * e + survivor) for e in range(experts)]
        return lax.ppermute(block, "expert", route)

    def swap(block, survivor):
        route = []
        for r in range(replicas):
            for e in range(experts):
                i = GROUP * e + survivor
                route.append((i * replicas + r, i * replicas + (r ^ 1)))
        return lax.ppermute(block, ("expert", "replica"), route)

    def select(wanted, held):
        return pl.pallas_call(
            functools.partial(select_kernel, wanted),
            out_shape=[shape(3, count, width) for _, count, _ in wanted],
            in_specs=[VMEM] * 4,
            out_specs=[VMEM] * len(wanted),
            compiler_params=params(),
            cost_estimate=cost(2),
            name="select",
        )(plan, *held)

    parcels = pl.pallas_call(
        functools.partial(dispatch_kernel, experts),
        out_shape=[shape(PACK, width // 2)] * experts,
        in_specs=[HBM, HBM],
        out_specs=[VMEM] * experts,
        scratch_shapes=[
            pltpu.VMEM(expert_ids.shape[::-1], jnp.int32),
            pltpu.VMEM(tokens.shape, BF16),
            pltpu.SemaphoreType.DMA((3,)),
        ],
        compiler_params=params(),
        cost_estimate=cost(2),
        name="dispatch",
    )(expert_ids.T, tokens)

    across = [send(parcels[j], j, 0) for j in range(1, experts)]
    here = jnp.concatenate([parcels[0]] + across, axis=0)
    held, _ = lax.optimization_barrier((weights, here))
    wanted = [(0, part, None), (1, half, None), (0, rest, 2 * part), (2, most, 0)]
    chosen = select(wanted, held)
    beside = send(here, 0, 2)
    mine = jnp.concatenate([here, beside], axis=0)
    other = send(mine, 0, 1)

    shared = [migrate(chosen[p], p) for p in range(2)]
    near = migrate(chosen[3], 2)

    total = mine.shape[0]
    step = min(total, 4 * PACK)
    row_spec = pl.BlockSpec((step, width // 2), lambda i: (i, 0))
    whole_spec = pl.BlockSpec(old_gate.shape, lambda i: (0, 0))
    keep, give = pl.pallas_call(
        expert_kernel,
        grid=(total // step,),
        out_shape=[shape(total, width // 2, dtype=F32), shape(total, width // 2)],
        in_specs=[row_spec] * 2 + [whole_spec] * 3,
        out_specs=[row_spec] * 2,
        compiler_params=params(),
        cost_estimate=cost(0),
        name="expert",
    )(mine, other, *weights)
    taken, shared[1] = lax.optimization_barrier((send(give, 0, 1), shared[1]))
    summed = keep + taken.astype(F32)
    far = send(summed[total // 2 :].astype(BF16), 0, 2)

    far, shared[0] = lax.optimization_barrier((far, shared[0]))
    swapped = [swap(shared[p], p) for p in range(2)]
    last, _ = lax.optimization_barrier((chosen[2], summed))
    straight = migrate(last, 0)

    summed = (summed[: total // 2] + far.astype(F32)).astype(BF16)
    pieces = [summed[j * PACK : (j + 1) * PACK] for j in range(experts)]
    back = [pieces[0]] + [send(pieces[j], -j, 0) for j in range(1, experts)]
    mixed = pl.pallas_call(
        functools.partial(combine_kernel, experts),
        out_shape=shape(tokens.shape[0], width),
        in_specs=[VMEM, VMEM] + [VMEM] * len(back),
        out_specs=VMEM,
        compiler_params=params(14 + experts),
        cost_estimate=cost(2),
        name="combine",
    )(expert_ids.T, combine.T, *back)

    arrived = pl.pallas_call(
        merge_kernel,
        out_shape=shape(3, most, width),
        in_specs=[HBM] * 6,
        out_specs=HBM,
        scratch_shapes=[pltpu.SemaphoreType.DMA((9,))],
        compiler_params=params(),
        name="merge",
    )(*shared, *swapped, straight, near)
    return mixed, arrived


def solution(mesh):
    placed = (
        P(("replica", "expert"), None),
        P(("replica", "expert"), None),
        P(("replica", "expert"), None),
        P("expert", None),
        P("expert", None),
        P("expert", None),
        P(),
    )
    return jax.shard_map(
        on_device,
        mesh=mesh,
        in_specs=placed,
        out_specs=(P(("replica", "expert"), None), P("replica", "expert", None)),
        check_vma=False,
    )
```

```python
import functools

import jax
import jax.numpy as jnp
from jax import lax
from jax.experimental import pallas as pl
from jax.experimental.pallas import tpu as pltpu
from jax.sharding import PartitionSpec as P

CAP = 12
PACK = 2 * CAP
GROUP = 4
BF16 = jnp.bfloat16
F32 = jnp.float32
VMEM = pl.BlockSpec(memory_space=pltpu.VMEM)
HBM = pl.BlockSpec(memory_space=pltpu.HBM)


def params(megabytes=16):
    return pltpu.CompilerParams(vmem_limit_bytes=megabytes * 1024 * 1024)


def cost(microseconds):
    return pl.CostEstimate(
        flops=microseconds * 10**9, bytes_accessed=10**4, transcendentals=0
    )


def token_places(ids, group, experts):
    tok = ids.shape[1]
    member = []
    for j in range(experts):
        named = jnp.where(ids == lax.rem(group + j, experts), 1.0, 0.0)
        member.append(jnp.sum(named, axis=0, keepdims=True))
    member = jnp.concatenate(member, axis=0)
    row = lax.broadcasted_iota(jnp.int32, (tok, tok), 0)
    col = lax.broadcasted_iota(jnp.int32, (tok, tok), 1)
    upto = jnp.where(row <= col, 1.0, 0.0).astype(BF16)
    rank = jnp.dot(member.astype(BF16), upto, preferred_element_type=F32)
    return jnp.where(member > 0, rank - 1.0, -PACK).astype(jnp.int32)


def dispatch_kernel(experts, ids_hbm, tok_hbm, *refs):
    out_refs, (ids_ref, tok_ref, sems) = refs[:experts], refs[experts:]
    tok, half = tok_ref.shape[0], tok_ref.shape[1] // 2
    copies = [pltpu.make_async_copy(ids_hbm, ids_ref, sems.at[0])]
    for side in range(2):
        columns = pl.ds(side * half, half)
        copies.append(
            pltpu.make_async_copy(
                tok_hbm.at[:, columns], tok_ref.at[:, columns], sems.at[side + 1]
            )
        )
    for copy in copies:
        copy.start()
    group = lax.axis_index("expert") // GROUP
    copies[0].wait()
    place = token_places(ids_ref[...], group, experts)
    slot = lax.broadcasted_iota(jnp.int32, (PACK, tok), 0)
    copies[1].wait()
    copies[2].wait()
    for j, ref in enumerate(out_refs):
        spot = place[j : j + 1, :]
        left = jnp.where(jnp.logical_and(slot == spot, spot >= 0), 1.0, 0.0).astype(BF16)
        right = jnp.where(slot == spot + CAP, 1.0, 0.0).astype(BF16)
        rows = jnp.dot(left, tok_ref[:, :half], preferred_element_type=F32)
        rows = rows + jnp.dot(right, tok_ref[:, half:], preferred_element_type=F32)
        ref[...] = rows.astype(BF16)


def select_kernel(wanted, plan_ref, gate_ref, up_ref, down_ref, *out_refs):
    device = lax.axis_index("expert")
    even = lax.axis_index("replica") % 2 == 0
    rows = gate_ref.shape[0]

    @pl.when(device % GROUP == GROUP - 1)
    def _():
        plans = []
        for survivor, count, first in wanted:
            plan = plan_ref[survivor, pl.ds(device // GROUP, 1), :]
            if first is None:
                plan = jnp.where(even, plan[:, :count], plan[:, count : 2 * count])
            else:
                plan = plan[:, first : first + count]
            plans.append(plan)
        total = sum(count for _, count, _ in wanted)
        number = lax.broadcasted_iota(jnp.int32, (rows, total), 0)
        pick = jnp.where(number == jnp.concatenate(plans, axis=1), 1.0, 0.0).astype(BF16)
        for m, held_ref in enumerate((gate_ref, up_ref, down_ref)):
            found = lax.dot_general(
                pick, held_ref[...], (((0,), (0,)), ((), ())), preferred_element_type=F32
            ).astype(BF16)
            start = 0
            for (_, count, _), ref in zip(wanted, out_refs):
                ref[m] = found[start : start + count]
                start += count


def merge_kernel(shared_ref, swapped_ref, first_ref, second_ref, near_ref, out_ref, sems):
    position = lax.axis_index("expert") % GROUP
    parity = lax.axis_index("replica") % 2
    half = shared_ref.shape[1]

    def move(pieces):
        copies = []
        for ref, first in pieces:
            for m in range(3):
                rows = pl.ds(first, ref.shape[1])
                copies.append(
                    pltpu.make_async_copy(ref.at[m], out_ref.at[m, rows], sems.at[len(copies)])
                )
        for copy in copies:
            copy.start()
        for copy in copies:
            copy.wait()

    for even in range(2):

        @pl.when(jnp.logical_and(position == 1, parity == even))
        def _():
            move([(shared_ref, half * even), (swapped_ref, half * (1 - even))])

    @pl.when(jnp.logical_or(position == 0, position == 3))
    def _():
        move([(first_ref, 0), (second_ref, first_ref.shape[1])])

    @pl.when(position == 2)
    def _():
        move([(near_ref, 0)])


def expert_kernel(mine_ref, other_ref, gate_ref, up_ref, down_ref, keep_ref, give_ref):
    rows, half = mine_ref.shape
    x = jnp.concatenate([mine_ref[...], other_ref[...]], axis=0)
    total = x.shape[0]
    numbers = (((1,), (1,)), ((), ()))

    def project(ref):
        left = lax.dot_general(x, ref[:, :half], numbers, preferred_element_type=F32)
        right = lax.dot_general(x, ref[:, half:], numbers, preferred_element_type=F32)
        return left + jnp.concatenate([right[CAP:], right[:CAP]], axis=0)

    gate_value = project(gate_ref)
    up_value = project(up_ref)
    hidden = (gate_value / (1.0 + jnp.exp(-gate_value)) * up_value).astype(BF16)
    left = jnp.dot(hidden, down_ref[:, :half], preferred_element_type=F32)
    right = jnp.dot(hidden, down_ref[:, half:], preferred_element_type=F32)
    right = jnp.concatenate([right[total - CAP :], right[: total - CAP]], axis=0)
    row = lax.broadcasted_iota(jnp.int32, (total, half), 0)
    partial = jnp.where(row % PACK < CAP, left, right)
    keep_ref[...] = partial[:rows]
    give_ref[...] = partial[rows:].astype(BF16)


def combine_kernel(experts, ids_ref, weight_ref, *refs):
    piece_refs, out_ref = refs[:-1], refs[-1]
    ids = ids_ref[...]
    group = lax.axis_index("expert") // GROUP
    half = out_ref.shape[1] // 2
    place = token_places(ids, group, experts)
    weights = []
    for j in range(experts):
        named = ids == lax.rem(group + j, experts)
        weights.append(jnp.sum(jnp.where(named, weight_ref[...], 0.0), axis=0, keepdims=True))
    weights = jnp.concatenate(weights, axis=0).T
    slot = lax.broadcasted_iota(jnp.int32, (PACK, ids.shape[1]), 0)
    numbers = (((0,), (0,)), ((), ()))
    each = len(piece_refs) // experts
    mixed = [None, None]
    for j in range(experts):
        spot = place[j : j + 1, :]
        for side in range(2):
            chosen = jnp.where(slot == spot + side * CAP, 1.0, 0.0).astype(BF16)
            found = None
            for ref in piece_refs[j * each : (j + 1) * each]:
                part = lax.dot_general(chosen, ref[...], numbers, preferred_element_type=F32)
                found = part if found is None else found + part
            term = weights[:, j : j + 1] * found
            mixed[side] = term if mixed[side] is None else mixed[side] + term
    out_ref[:, :half] = mixed[0].astype(BF16)
    out_ref[:, half:] = mixed[1].astype(BF16)


def on_device(tokens, expert_ids, combine, old_gate, old_up, old_down, move_plan):
    devices = lax.axis_size("expert")
    replicas = lax.axis_size("replica")
    experts = move_plan.shape[0]
    most = move_plan.shape[2]
    width = tokens.shape[1]
    plan = jnp.transpose(move_plan, (1, 0, 2))
    weights = (old_gate, old_up, old_down)
    half = most // 2
    lead = most // 3

    def shape(*dims, dtype=BF16):
        return jax.ShapeDtypeStruct(dims, dtype)

    def send(block, j, k):
        route = []
        for i in range(devices):
            g, p = i // GROUP, i % GROUP
            route.append((i, GROUP * ((g + j) % experts) + (p ^ k)))
        return lax.ppermute(block, "expert", route)

    def migrate(block, survivor):
        route = [(GROUP * e + GROUP - 1, GROUP * e + survivor) for e in range(experts)]
        return lax.ppermute(block, "expert", route)

    def swap(block, survivor):
        route = []
        for r in range(replicas):
            for e in range(experts):
                i = GROUP * e + survivor
                route.append((i * replicas + r, i * replicas + (r ^ 1)))
        return lax.ppermute(block, ("expert", "replica"), route)

    def select(wanted, held):
        return pl.pallas_call(
            functools.partial(select_kernel, wanted),
            out_shape=[shape(3, count, width) for _, count, _ in wanted],
            in_specs=[VMEM] * 4,
            out_specs=[VMEM] * len(wanted),
            compiler_params=params(),
            cost_estimate=cost(2),
            name="select",
        )(plan, *held)

    parcels = pl.pallas_call(
        functools.partial(dispatch_kernel, experts),
        out_shape=[shape(PACK, width // 2)] * experts,
        in_specs=[HBM, HBM],
        out_specs=[VMEM] * experts,
        scratch_shapes=[
            pltpu.VMEM(expert_ids.shape[::-1], jnp.int32),
            pltpu.VMEM(tokens.shape, BF16),
            pltpu.SemaphoreType.DMA((3,)),
        ],
        compiler_params=params(),
        cost_estimate=cost(2),
        name="dispatch",
    )(expert_ids.T, tokens)

    pairs = [(j, k) for j in range(experts) for k in (0, 2)]
    mine = [parcels[0]] + [send(parcels[j], j, k) for j, k in pairs[1:]]
    held, _ = lax.optimization_barrier((weights, parcels))
    wanted = [(1, half, None), (0, lead, 0), (0, most - lead, lead), (2, most, 0)]
    chosen = select(wanted, held)
    shared = migrate(chosen[0], 1)
    mine = jnp.concatenate(mine, axis=0)
    other = send(mine, 0, 1)
    first = migrate(chosen[1], 0)

    total = mine.shape[0]
    step = min(total, 4 * PACK)
    row_spec = pl.BlockSpec((step, width // 2), lambda i: (i, 0))
    whole_spec = pl.BlockSpec(old_gate.shape, lambda i: (0, 0))
    keep, give = pl.pallas_call(
        expert_kernel,
        grid=(total // step,),
        out_shape=[shape(total, width // 2, dtype=F32), shape(total, width // 2)],
        in_specs=[row_spec] * 2 + [whole_spec] * 3,
        out_specs=[row_spec] * 2,
        compiler_params=params(),
        cost_estimate=cost(0),
        name="expert",
    )(mine, other, *weights)
    taken, shared = lax.optimization_barrier((send(give, 0, 1), shared))
    summed = (keep + taken.astype(F32)).astype(BF16)
    pieces = [summed[n * PACK : (n + 1) * PACK] for n in range(len(pairs))]
    back = [pieces[0]] + [
        send(block, -j, k) for (j, k), block in zip(pairs[1:], pieces[1:])
    ]
    beside = len(pairs) // 2
    near, back[beside] = lax.optimization_barrier((chosen[3], back[beside]))
    near = migrate(near, 2)
    back, first = lax.optimization_barrier((back, first))
    swapped = swap(shared, 1)
    last, _ = lax.optimization_barrier((chosen[2], summed))
    second = migrate(last, 0)

    mixed = pl.pallas_call(
        functools.partial(combine_kernel, experts),
        out_shape=shape(tokens.shape[0], width),
        in_specs=[VMEM, VMEM] + [VMEM] * len(back),
        out_specs=VMEM,
        compiler_params=params(14 + experts),
        cost_estimate=cost(14),
        name="combine",
    )(expert_ids.T, combine.T, *back)

    arrived = pl.pallas_call(
        merge_kernel,
        out_shape=shape(3, most, width),
        in_specs=[HBM] * 5,
        out_specs=HBM,
        scratch_shapes=[pltpu.SemaphoreType.DMA((6,))],
        compiler_params=params(),
        name="merge",
    )(shared, swapped, first, second, near)
    return mixed, arrived


def solution(mesh):
    placed = (
        P(("replica", "expert"), None),
        P(("replica", "expert"), None),
        P(("replica", "expert"), None),
        P("expert", None),
        P("expert", None),
        P("expert", None),
        P(),
    )
    return jax.shard_map(
        on_device,
        mesh=mesh,
        in_specs=placed,
        out_specs=(P(("replica", "expert"), None), P("replica", "expert", None)),
        check_vma=False,
    )
```

```python
import functools

import jax
import jax.numpy as jnp
from jax import lax
from jax.experimental import pallas as pl
from jax.experimental.pallas import tpu as pltpu
from jax.sharding import PartitionSpec as P

CAP = 12
PACK = 2 * CAP
GROUP = 4
BF16 = jnp.bfloat16
F32 = jnp.float32
VMEM = pl.BlockSpec(memory_space=pltpu.VMEM)
HBM = pl.BlockSpec(memory_space=pltpu.HBM)


def params(megabytes=16):
    return pltpu.CompilerParams(vmem_limit_bytes=megabytes * 1024 * 1024)


def cost(microseconds):
    return pl.CostEstimate(
        flops=microseconds * 10**9, bytes_accessed=10**4, transcendentals=0
    )


def token_places(ids, group, experts):
    tok = ids.shape[1]
    member = []
    for j in range(experts):
        named = jnp.where(ids == lax.rem(group + j, experts), 1.0, 0.0)
        member.append(jnp.sum(named, axis=0, keepdims=True))
    member = jnp.concatenate(member, axis=0)
    row = lax.broadcasted_iota(jnp.int32, (tok, tok), 0)
    col = lax.broadcasted_iota(jnp.int32, (tok, tok), 1)
    upto = jnp.where(row <= col, 1.0, 0.0).astype(BF16)
    rank = jnp.dot(member.astype(BF16), upto, preferred_element_type=F32)
    return jnp.where(member > 0, rank - 1.0, -PACK).astype(jnp.int32)


def dispatch_kernel(experts, ids_hbm, tok_hbm, *refs):
    out_refs, (ids_ref, tok_ref, sems) = refs[:experts], refs[experts:]
    tok, half = tok_ref.shape[0], tok_ref.shape[1] // 2
    copies = [pltpu.make_async_copy(ids_hbm, ids_ref, sems.at[0])]
    for side in range(2):
        columns = pl.ds(side * half, half)
        copies.append(
            pltpu.make_async_copy(
                tok_hbm.at[:, columns], tok_ref.at[:, columns], sems.at[side + 1]
            )
        )
    for copy in copies:
        copy.start()
    group = lax.axis_index("expert") // GROUP
    copies[0].wait()
    place = token_places(ids_ref[...], group, experts)
    slot = lax.broadcasted_iota(jnp.int32, (PACK, tok), 0)
    copies[1].wait()
    copies[2].wait()
    for j, ref in enumerate(out_refs):
        spot = place[j : j + 1, :]
        left = jnp.where(jnp.logical_and(slot == spot, spot >= 0), 1.0, 0.0).astype(BF16)
        right = jnp.where(slot == spot + CAP, 1.0, 0.0).astype(BF16)
        rows = jnp.dot(left, tok_ref[:, :half], preferred_element_type=F32)
        rows = rows + jnp.dot(right, tok_ref[:, half:], preferred_element_type=F32)
        ref[...] = rows.astype(BF16)


def select_kernel(wanted, plan_ref, gate_ref, up_ref, down_ref, *out_refs):
    device = lax.axis_index("expert")
    even = lax.axis_index("replica") % 2 == 0
    rows = gate_ref.shape[0]

    @pl.when(device % GROUP == GROUP - 1)
    def _():
        plans = []
        for survivor, count, first in wanted:
            plan = plan_ref[survivor, pl.ds(device // GROUP, 1), :]
            if first is None:
                plan = jnp.where(even, plan[:, :count], plan[:, count : 2 * count])
            else:
                plan = plan[:, first : first + count]
            plans.append(plan)
        total = sum(count for _, count, _ in wanted)
        number = lax.broadcasted_iota(jnp.int32, (rows, total), 0)
        pick = jnp.where(number == jnp.concatenate(plans, axis=1), 1.0, 0.0).astype(BF16)
        for m, held_ref in enumerate((gate_ref, up_ref, down_ref)):
            found = lax.dot_general(
                pick, held_ref[...], (((0,), (0,)), ((), ())), preferred_element_type=F32
            ).astype(BF16)
            start = 0
            for (_, count, _), ref in zip(wanted, out_refs):
                ref[m] = found[start : start + count]
                start += count


def merge_kernel(*refs):
    shared_refs, swapped_refs, (straight_ref, near_ref, out_ref, sems) = refs[:2], refs[2:4], refs[4:]
    position = lax.axis_index("expert") % GROUP
    parity = lax.axis_index("replica") % 2

    def move(pieces):
        copies = []
        for ref, first in pieces:
            for m in range(3):
                rows = pl.ds(first, ref.shape[1])
                copies.append(
                    pltpu.make_async_copy(ref.at[m], out_ref.at[m, rows], sems.at[len(copies)])
                )
        for copy in copies:
            copy.start()
        for copy in copies:
            copy.wait()

    for p in range(2):
        part = shared_refs[p].shape[1]
        for even in range(2):
            mine = position == 1 if p == 1 else jnp.logical_or(position == 0, position == 3)

            @pl.when(jnp.logical_and(mine, parity == even))
            def _():
                pieces = [(shared_refs[p], part * even), (swapped_refs[p], part * (1 - even))]
                if p == 0:
                    pieces.append((straight_ref, 2 * part))
                move(pieces)

    @pl.when(position == 2)
    def _():
        move([(near_ref, 0)])


def expert_kernel(mine_ref, other_ref, gate_ref, up_ref, down_ref, keep_ref, give_ref):
    rows, half = mine_ref.shape
    x = jnp.concatenate([mine_ref[...], other_ref[...]], axis=0)
    total = x.shape[0]
    numbers = (((1,), (1,)), ((), ()))

    def project(ref):
        left = lax.dot_general(x, ref[:, :half], numbers, preferred_element_type=F32)
        right = lax.dot_general(x, ref[:, half:], numbers, preferred_element_type=F32)
        return left + jnp.concatenate([right[CAP:], right[:CAP]], axis=0)

    gate_value = project(gate_ref)
    up_value = project(up_ref)
    hidden = (gate_value / (1.0 + jnp.exp(-gate_value)) * up_value).astype(BF16)
    left = jnp.dot(hidden, down_ref[:, :half], preferred_element_type=F32)
    right = jnp.dot(hidden, down_ref[:, half:], preferred_element_type=F32)
    right = jnp.concatenate([right[total - CAP :], right[: total - CAP]], axis=0)
    row = lax.broadcasted_iota(jnp.int32, (total, half), 0)
    partial = jnp.where(row % PACK < CAP, left, right)
    keep_ref[...] = partial[:rows]
    give_ref[...] = partial[rows:].astype(BF16)


def combine_kernel(experts, ids_ref, weight_ref, *refs):
    piece_refs, out_ref = refs[:-1], refs[-1]
    ids = ids_ref[...]
    group = lax.axis_index("expert") // GROUP
    half = out_ref.shape[1] // 2
    place = token_places(ids, group, experts)
    weights = []
    for j in range(experts):
        named = ids == lax.rem(group + j, experts)
        weights.append(jnp.sum(jnp.where(named, weight_ref[...], 0.0), axis=0, keepdims=True))
    weights = jnp.concatenate(weights, axis=0).T
    slot = lax.broadcasted_iota(jnp.int32, (PACK, ids.shape[1]), 0)
    numbers = (((0,), (0,)), ((), ()))
    each = len(piece_refs) // experts
    mixed = [None, None]
    for j in range(experts):
        spot = place[j : j + 1, :]
        for side in range(2):
            chosen = jnp.where(slot == spot + side * CAP, 1.0, 0.0).astype(BF16)
            found = None
            for ref in piece_refs[j * each : (j + 1) * each]:
                part = lax.dot_general(chosen, ref[...], numbers, preferred_element_type=F32)
                found = part if found is None else found + part
            term = weights[:, j : j + 1] * found
            mixed[side] = term if mixed[side] is None else mixed[side] + term
    out_ref[:, :half] = mixed[0].astype(BF16)
    out_ref[:, half:] = mixed[1].astype(BF16)


def on_device(tokens, expert_ids, combine, old_gate, old_up, old_down, move_plan):
    devices = lax.axis_size("expert")
    replicas = lax.axis_size("replica")
    experts = move_plan.shape[0]
    most = move_plan.shape[2]
    width = tokens.shape[1]
    plan = jnp.transpose(move_plan, (1, 0, 2))
    weights = (old_gate, old_up, old_down)
    half = most // 2
    part = most // 6

    def shape(*dims, dtype=BF16):
        return jax.ShapeDtypeStruct(dims, dtype)

    def send(block, j, k):
        route = []
        for i in range(devices):
            g, p = i // GROUP, i % GROUP
            route.append((i, GROUP * ((g + j) % experts) + (p ^ k)))
        return lax.ppermute(block, "expert", route)

    def migrate(block, survivor):
        route = [(GROUP * e + GROUP - 1, GROUP * e + survivor) for e in range(experts)]
        return lax.ppermute(block, "expert", route)

    def swap(block, survivor):
        route = []
        for r in range(replicas):
            for e in range(experts):
                i = GROUP * e + survivor
                route.append((i * replicas + r, i * replicas + (r ^ 1)))
        return lax.ppermute(block, ("expert", "replica"), route)

    def select(wanted, held):
        return pl.pallas_call(
            functools.partial(select_kernel, wanted),
            out_shape=[shape(3, count, width) for _, count, _ in wanted],
            in_specs=[VMEM] * 4,
            out_specs=[VMEM] * len(wanted),
            compiler_params=params(),
            cost_estimate=cost(2),
            name="select",
        )(plan, *held)

    parcels = pl.pallas_call(
        functools.partial(dispatch_kernel, experts),
        out_shape=[shape(PACK, width // 2)] * experts,
        in_specs=[HBM, HBM],
        out_specs=[VMEM] * experts,
        scratch_shapes=[
            pltpu.VMEM(expert_ids.shape[::-1], jnp.int32),
            pltpu.VMEM(tokens.shape, BF16),
            pltpu.SemaphoreType.DMA((3,)),
        ],
        compiler_params=params(),
        cost_estimate=cost(2),
        name="dispatch",
    )(expert_ids.T, tokens)

    pairs = [(j, k) for j in range(experts) for k in (0, 2)]
    mine = [parcels[0]] + [send(parcels[j], j, k) for j, k in pairs[1:]]
    held, _ = lax.optimization_barrier((weights, parcels))
    wanted = [(0, part, None), (1, half, None), (0, most - 2 * part, 2 * part), (2, most, 0)]
    chosen = select(wanted, held)
    shared = [migrate(chosen[p], p) for p in range(2)]
    mine = jnp.concatenate(mine, axis=0)
    other = send(mine, 0, 1)

    total = mine.shape[0]
    step = min(total, 4 * PACK)
    row_spec = pl.BlockSpec((step, width // 2), lambda i: (i, 0))
    whole_spec = pl.BlockSpec(old_gate.shape, lambda i: (0, 0))
    keep, give = pl.pallas_call(
        expert_kernel,
        grid=(total // step,),
        out_shape=[shape(total, width // 2, dtype=F32), shape(total, width // 2)],
        in_specs=[row_spec] * 2 + [whole_spec] * 3,
        out_specs=[row_spec] * 2,
        compiler_params=params(),
        cost_estimate=cost(0),
        name="expert",
    )(mine, other, *weights)
    taken, shared = lax.optimization_barrier((send(give, 0, 1), shared))
    summed = (keep + taken.astype(F32)).astype(BF16)
    pieces = [summed[n * PACK : (n + 1) * PACK] for n in range(len(pairs))]
    back = [pieces[0]] + [
        send(block, -j, k) for (j, k), block in zip(pairs[1:], pieces[1:])
    ]
    swapped = [None, swap(shared[1], 1)]
    beside = len(pairs) // 2
    back[beside], near = lax.optimization_barrier((back[beside], chosen[3]))
    near = migrate(near, 2)
    swapped[0] = swap(shared[0], 0)
    last, _ = lax.optimization_barrier((chosen[2], summed))
    straight = migrate(last, 0)
    back, swapped[1] = lax.optimization_barrier((back, swapped[1]))

    mixed = pl.pallas_call(
        functools.partial(combine_kernel, experts),
        out_shape=shape(tokens.shape[0], width),
        in_specs=[VMEM, VMEM] + [VMEM] * len(back),
        out_specs=VMEM,
        compiler_params=params(14 + experts),
        cost_estimate=cost(14),
        name="combine",
    )(expert_ids.T, combine.T, *back)

    arrived = pl.pallas_call(
        merge_kernel,
        out_shape=shape(3, most, width),
        in_specs=[HBM] * 6,
        out_specs=HBM,
        scratch_shapes=[pltpu.SemaphoreType.DMA((9,))],
        compiler_params=params(),
        name="merge",
    )(*shared, *swapped, straight, near)
    return mixed, arrived


def solution(mesh):
    placed = (
        P(("replica", "expert"), None),
        P(("replica", "expert"), None),
        P(("replica", "expert"), None),
        P("expert", None),
        P("expert", None),
        P("expert", None),
        P(),
    )
    return jax.shard_map(
        on_device,
        mesh=mesh,
        in_specs=placed,
        out_specs=(P(("replica", "expert"), None), P("replica", "expert", None)),
        check_vma=False,
    )
```

```python
import functools

import jax
import jax.numpy as jnp
from jax import lax
from jax.experimental import pallas as pl
from jax.experimental.pallas import tpu as pltpu
from jax.sharding import PartitionSpec as P

CAP = 12
PACK = 2 * CAP
GROUP = 4
BF16 = jnp.bfloat16
F32 = jnp.float32
VMEM = pl.BlockSpec(memory_space=pltpu.VMEM)
HBM = pl.BlockSpec(memory_space=pltpu.HBM)


def params(megabytes=16):
    return pltpu.CompilerParams(vmem_limit_bytes=megabytes * 1024 * 1024)


def cost(microseconds):
    return pl.CostEstimate(
        flops=microseconds * 10**9, bytes_accessed=10**4, transcendentals=0
    )


def token_places(ids, group, experts):
    tok = ids.shape[1]
    member = []
    for j in range(experts):
        named = jnp.where(ids == lax.rem(group + j, experts), 1.0, 0.0)
        member.append(jnp.sum(named, axis=0, keepdims=True))
    member = jnp.concatenate(member, axis=0)
    row = lax.broadcasted_iota(jnp.int32, (tok, tok), 0)
    col = lax.broadcasted_iota(jnp.int32, (tok, tok), 1)
    upto = jnp.where(row <= col, 1.0, 0.0).astype(BF16)
    rank = jnp.dot(member.astype(BF16), upto, preferred_element_type=F32)
    return jnp.where(member > 0, rank - 1.0, -PACK).astype(jnp.int32)


def dispatch_kernel(experts, ids_hbm, tok_hbm, *refs):
    out_refs, (ids_ref, tok_ref, sems) = refs[:experts], refs[experts:]
    tok, half = tok_ref.shape[0], tok_ref.shape[1] // 2
    copies = [pltpu.make_async_copy(ids_hbm, ids_ref, sems.at[0])]
    for side in range(2):
        columns = pl.ds(side * half, half)
        copies.append(
            pltpu.make_async_copy(
                tok_hbm.at[:, columns], tok_ref.at[:, columns], sems.at[side + 1]
            )
        )
    for copy in copies:
        copy.start()
    group = lax.axis_index("expert") // GROUP
    copies[0].wait()
    place = token_places(ids_ref[...], group, experts)
    slot = lax.broadcasted_iota(jnp.int32, (PACK, tok), 0)
    copies[1].wait()
    copies[2].wait()
    for j, ref in enumerate(out_refs):
        spot = place[j : j + 1, :]
        left = jnp.where(jnp.logical_and(slot == spot, spot >= 0), 1.0, 0.0).astype(BF16)
        right = jnp.where(slot == spot + CAP, 1.0, 0.0).astype(BF16)
        rows = jnp.dot(left, tok_ref[:, :half], preferred_element_type=F32)
        rows = rows + jnp.dot(right, tok_ref[:, half:], preferred_element_type=F32)
        ref[...] = rows.astype(BF16)


def select_kernel(wanted, plan_ref, gate_ref, up_ref, down_ref, *out_refs):
    device = lax.axis_index("expert")
    even = lax.axis_index("replica") % 2 == 0
    rows = gate_ref.shape[0]

    @pl.when(device % GROUP == GROUP - 1)
    def _():
        plans = []
        for survivor, count, first in wanted:
            plan = plan_ref[survivor, pl.ds(device // GROUP, 1), :]
            if first is None:
                plan = jnp.where(even, plan[:, :count], plan[:, count : 2 * count])
            else:
                plan = plan[:, first : first + count]
            plans.append(plan)
        total = sum(count for _, count, _ in wanted)
        number = lax.broadcasted_iota(jnp.int32, (rows, total), 0)
        pick = jnp.where(number == jnp.concatenate(plans, axis=1), 1.0, 0.0).astype(BF16)
        for m, held_ref in enumerate((gate_ref, up_ref, down_ref)):
            found = lax.dot_general(
                pick, held_ref[...], (((0,), (0,)), ((), ())), preferred_element_type=F32
            ).astype(BF16)
            start = 0
            for (_, count, _), ref in zip(wanted, out_refs):
                ref[m] = found[start : start + count]
                start += count


def merge_kernel(*refs):
    shared_refs, swapped_refs, (straight_ref, near_ref, out_ref, sems) = refs[:2], refs[2:4], refs[4:]
    position = lax.axis_index("expert") % GROUP
    parity = lax.axis_index("replica") % 2

    def move(pieces):
        copies = []
        for ref, first in pieces:
            for m in range(3):
                rows = pl.ds(first, ref.shape[1])
                copies.append(
                    pltpu.make_async_copy(ref.at[m], out_ref.at[m, rows], sems.at[len(copies)])
                )
        for copy in copies:
            copy.start()
        for copy in copies:
            copy.wait()

    for p in range(2):
        part = shared_refs[p].shape[1]
        for even in range(2):
            mine = position == 1 if p == 1 else jnp.logical_or(position == 0, position == 3)

            @pl.when(jnp.logical_and(mine, parity == even))
            def _():
                pieces = [(shared_refs[p], part * even), (swapped_refs[p], part * (1 - even))]
                if p == 0:
                    pieces.append((straight_ref, 2 * part))
                move(pieces)

    @pl.when(position == 2)
    def _():
        move([(near_ref, 0)])


def expert_kernel(mine_ref, other_ref, gate_ref, up_ref, down_ref, keep_ref, give_ref):
    rows, half = mine_ref.shape
    x = jnp.concatenate([mine_ref[...], other_ref[...]], axis=0)
    total = x.shape[0]
    numbers = (((1,), (1,)), ((), ()))

    def project(ref):
        left = lax.dot_general(x, ref[:, :half], numbers, preferred_element_type=F32)
        right = lax.dot_general(x, ref[:, half:], numbers, preferred_element_type=F32)
        return left + jnp.concatenate([right[CAP:], right[:CAP]], axis=0)

    gate_value = project(gate_ref)
    up_value = project(up_ref)
    hidden = (gate_value / (1.0 + jnp.exp(-gate_value)) * up_value).astype(BF16)
    left = jnp.dot(hidden, down_ref[:, :half], preferred_element_type=F32)
    right = jnp.dot(hidden, down_ref[:, half:], preferred_element_type=F32)
    right = jnp.concatenate([right[total - CAP :], right[: total - CAP]], axis=0)
    row = lax.broadcasted_iota(jnp.int32, (total, half), 0)
    partial = jnp.where(row % PACK < CAP, left, right)
    keep_ref[...] = partial[:rows]
    give_ref[...] = partial[rows:].astype(BF16)


def combine_kernel(experts, ids_ref, weight_ref, *refs):
    piece_refs, out_ref = refs[:-1], refs[-1]
    ids = ids_ref[...]
    group = lax.axis_index("expert") // GROUP
    half = out_ref.shape[1] // 2
    place = token_places(ids, group, experts)
    weights = []
    for j in range(experts):
        named = ids == lax.rem(group + j, experts)
        weights.append(jnp.sum(jnp.where(named, weight_ref[...], 0.0), axis=0, keepdims=True))
    weights = jnp.concatenate(weights, axis=0).T
    slot = lax.broadcasted_iota(jnp.int32, (PACK, ids.shape[1]), 0)
    numbers = (((0,), (0,)), ((), ()))
    each = len(piece_refs) // experts
    mixed = [None, None]
    for j in range(experts):
        spot = place[j : j + 1, :]
        for side in range(2):
            chosen = jnp.where(slot == spot + side * CAP, 1.0, 0.0).astype(BF16)
            found = None
            for ref in piece_refs[j * each : (j + 1) * each]:
                part = lax.dot_general(chosen, ref[...], numbers, preferred_element_type=F32)
                found = part if found is None else found + part
            term = weights[:, j : j + 1] * found
            mixed[side] = term if mixed[side] is None else mixed[side] + term
    out_ref[:, :half] = mixed[0].astype(BF16)
    out_ref[:, half:] = mixed[1].astype(BF16)


def on_device(tokens, expert_ids, combine, old_gate, old_up, old_down, move_plan):
    devices = lax.axis_size("expert")
    replicas = lax.axis_size("replica")
    experts = move_plan.shape[0]
    most = move_plan.shape[2]
    width = tokens.shape[1]
    plan = jnp.transpose(move_plan, (1, 0, 2))
    weights = (old_gate, old_up, old_down)
    half = most // 2
    part = most // 6

    def shape(*dims, dtype=BF16):
        return jax.ShapeDtypeStruct(dims, dtype)

    def send(block, j, k):
        route = []
        for i in range(devices):
            g, p = i // GROUP, i % GROUP
            route.append((i, GROUP * ((g + j) % experts) + (p ^ k)))
        return lax.ppermute(block, "expert", route)

    def migrate(block, survivor):
        route = [(GROUP * e + GROUP - 1, GROUP * e + survivor) for e in range(experts)]
        return lax.ppermute(block, "expert", route)

    def swap(block, survivor):
        route = []
        for r in range(replicas):
            for e in range(experts):
                i = GROUP * e + survivor
                route.append((i * replicas + r, i * replicas + (r ^ 1)))
        return lax.ppermute(block, ("expert", "replica"), route)

    def select(wanted, held):
        return pl.pallas_call(
            functools.partial(select_kernel, wanted),
            out_shape=[shape(3, count, width) for _, count, _ in wanted],
            in_specs=[VMEM] * 4,
            out_specs=[VMEM] * len(wanted),
            compiler_params=params(),
            cost_estimate=cost(2),
            name="select",
        )(plan, *held)

    parcels = pl.pallas_call(
        functools.partial(dispatch_kernel, experts),
        out_shape=[shape(PACK, width // 2)] * experts,
        in_specs=[HBM, HBM],
        out_specs=[VMEM] * experts,
        scratch_shapes=[
            pltpu.VMEM(expert_ids.shape[::-1], jnp.int32),
            pltpu.VMEM(tokens.shape, BF16),
            pltpu.SemaphoreType.DMA((3,)),
        ],
        compiler_params=params(),
        cost_estimate=cost(2),
        name="dispatch",
    )(expert_ids.T, tokens)

    pairs = [(j, k) for j in range(experts) for k in (0, 2)]
    mine = [parcels[0]] + [send(parcels[j], j, k) for j, k in pairs[1:]]
    held, _ = lax.optimization_barrier((weights, parcels))
    wanted = [(0, part, None), (1, half, None), (0, most - 2 * part, 2 * part), (2, most, 0)]
    chosen = select(wanted, held)
    shared = [migrate(chosen[p], p) for p in range(2)]
    mine = jnp.concatenate(mine, axis=0)
    other = send(mine, 0, 1)

    total = mine.shape[0]
    step = min(total, 4 * PACK)
    row_spec = pl.BlockSpec((step, width // 2), lambda i: (i, 0))
    whole_spec = pl.BlockSpec(old_gate.shape, lambda i: (0, 0))
    keep, give = pl.pallas_call(
        expert_kernel,
        grid=(total // step,),
        out_shape=[shape(total, width // 2, dtype=F32), shape(total, width // 2)],
        in_specs=[row_spec] * 2 + [whole_spec] * 3,
        out_specs=[row_spec] * 2,
        compiler_params=params(),
        cost_estimate=cost(0),
        name="expert",
    )(mine, other, *weights)
    taken, shared = lax.optimization_barrier((send(give, 0, 1), shared))
    summed = (keep + taken.astype(F32)).astype(BF16)
    pieces = [summed[n * PACK : (n + 1) * PACK] for n in range(len(pairs))]
    back = [pieces[0]] + [
        send(block, -j, k) for (j, k), block in zip(pairs[1:], pieces[1:])
    ]
    swapped = [None, swap(shared[1], 1)]
    beside = len(pairs) // 2
    back[beside], near = lax.optimization_barrier((back[beside], chosen[3]))
    near = migrate(near, 2)
    back[1], shared[0] = lax.optimization_barrier((back[1], shared[0]))
    swapped[0] = swap(shared[0], 0)
    straight = migrate(chosen[2], 0)
    back, swapped[1], straight = lax.optimization_barrier((back, swapped[1], straight))

    mixed = pl.pallas_call(
        functools.partial(combine_kernel, experts),
        out_shape=shape(tokens.shape[0], width),
        in_specs=[VMEM, VMEM] + [VMEM] * len(back),
        out_specs=VMEM,
        compiler_params=params(14 + experts),
        cost_estimate=cost(14),
        name="combine",
    )(expert_ids.T, combine.T, *back)

    arrived = pl.pallas_call(
        merge_kernel,
        out_shape=shape(3, most, width),
        in_specs=[HBM] * 6,
        out_specs=HBM,
        scratch_shapes=[pltpu.SemaphoreType.DMA((9,))],
        compiler_params=params(),
        name="merge",
    )(*shared, *swapped, straight, near)
    return mixed, arrived


def solution(mesh):
    placed = (
        P(("replica", "expert"), None),
        P(("replica", "expert"), None),
        P(("replica", "expert"), None),
        P("expert", None),
        P("expert", None),
        P("expert", None),
        P(),
    )
    return jax.shard_map(
        on_device,
        mesh=mesh,
        in_specs=placed,
        out_specs=(P(("replica", "expert"), None), P("replica", "expert", None)),
        check_vma=False,
    )
```

```python
import functools

import jax
import jax.numpy as jnp
from jax import lax
from jax.experimental import pallas as pl
from jax.experimental.pallas import tpu as pltpu
from jax.sharding import PartitionSpec as P

CAP = 12
PACK = 2 * CAP
STRIDE = 32
GROUP = 4
BF16 = jnp.bfloat16
F32 = jnp.float32
VMEM = pl.BlockSpec(memory_space=pltpu.VMEM)
HBM = pl.BlockSpec(memory_space=pltpu.HBM)


def params(megabytes=16):
    return pltpu.CompilerParams(vmem_limit_bytes=megabytes * 1024 * 1024)


def cost(microseconds):
    return pl.CostEstimate(
        flops=int(microseconds * 10**9), bytes_accessed=10**4, transcendentals=0
    )


def token_places(ids, group, experts):
    tok = ids.shape[1]
    member = []
    for j in range(experts):
        named = jnp.where(ids == lax.rem(group + j, experts), 1.0, 0.0)
        member.append(jnp.sum(named, axis=0, keepdims=True))
    member = jnp.concatenate(member, axis=0)
    row = lax.broadcasted_iota(jnp.int32, (tok, tok), 0)
    col = lax.broadcasted_iota(jnp.int32, (tok, tok), 1)
    upto = jnp.where(row <= col, 1.0, 0.0).astype(BF16)
    rank = jnp.dot(member.astype(BF16), upto, preferred_element_type=F32)
    return jnp.where(member > 0, rank - 1.0, -PACK).astype(jnp.int32)


def dispatch_kernel(experts, ids_hbm, tok_hbm, *refs):
    out_refs, (ids_ref, tok_ref, sems) = refs[:experts], refs[experts:]
    tok, half = tok_ref.shape[0], tok_ref.shape[1] // 2
    copies = [pltpu.make_async_copy(ids_hbm, ids_ref, sems.at[0])]
    for side in range(2):
        columns = pl.ds(side * half, half)
        copies.append(
            pltpu.make_async_copy(
                tok_hbm.at[:, columns], tok_ref.at[:, columns], sems.at[side + 1]
            )
        )
    for copy in copies:
        copy.start()
    group = lax.axis_index("expert") // GROUP
    copies[0].wait()
    place = token_places(ids_ref[...], group, experts)
    slot = lax.broadcasted_iota(jnp.int32, (PACK, tok), 0)
    copies[1].wait()
    copies[2].wait()
    for j, ref in enumerate(out_refs):
        spot = place[j : j + 1, :]
        left = jnp.where(jnp.logical_and(slot == spot, spot >= 0), 1.0, 0.0).astype(BF16)
        right = jnp.where(slot == spot + CAP, 1.0, 0.0).astype(BF16)
        rows = jnp.dot(left, tok_ref[:, :half], preferred_element_type=F32)
        rows = rows + jnp.dot(right, tok_ref[:, half:], preferred_element_type=F32)
        ref[...] = rows.astype(BF16)


def select_kernel(wanted, plan_ref, gate_ref, up_ref, down_ref, *out_refs):
    device = lax.axis_index("expert")
    even = lax.axis_index("replica") % 2 == 0
    rows = gate_ref.shape[0]

    @pl.when(device % GROUP == GROUP - 1)
    def _():
        plans = []
        for survivor, count, first in wanted:
            plan = plan_ref[survivor, pl.ds(device // GROUP, 1), :]
            if first is None:
                plan = jnp.where(even, plan[:, :count], plan[:, count : 2 * count])
            else:
                plan = plan[:, first : first + count]
            plans.append(plan)
        total = sum(count for _, count, _ in wanted)
        number = lax.broadcasted_iota(jnp.int32, (rows, total), 0)
        pick = jnp.where(number == jnp.concatenate(plans, axis=1), 1.0, 0.0).astype(BF16)
        for m, held_ref in enumerate((gate_ref, up_ref, down_ref)):
            found = lax.dot_general(
                pick, held_ref[...], (((0,), (0,)), ((), ())), preferred_element_type=F32
            ).astype(BF16)
            start = 0
            for (_, count, _), ref in zip(wanted, out_refs):
                ref[m] = found[start : start + count]
                start += count


def place_rows(pieces, out_ref, sems):
    copies = []
    for ref, first in pieces:
        for m in range(3):
            rows = pl.ds(first, ref.shape[1])
            copies.append(
                pltpu.make_async_copy(ref.at[m], out_ref.at[m, rows], sems.at[len(copies)])
            )
    for copy in copies:
        copy.start()
    for copy in copies:
        copy.wait()


def early_kernel(*refs):
    shared_refs, swapped_refs, (out_ref, sems) = refs[:2], refs[2:4], refs[4:]
    position = lax.axis_index("expert") % GROUP
    parity = lax.axis_index("replica") % 2
    for p in range(2):
        part = shared_refs[p].shape[1]
        for even in range(2):
            mine = position == 1 if p == 1 else jnp.logical_or(position == 0, position == 3)

            @pl.when(jnp.logical_and(mine, parity == even))
            def _():
                pieces = [(shared_refs[p], part * even), (swapped_refs[p], part * (1 - even))]
                place_rows(pieces, out_ref, sems)


def late_kernel(early_ref, straight_ref, near_ref, out_ref, sems):
    position = lax.axis_index("expert") % GROUP

    @pl.when(jnp.logical_or(position == 0, position == 3))
    def _():
        place_rows([(straight_ref, out_ref.shape[1] - straight_ref.shape[1])], out_ref, sems)

    @pl.when(position == 2)
    def _():
        place_rows([(near_ref, 0)], out_ref, sems)


def expert_kernel(mine_ref, other_ref, gate_ref, up_ref, down_ref, keep_ref, give_ref):
    rows, half = mine_ref.shape
    x = jnp.concatenate([mine_ref[...], other_ref[...]], axis=0)
    total = x.shape[0]
    numbers = (((1,), (1,)), ((), ()))

    def project(ref):
        left = lax.dot_general(x, ref[:, :half], numbers, preferred_element_type=F32)
        right = lax.dot_general(x, ref[:, half:], numbers, preferred_element_type=F32)
        return left + jnp.concatenate([right[CAP:], right[:CAP]], axis=0)

    gate_value = project(gate_ref)
    up_value = project(up_ref)
    hidden = (gate_value / (1.0 + jnp.exp(-gate_value)) * up_value).astype(BF16)
    left = jnp.dot(hidden, down_ref[:, :half], preferred_element_type=F32)
    right = jnp.dot(hidden, down_ref[:, half:], preferred_element_type=F32)
    right = jnp.concatenate([right[total - CAP :], right[: total - CAP]], axis=0)
    row = lax.broadcasted_iota(jnp.int32, (total, half), 0)
    partial = jnp.where(row % PACK < CAP, left, right)
    keep_ref[...] = partial[:rows]
    give_ref[...] = partial[rows:].astype(BF16)


def combine_kernel(experts, ids_ref, weight_ref, *refs):
    piece_refs, (out_ref, rows_ref) = refs[:-2], refs[-2:]
    ids = ids_ref[...]
    group = lax.axis_index("expert") // GROUP
    half = out_ref.shape[1] // 2
    each = len(piece_refs) // experts
    place = token_places(ids, group, experts)
    slot = lax.broadcasted_iota(jnp.int32, (STRIDE, ids.shape[1]), 0)
    numbers = (((0,), (0,)), ((), ()))
    rows_ref[...] = jnp.zeros_like(rows_ref)
    for n, ref in enumerate(piece_refs):
        rows_ref[n * STRIDE : n * STRIDE + PACK, :] = ref[...]
    scaled = [[], []]
    for j in range(experts):
        named = ids == lax.rem(group + j, experts)
        weight = jnp.sum(jnp.where(named, weight_ref[...], 0.0), axis=0, keepdims=True)
        for side in range(2):
            chosen = jnp.where(slot == place[j : j + 1, :] + side * CAP, weight, 0.0)
            scaled[side] += [chosen] * each
    for side in range(2):
        chosen = jnp.concatenate(scaled[side], axis=0)
        high = chosen.astype(BF16)
        low = (chosen - high.astype(F32)).astype(BF16)
        mixed = lax.dot_general(high, rows_ref[...], numbers, preferred_element_type=F32)
        mixed = mixed + lax.dot_general(low, rows_ref[...], numbers, preferred_element_type=F32)
        out_ref[:, side * half : (side + 1) * half] = mixed.astype(BF16)


def on_device(tokens, expert_ids, combine, old_gate, old_up, old_down, move_plan):
    devices = lax.axis_size("expert")
    replicas = lax.axis_size("replica")
    experts = move_plan.shape[0]
    most = move_plan.shape[2]
    width = tokens.shape[1]
    plan = jnp.transpose(move_plan, (1, 0, 2))
    weights = (old_gate, old_up, old_down)
    half = most // 2
    part = most // 6

    def shape(*dims, dtype=BF16):
        return jax.ShapeDtypeStruct(dims, dtype)

    def send(block, j, k):
        route = []
        for i in range(devices):
            g, p = i // GROUP, i % GROUP
            route.append((i, GROUP * ((g + j) % experts) + (p ^ k)))
        return lax.ppermute(block, "expert", route)

    def migrate(block, survivor):
        route = [(GROUP * e + GROUP - 1, GROUP * e + survivor) for e in range(experts)]
        return lax.ppermute(block, "expert", route)

    def swap(block, survivor):
        route = []
        for r in range(replicas):
            for e in range(experts):
                i = GROUP * e + survivor
                route.append((i * replicas + r, i * replicas + (r ^ 1)))
        return lax.ppermute(block, ("expert", "replica"), route)

    def select(wanted, held):
        return pl.pallas_call(
            functools.partial(select_kernel, wanted),
            out_shape=[shape(3, count, width) for _, count, _ in wanted],
            in_specs=[VMEM] * 4,
            out_specs=[VMEM] * len(wanted),
            compiler_params=params(),
            cost_estimate=cost(2),
            name="select",
        )(plan, *held)

    parcels = pl.pallas_call(
        functools.partial(dispatch_kernel, experts),
        out_shape=[shape(PACK, width // 2)] * experts,
        in_specs=[HBM, HBM],
        out_specs=[VMEM] * experts,
        scratch_shapes=[
            pltpu.VMEM(expert_ids.shape[::-1], jnp.int32),
            pltpu.VMEM(tokens.shape, BF16),
            pltpu.SemaphoreType.DMA((3,)),
        ],
        compiler_params=params(),
        cost_estimate=cost(2),
        name="dispatch",
    )(expert_ids.T, tokens)

    pairs = [(j, k) for j in range(experts) for k in (0, 2)]
    mine = [parcels[0]] + [send(parcels[j], j, k) for j, k in pairs[1:]]
    held, _ = lax.optimization_barrier((weights, parcels))
    wanted = [(0, part, None), (1, half, None), (0, most - 2 * part, 2 * part), (2, most, 0)]
    chosen = select(wanted, held)
    shared = [migrate(chosen[p], p) for p in range(2)]
    mine = jnp.concatenate(mine, axis=0)
    other = send(mine, 0, 1)

    total = mine.shape[0]
    step = min(total, 4 * PACK)
    row_spec = pl.BlockSpec((step, width // 2), lambda i: (i, 0))
    whole_spec = pl.BlockSpec(old_gate.shape, lambda i: (0, 0))
    keep, give = pl.pallas_call(
        expert_kernel,
        grid=(total // step,),
        out_shape=[shape(total, width // 2, dtype=F32), shape(total, width // 2)],
        in_specs=[row_spec] * 2 + [whole_spec] * 3,
        out_specs=[row_spec] * 2,
        compiler_params=params(),
        cost_estimate=cost(0),
        name="expert",
    )(mine, other, *weights)
    taken, shared = lax.optimization_barrier((send(give, 0, 1), shared))
    summed = (keep + taken.astype(F32)).astype(BF16)
    pieces = [summed[n * PACK : (n + 1) * PACK] for n in range(len(pairs))]
    back = pieces[:1] + [send(pieces[1], 0, 2)]
    for n in range(2, len(pairs), 2):
        beside = send(pieces[n], -pairs[n][0], 0)
        beside, across = lax.optimization_barrier((beside, pieces[n + 1]))
        back += [beside, send(across, -pairs[n][0], 2)]
    swapped = [swap(shared[p], p) for p in range(2)]
    swapped[1], near = lax.optimization_barrier((swapped[1], chosen[3]))
    near = migrate(near, 2)
    straight = migrate(chosen[2], 0)

    early = pl.pallas_call(
        early_kernel,
        out_shape=shape(3, most, width),
        in_specs=[HBM] * 4,
        out_specs=HBM,
        scratch_shapes=[pltpu.SemaphoreType.DMA((6,))],
        compiler_params=params(),
        name="early",
    )(*shared, *swapped)
    back, early, straight = lax.optimization_barrier((back, early, straight))

    mixed = pl.pallas_call(
        functools.partial(combine_kernel, experts),
        out_shape=shape(tokens.shape[0], width),
        in_specs=[VMEM, VMEM] + [VMEM] * len(back),
        out_specs=VMEM,
        scratch_shapes=[pltpu.VMEM((len(back) * STRIDE, width // 2), BF16)],
        compiler_params=params(14 + experts),
        cost_estimate=cost(12.3),
        name="combine",
    )(expert_ids.T, combine.T, *back)

    arrived = pl.pallas_call(
        late_kernel,
        out_shape=shape(3, most, width),
        in_specs=[HBM] * 3,
        out_specs=HBM,
        input_output_aliases={0: 0},
        scratch_shapes=[pltpu.SemaphoreType.DMA((3,))],
        compiler_params=params(),
        name="late",
    )(early, straight, near)
    return mixed, arrived


def solution(mesh):
    placed = (
        P(("replica", "expert"), None),
        P(("replica", "expert"), None),
        P(("replica", "expert"), None),
        P("expert", None),
        P("expert", None),
        P("expert", None),
        P(),
    )
    return jax.shard_map(
        on_device,
        mesh=mesh,
        in_specs=placed,
        out_specs=(P(("replica", "expert"), None), P("replica", "expert", None)),
        check_vma=False,
    )
```

```python
import functools

import jax
import jax.numpy as jnp
from jax import lax
from jax.experimental import pallas as pl
from jax.experimental.pallas import tpu as pltpu
from jax.sharding import PartitionSpec as P

CAP = 12
PACK = 2 * CAP
STRIDE = 32
GROUP = 4
BF16 = jnp.bfloat16
F32 = jnp.float32
VMEM = pl.BlockSpec(memory_space=pltpu.VMEM)
HBM = pl.BlockSpec(memory_space=pltpu.HBM)


def params(megabytes=16):
    return pltpu.CompilerParams(vmem_limit_bytes=megabytes * 1024 * 1024)


def cost(microseconds):
    return pl.CostEstimate(
        flops=int(microseconds * 10**9), bytes_accessed=10**4, transcendentals=0
    )


def token_places(ids, group, experts):
    tok = ids.shape[1]
    member = []
    for j in range(experts):
        named = jnp.where(ids == lax.rem(group + j, experts), 1.0, 0.0)
        member.append(jnp.sum(named, axis=0, keepdims=True))
    member = jnp.concatenate(member, axis=0)
    row = lax.broadcasted_iota(jnp.int32, (tok, tok), 0)
    col = lax.broadcasted_iota(jnp.int32, (tok, tok), 1)
    upto = jnp.where(row <= col, 1.0, 0.0).astype(BF16)
    rank = jnp.dot(member.astype(BF16), upto, preferred_element_type=F32)
    return jnp.where(member > 0, rank - 1.0, -PACK).astype(jnp.int32)


def dispatch_kernel(experts, ids_ref, tok_ref, begun_ref, *out_refs):
    group = lax.axis_index("expert") // GROUP
    place = token_places(ids_ref[...], group, experts)
    tok, half = tok_ref.shape[0], tok_ref.shape[1] // 2
    slot = lax.broadcasted_iota(jnp.int32, (PACK, tok), 0)
    for j, ref in enumerate(out_refs):
        spot = place[j : j + 1, :]
        left = jnp.where(jnp.logical_and(slot == spot, spot >= 0), 1.0, 0.0).astype(BF16)
        right = jnp.where(slot == spot + CAP, 1.0, 0.0).astype(BF16)
        rows = jnp.dot(left, tok_ref[:, :half], preferred_element_type=F32)
        rows = rows + jnp.dot(right, tok_ref[:, half:], preferred_element_type=F32)
        ref[...] = rows.astype(BF16)


def select_kernel(wanted, plan_ref, gate_ref, up_ref, down_ref, *out_refs):
    device = lax.axis_index("expert")
    even = lax.axis_index("replica") % 2 == 0
    rows = gate_ref.shape[0]

    @pl.when(device % GROUP == GROUP - 1)
    def _():
        plans = []
        for survivor, count, first in wanted:
            plan = plan_ref[survivor, pl.ds(device // GROUP, 1), :]
            if first is None:
                plan = jnp.where(even, plan[:, :count], plan[:, count : 2 * count])
            else:
                plan = plan[:, first : first + count]
            plans.append(plan)
        total = sum(count for _, count, _ in wanted)
        number = lax.broadcasted_iota(jnp.int32, (rows, total), 0)
        pick = jnp.where(number == jnp.concatenate(plans, axis=1), 1.0, 0.0).astype(BF16)
        for m, held_ref in enumerate((gate_ref, up_ref, down_ref)):
            found = lax.dot_general(
                pick, held_ref[...], (((0,), (0,)), ((), ())), preferred_element_type=F32
            ).astype(BF16)
            start = 0
            for (_, count, _), ref in zip(wanted, out_refs):
                ref[m] = found[start : start + count]
                start += count


def place_rows(pieces, out_ref, sems):
    copies = []
    for ref, first in pieces:
        for m in range(3):
            rows = pl.ds(first, ref.shape[1])
            copies.append(
                pltpu.make_async_copy(ref.at[m], out_ref.at[m, rows], sems.at[len(copies)])
            )
    for copy in copies:
        copy.start()
    for copy in copies:
        copy.wait()


def early_kernel(shared_ref, swapped_ref, out_ref, sems):
    position = lax.axis_index("expert") % GROUP
    parity = lax.axis_index("replica") % 2
    half = shared_ref.shape[1]
    for even in range(2):

        @pl.when(jnp.logical_and(position == 1, parity == even))
        def _():
            place_rows([(shared_ref, half * even), (swapped_ref, half * (1 - even))], out_ref, sems)


def late_kernel(early_ref, straight_ref, near_ref, out_ref, sems):
    position = lax.axis_index("expert") % GROUP

    @pl.when(jnp.logical_or(position == 0, position == 3))
    def _():
        place_rows([(straight_ref, 0)], out_ref, sems)

    @pl.when(position == 2)
    def _():
        place_rows([(near_ref, 0)], out_ref, sems)


def begin_kernel(out_ref):
    out_ref[...] = jnp.zeros_like(out_ref)


def expert_kernel(mine_ref, other_ref, gate_ref, up_ref, down_ref, keep_ref, give_ref):
    rows, half = mine_ref.shape
    x = jnp.concatenate([mine_ref[...], other_ref[...]], axis=0)
    total = x.shape[0]
    numbers = (((1,), (1,)), ((), ()))

    def project(ref):
        left = lax.dot_general(x, ref[:, :half], numbers, preferred_element_type=F32)
        right = lax.dot_general(x, ref[:, half:], numbers, preferred_element_type=F32)
        return left + jnp.concatenate([right[CAP:], right[:CAP]], axis=0)

    gate_value = project(gate_ref)
    up_value = project(up_ref)
    hidden = (gate_value / (1.0 + jnp.exp(-gate_value)) * up_value).astype(BF16)
    left = jnp.dot(hidden, down_ref[:, :half], preferred_element_type=F32)
    right = jnp.dot(hidden, down_ref[:, half:], preferred_element_type=F32)
    right = jnp.concatenate([right[total - CAP :], right[: total - CAP]], axis=0)
    row = lax.broadcasted_iota(jnp.int32, (total, half), 0)
    partial = jnp.where(row % PACK < CAP, left, right)
    keep_ref[...] = partial[:rows]
    give_ref[...] = partial[rows:].astype(BF16)


def combine_kernel(experts, ids_ref, weight_ref, *refs):
    piece_refs, (out_ref, rows_ref) = refs[:-2], refs[-2:]
    ids = ids_ref[...]
    group = lax.axis_index("expert") // GROUP
    half = out_ref.shape[1] // 2
    each = len(piece_refs) // experts
    place = token_places(ids, group, experts)
    slot = lax.broadcasted_iota(jnp.int32, (STRIDE, ids.shape[1]), 0)
    numbers = (((0,), (0,)), ((), ()))
    rows_ref[...] = jnp.zeros_like(rows_ref)
    for n, ref in enumerate(piece_refs):
        rows_ref[n * STRIDE : n * STRIDE + PACK, :] = ref[...]
    scaled = [[], []]
    for j in range(experts):
        named = ids == lax.rem(group + j, experts)
        weight = jnp.sum(jnp.where(named, weight_ref[...], 0.0), axis=0, keepdims=True)
        for side in range(2):
            chosen = jnp.where(slot == place[j : j + 1, :] + side * CAP, weight, 0.0)
            scaled[side] += [chosen] * each
    for side in range(2):
        chosen = jnp.concatenate(scaled[side], axis=0)
        high = chosen.astype(BF16)
        low = (chosen - high.astype(F32)).astype(BF16)
        mixed = lax.dot_general(high, rows_ref[...], numbers, preferred_element_type=F32)
        mixed = mixed + lax.dot_general(low, rows_ref[...], numbers, preferred_element_type=F32)
        out_ref[:, side * half : (side + 1) * half] = mixed.astype(BF16)


def on_device(tokens, expert_ids, combine, old_gate, old_up, old_down, move_plan):
    devices = lax.axis_size("expert")
    replicas = lax.axis_size("replica")
    experts = move_plan.shape[0]
    most = move_plan.shape[2]
    width = tokens.shape[1]
    plan = jnp.transpose(move_plan, (1, 0, 2))
    weights = (old_gate, old_up, old_down)
    half = most // 2

    def shape(*dims, dtype=BF16):
        return jax.ShapeDtypeStruct(dims, dtype)

    def send(block, j, k):
        route = []
        for i in range(devices):
            g, p = i // GROUP, i % GROUP
            route.append((i, GROUP * ((g + j) % experts) + (p ^ k)))
        return lax.ppermute(block, "expert", route)

    def migrate(block, survivor):
        route = [(GROUP * e + GROUP - 1, GROUP * e + survivor) for e in range(experts)]
        return lax.ppermute(block, "expert", route)

    def swap(block, survivor):
        route = []
        for r in range(replicas):
            for e in range(experts):
                i = GROUP * e + survivor
                route.append((i * replicas + r, i * replicas + (r ^ 1)))
        return lax.ppermute(block, ("expert", "replica"), route)

    def select(wanted, held):
        return pl.pallas_call(
            functools.partial(select_kernel, wanted),
            out_shape=[shape(3, count, width) for _, count, _ in wanted],
            in_specs=[VMEM] * 4,
            out_specs=[VMEM] * len(wanted),
            compiler_params=params(),
            cost_estimate=cost(2),
            name="select",
        )(plan, *held)

    begun = pl.pallas_call(
        begin_kernel,
        out_shape=shape(8, 128, dtype=F32),
        out_specs=VMEM,
        cost_estimate=cost(5),
        name="begin",
    )()
    parcels = pl.pallas_call(
        functools.partial(dispatch_kernel, experts),
        out_shape=[shape(PACK, width // 2)] * experts,
        in_specs=[VMEM, VMEM, HBM],
        out_specs=[VMEM] * experts,
        compiler_params=params(),
        cost_estimate=cost(2),
        name="dispatch",
    )(expert_ids.T, tokens, begun)

    pairs = [(j, k) for j in range(experts) for k in (0, 2)]
    mine = [parcels[0]] + [send(parcels[j], j, k) for j, k in pairs[1:]]
    held, _ = lax.optimization_barrier((weights, parcels))
    wanted = [(1, half, None), (0, most, 0), (2, most, 0)]
    chosen = select(wanted, held)
    shared = migrate(chosen[0], 1)
    straight = migrate(chosen[1], 0)
    mine = jnp.concatenate(mine, axis=0)
    other = send(mine, 0, 1)

    total = mine.shape[0]
    step = min(total, 4 * PACK)
    row_spec = pl.BlockSpec((step, width // 2), lambda i: (i, 0))
    whole_spec = pl.BlockSpec(old_gate.shape, lambda i: (0, 0))
    keep, give = pl.pallas_call(
        expert_kernel,
        grid=(total // step,),
        out_shape=[shape(total, width // 2, dtype=F32), shape(total, width // 2)],
        in_specs=[row_spec] * 2 + [whole_spec] * 3,
        out_specs=[row_spec] * 2,
        compiler_params=params(),
        cost_estimate=cost(0),
        name="expert",
    )(mine, other, *weights)
    taken, shared = lax.optimization_barrier((send(give, 0, 1), shared))
    summed = (keep + taken.astype(F32)).astype(BF16)
    pieces = [summed[n * PACK : (n + 1) * PACK] for n in range(len(pairs))]
    back = [pieces[0]] + [
        send(block, -j, k) for (j, k), block in zip(pairs[1:], pieces[1:])
    ]
    swapped = swap(shared, 1)
    swapped, near = lax.optimization_barrier((swapped, chosen[2]))
    near = migrate(near, 2)

    early = pl.pallas_call(
        early_kernel,
        out_shape=shape(3, most, width),
        in_specs=[HBM] * 2,
        out_specs=HBM,
        scratch_shapes=[pltpu.SemaphoreType.DMA((6,))],
        compiler_params=params(),
        name="early",
    )(shared, swapped)
    back, early, straight = lax.optimization_barrier((back, early, straight))

    mixed = pl.pallas_call(
        functools.partial(combine_kernel, experts),
        out_shape=shape(tokens.shape[0], width),
        in_specs=[VMEM, VMEM] + [VMEM] * len(back),
        out_specs=VMEM,
        scratch_shapes=[pltpu.VMEM((len(back) * STRIDE, width // 2), BF16)],
        compiler_params=params(14 + experts),
        cost_estimate=cost(12.3),
        name="combine",
    )(expert_ids.T, combine.T, *back)

    arrived = pl.pallas_call(
        late_kernel,
        out_shape=shape(3, most, width),
        in_specs=[HBM] * 3,
        out_specs=HBM,
        input_output_aliases={0: 0},
        scratch_shapes=[pltpu.SemaphoreType.DMA((3,))],
        compiler_params=params(),
        name="late",
    )(early, straight, near)
    return mixed, arrived


def solution(mesh):
    placed = (
        P(("replica", "expert"), None),
        P(("replica", "expert"), None),
        P(("replica", "expert"), None),
        P("expert", None),
        P("expert", None),
        P("expert", None),
        P(),
    )
    return jax.shard_map(
        on_device,
        mesh=mesh,
        in_specs=placed,
        out_specs=(P(("replica", "expert"), None), P("replica", "expert", None)),
        check_vma=False,
    )
```

```python
import functools

import jax
import jax.numpy as jnp
from jax import lax
from jax.experimental import pallas as pl
from jax.experimental.pallas import tpu as pltpu
from jax.sharding import PartitionSpec as P

CAP = 12
PACK = 2 * CAP
STRIDE = 32
GROUP = 4
BF16 = jnp.bfloat16
F32 = jnp.float32
VMEM = pl.BlockSpec(memory_space=pltpu.VMEM)
HBM = pl.BlockSpec(memory_space=pltpu.HBM)


def params(megabytes=16):
    return pltpu.CompilerParams(vmem_limit_bytes=megabytes * 1024 * 1024)


def cost(microseconds):
    return pl.CostEstimate(
        flops=microseconds * 10**9, bytes_accessed=10**4, transcendentals=0
    )


def token_places(ids, group, experts):
    tok = ids.shape[1]
    member = []
    for j in range(experts):
        named = jnp.where(ids == lax.rem(group + j, experts), 1.0, 0.0)
        member.append(jnp.sum(named, axis=0, keepdims=True))
    member = jnp.concatenate(member, axis=0)
    row = lax.broadcasted_iota(jnp.int32, (tok, tok), 0)
    col = lax.broadcasted_iota(jnp.int32, (tok, tok), 1)
    upto = jnp.where(row <= col, 1.0, 0.0).astype(BF16)
    rank = jnp.dot(member.astype(BF16), upto, preferred_element_type=F32)
    return jnp.where(member > 0, rank - 1.0, -PACK).astype(jnp.int32)


def dispatch_kernel(experts, ids_ref, tok_ref, begun_ref, *out_refs):
    group = lax.axis_index("expert") // GROUP
    place = token_places(ids_ref[...], group, experts)
    tok, half = tok_ref.shape[0], tok_ref.shape[1] // 2
    slot = lax.broadcasted_iota(jnp.int32, (PACK, tok), 0)
    for j, ref in enumerate(out_refs):
        spot = place[j : j + 1, :]
        left = jnp.where(jnp.logical_and(slot == spot, spot >= 0), 1.0, 0.0).astype(BF16)
        right = jnp.where(slot == spot + CAP, 1.0, 0.0).astype(BF16)
        rows = jnp.dot(left, tok_ref[:, :half], preferred_element_type=F32)
        rows = rows + jnp.dot(right, tok_ref[:, half:], preferred_element_type=F32)
        ref[...] = rows.astype(BF16)


def select_kernel(wanted, plan_ref, gate_ref, up_ref, down_ref, *out_refs):
    device = lax.axis_index("expert")
    even = lax.axis_index("replica") % 2 == 0
    rows = gate_ref.shape[0]

    @pl.when(device % GROUP == GROUP - 1)
    def _():
        plans = []
        for survivor, count, first in wanted:
            plan = plan_ref[survivor, pl.ds(device // GROUP, 1), :]
            if first is None:
                plan = jnp.where(even, plan[:, :count], plan[:, count : 2 * count])
            else:
                plan = plan[:, first : first + count]
            plans.append(plan)
        total = sum(count for _, count, _ in wanted)
        number = lax.broadcasted_iota(jnp.int32, (rows, total), 0)
        pick = jnp.where(number == jnp.concatenate(plans, axis=1), 1.0, 0.0).astype(BF16)
        for m, held_ref in enumerate((gate_ref, up_ref, down_ref)):
            found = lax.dot_general(
                pick, held_ref[...], (((0,), (0,)), ((), ())), preferred_element_type=F32
            ).astype(BF16)
            start = 0
            for (_, count, _), ref in zip(wanted, out_refs):
                ref[m] = found[start : start + count]
                start += count


def place_rows(pieces, out_ref, sems):
    copies = []
    for ref, first in pieces:
        for m in range(3):
            rows = pl.ds(first, ref.shape[1])
            copies.append(
                pltpu.make_async_copy(ref.at[m], out_ref.at[m, rows], sems.at[len(copies)])
            )
    for copy in copies:
        copy.start()
    for copy in copies:
        copy.wait()


def early_kernel(shared_ref, swapped_ref, first_ref, near_ref, out_ref, sems):
    position = lax.axis_index("expert") % GROUP
    parity = lax.axis_index("replica") % 2
    half = shared_ref.shape[1]
    for even in range(2):

        @pl.when(jnp.logical_and(position == 1, parity == even))
        def _():
            place_rows([(shared_ref, half * even), (swapped_ref, half * (1 - even))], out_ref, sems)

    @pl.when(jnp.logical_or(position == 0, position == 3))
    def _():
        place_rows([(first_ref, 0)], out_ref, sems)

    @pl.when(position == 2)
    def _():
        place_rows([(near_ref, 0)], out_ref, sems)


def late_kernel(early_ref, second_ref, out_ref, sems):
    position = lax.axis_index("expert") % GROUP

    @pl.when(jnp.logical_or(position == 0, position == 3))
    def _():
        place_rows([(second_ref, out_ref.shape[1] - second_ref.shape[1])], out_ref, sems)


def begin_kernel(out_ref):
    out_ref[...] = jnp.zeros_like(out_ref)


def expert_kernel(mine_ref, other_ref, gate_ref, up_ref, down_ref, keep_ref, give_ref):
    rows, half = mine_ref.shape
    x = jnp.concatenate([mine_ref[...], other_ref[...]], axis=0)
    total = x.shape[0]
    numbers = (((1,), (1,)), ((), ()))

    def project(ref):
        left = lax.dot_general(x, ref[:, :half], numbers, preferred_element_type=F32)
        right = lax.dot_general(x, ref[:, half:], numbers, preferred_element_type=F32)
        return left + jnp.concatenate([right[CAP:], right[:CAP]], axis=0)

    gate_value = project(gate_ref)
    up_value = project(up_ref)
    hidden = (gate_value / (1.0 + jnp.exp(-gate_value)) * up_value).astype(BF16)
    left = jnp.dot(hidden, down_ref[:, :half], preferred_element_type=F32)
    right = jnp.dot(hidden, down_ref[:, half:], preferred_element_type=F32)
    right = jnp.concatenate([right[total - CAP :], right[: total - CAP]], axis=0)
    row = lax.broadcasted_iota(jnp.int32, (total, half), 0)
    partial = jnp.where(row % PACK < CAP, left, right)
    keep_ref[...] = partial[:rows]
    give_ref[...] = partial[rows:].astype(BF16)


def combine_kernel(experts, ids_ref, weight_ref, *refs):
    piece_refs, (out_ref, rows_ref) = refs[:-2], refs[-2:]
    ids = ids_ref[...]
    group = lax.axis_index("expert") // GROUP
    half = out_ref.shape[1] // 2
    each = len(piece_refs) // experts
    place = token_places(ids, group, experts)
    slot = lax.broadcasted_iota(jnp.int32, (STRIDE, ids.shape[1]), 0)
    numbers = (((0,), (0,)), ((), ()))
    rows_ref[...] = jnp.zeros_like(rows_ref)
    for n, ref in enumerate(piece_refs):
        rows_ref[n * STRIDE : n * STRIDE + PACK, :] = ref[...]
    scaled = [[], []]
    for j in range(experts):
        named = ids == lax.rem(group + j, experts)
        weight = jnp.sum(jnp.where(named, weight_ref[...], 0.0), axis=0, keepdims=True)
        for side in range(2):
            chosen = jnp.where(slot == place[j : j + 1, :] + side * CAP, weight, 0.0)
            scaled[side] += [chosen] * each
    for side in range(2):
        chosen = jnp.concatenate(scaled[side], axis=0)
        high = chosen.astype(BF16)
        low = (chosen - high.astype(F32)).astype(BF16)
        mixed = lax.dot_general(high, rows_ref[...], numbers, preferred_element_type=F32)
        mixed = mixed + lax.dot_general(low, rows_ref[...], numbers, preferred_element_type=F32)
        out_ref[:, side * half : (side + 1) * half] = mixed.astype(BF16)


def on_device(tokens, expert_ids, combine, old_gate, old_up, old_down, move_plan):
    devices = lax.axis_size("expert")
    replicas = lax.axis_size("replica")
    experts = move_plan.shape[0]
    most = move_plan.shape[2]
    width = tokens.shape[1]
    plan = jnp.transpose(move_plan, (1, 0, 2))
    weights = (old_gate, old_up, old_down)
    half = most // 2
    lead = most // 3 * 2

    def shape(*dims, dtype=BF16):
        return jax.ShapeDtypeStruct(dims, dtype)

    def send(block, j, k):
        route = []
        for i in range(devices):
            g, p = i // GROUP, i % GROUP
            route.append((i, GROUP * ((g + j) % experts) + (p ^ k)))
        return lax.ppermute(block, "expert", route)

    def migrate(block, survivor):
        route = [(GROUP * e + GROUP - 1, GROUP * e + survivor) for e in range(experts)]
        return lax.ppermute(block, "expert", route)

    def swap(block, survivor):
        route = []
        for r in range(replicas):
            for e in range(experts):
                i = GROUP * e + survivor
                route.append((i * replicas + r, i * replicas + (r ^ 1)))
        return lax.ppermute(block, ("expert", "replica"), route)

    def select(wanted, held):
        return pl.pallas_call(
            functools.partial(select_kernel, wanted),
            out_shape=[shape(3, count, width) for _, count, _ in wanted],
            in_specs=[VMEM] * 4,
            out_specs=[VMEM] * len(wanted),
            compiler_params=params(),
            cost_estimate=cost(2),
            name="select",
        )(plan, *held)

    begun = pl.pallas_call(
        begin_kernel,
        out_shape=shape(8, 128, dtype=F32),
        out_specs=VMEM,
        cost_estimate=cost(5),
        name="begin",
    )()
    parcels = pl.pallas_call(
        functools.partial(dispatch_kernel, experts),
        out_shape=[shape(PACK, width // 2)] * experts,
        in_specs=[VMEM, VMEM, HBM],
        out_specs=[VMEM] * experts,
        compiler_params=params(),
        cost_estimate=cost(2),
        name="dispatch",
    )(expert_ids.T, tokens, begun)

    pairs = [(j, k) for j in range(experts) for k in (0, 2)]
    mine = [parcels[0]] + [send(parcels[j], j, k) for j, k in pairs[1:]]
    held, _ = lax.optimization_barrier((weights, parcels))
    wanted = [(1, half, None), (0, lead, 0), (0, most - lead, lead), (2, most, 0)]
    chosen = select(wanted, held)
    shared = migrate(chosen[0], 1)
    first = migrate(chosen[1], 0)
    near = migrate(chosen[3], 2)
    mine = jnp.concatenate(mine, axis=0)
    other = send(mine, 0, 1)

    total = mine.shape[0]
    step = min(total, 4 * PACK)
    row_spec = pl.BlockSpec((step, width // 2), lambda i: (i, 0))
    whole_spec = pl.BlockSpec(old_gate.shape, lambda i: (0, 0))
    keep, give = pl.pallas_call(
        expert_kernel,
        grid=(total // step,),
        out_shape=[shape(total, width // 2, dtype=F32), shape(total, width // 2)],
        in_specs=[row_spec] * 2 + [whole_spec] * 3,
        out_specs=[row_spec] * 2,
        compiler_params=params(),
        cost_estimate=cost(0),
        name="expert",
    )(mine, other, *weights)
    taken, shared = lax.optimization_barrier((send(give, 0, 1), shared))
    summed = (keep + taken.astype(F32)).astype(BF16)
    pieces = [summed[n * PACK : (n + 1) * PACK] for n in range(len(pairs))]
    back = [pieces[0]] + [
        send(block, -j, k) for (j, k), block in zip(pairs[1:], pieces[1:])
    ]
    swapped = swap(shared, 1)
    beside = len(pairs) // 2
    back[beside], near = lax.optimization_barrier((back[beside], near))
    last, _ = lax.optimization_barrier((chosen[2], summed))
    second = migrate(last, 0)

    early = pl.pallas_call(
        early_kernel,
        out_shape=shape(3, most, width),
        in_specs=[HBM] * 4,
        out_specs=HBM,
        scratch_shapes=[pltpu.SemaphoreType.DMA((6,))],
        compiler_params=params(),
        name="early",
    )(shared, swapped, first, near)
    back, early = lax.optimization_barrier((back, early))

    mixed = pl.pallas_call(
        functools.partial(combine_kernel, experts),
        out_shape=shape(tokens.shape[0], width),
        in_specs=[VMEM, VMEM] + [VMEM] * len(back),
        out_specs=VMEM,
        scratch_shapes=[pltpu.VMEM((len(back) * STRIDE, width // 2), BF16)],
        compiler_params=params(14 + experts),
        cost_estimate=cost(5),
        name="combine",
    )(expert_ids.T, combine.T, *back)

    arrived = pl.pallas_call(
        late_kernel,
        out_shape=shape(3, most, width),
        in_specs=[HBM] * 2,
        out_specs=HBM,
        input_output_aliases={0: 0},
        scratch_shapes=[pltpu.SemaphoreType.DMA((3,))],
        compiler_params=params(),
        name="late",
    )(early, second)
    return mixed, arrived


def solution(mesh):
    placed = (
        P(("replica", "expert"), None),
        P(("replica", "expert"), None),
        P(("replica", "expert"), None),
        P("expert", None),
        P("expert", None),
        P("expert", None),
        P(),
    )
    return jax.shard_map(
        on_device,
        mesh=mesh,
        in_specs=placed,
        out_specs=(P(("replica", "expert"), None), P("replica", "expert", None)),
        check_vma=False,
    )
```

```python
import functools

import jax
import jax.numpy as jnp
from jax import lax
from jax.experimental import pallas as pl
from jax.experimental.pallas import tpu as pltpu
from jax.sharding import PartitionSpec as P

CAP = 12
PACK = 2 * CAP
STRIDE = 32
GROUP = 4
BF16 = jnp.bfloat16
F32 = jnp.float32
VMEM = pl.BlockSpec(memory_space=pltpu.VMEM)
HBM = pl.BlockSpec(memory_space=pltpu.HBM)


def params(megabytes=16):
    return pltpu.CompilerParams(vmem_limit_bytes=megabytes * 1024 * 1024)


def cost(microseconds):
    return pl.CostEstimate(
        flops=microseconds * 10**9, bytes_accessed=10**4, transcendentals=0
    )


def token_places(ids, group, experts):
    tok = ids.shape[1]
    member = []
    for j in range(experts):
        named = jnp.where(ids == lax.rem(group + j, experts), 1.0, 0.0)
        member.append(jnp.sum(named, axis=0, keepdims=True))
    member = jnp.concatenate(member, axis=0)
    row = lax.broadcasted_iota(jnp.int32, (tok, tok), 0)
    col = lax.broadcasted_iota(jnp.int32, (tok, tok), 1)
    upto = jnp.where(row <= col, 1.0, 0.0).astype(BF16)
    rank = jnp.dot(member.astype(BF16), upto, preferred_element_type=F32)
    return jnp.where(member > 0, rank - 1.0, -PACK).astype(jnp.int32)


def dispatch_kernel(experts, ids_ref, tok_ref, begun_ref, *out_refs):
    group = lax.axis_index("expert") // GROUP
    place = token_places(ids_ref[...], group, experts)
    tok, half = tok_ref.shape[0], tok_ref.shape[1] // 2
    slot = lax.broadcasted_iota(jnp.int32, (PACK, tok), 0)
    for j, ref in enumerate(out_refs):
        spot = place[j : j + 1, :]
        left = jnp.where(jnp.logical_and(slot == spot, spot >= 0), 1.0, 0.0).astype(BF16)
        right = jnp.where(slot == spot + CAP, 1.0, 0.0).astype(BF16)
        rows = jnp.dot(left, tok_ref[:, :half], preferred_element_type=F32)
        rows = rows + jnp.dot(right, tok_ref[:, half:], preferred_element_type=F32)
        ref[...] = rows.astype(BF16)


def select_kernel(wanted, plan_ref, gate_ref, up_ref, down_ref, *out_refs):
    device = lax.axis_index("expert")
    even = lax.axis_index("replica") % 2 == 0
    rows = gate_ref.shape[0]

    @pl.when(device % GROUP == GROUP - 1)
    def _():
        plans = []
        for survivor, count, first in wanted:
            plan = plan_ref[survivor, pl.ds(device // GROUP, 1), :]
            if first is None:
                plan = jnp.where(even, plan[:, :count], plan[:, count : 2 * count])
            else:
                plan = plan[:, first : first + count]
            plans.append(plan)
        total = sum(count for _, count, _ in wanted)
        number = lax.broadcasted_iota(jnp.int32, (rows, total), 0)
        pick = jnp.where(number == jnp.concatenate(plans, axis=1), 1.0, 0.0).astype(BF16)
        for m, held_ref in enumerate((gate_ref, up_ref, down_ref)):
            found = lax.dot_general(
                pick, held_ref[...], (((0,), (0,)), ((), ())), preferred_element_type=F32
            ).astype(BF16)
            start = 0
            for (_, count, _), ref in zip(wanted, out_refs):
                ref[m] = found[start : start + count]
                start += count


def place_rows(pieces, out_ref, sems):
    copies = []
    for ref, first in pieces:
        for m in range(3):
            rows = pl.ds(first, ref.shape[1])
            copies.append(
                pltpu.make_async_copy(ref.at[m], out_ref.at[m, rows], sems.at[len(copies)])
            )
    for copy in copies:
        copy.start()
    for copy in copies:
        copy.wait()


def early_kernel(shared_ref, swapped_ref, first_ref, near_ref, out_ref, sems):
    position = lax.axis_index("expert") % GROUP
    parity = lax.axis_index("replica") % 2
    half = shared_ref.shape[1]
    for even in range(2):

        @pl.when(jnp.logical_and(position == 1, parity == even))
        def _():
            place_rows([(shared_ref, half * even), (swapped_ref, half * (1 - even))], out_ref, sems)

    @pl.when(jnp.logical_or(position == 0, position == 3))
    def _():
        place_rows([(first_ref, 0)], out_ref, sems)

    @pl.when(position == 2)
    def _():
        place_rows([(near_ref, 0)], out_ref, sems)


def late_kernel(early_ref, second_ref, out_ref, sems):
    position = lax.axis_index("expert") % GROUP

    @pl.when(jnp.logical_or(position == 0, position == 3))
    def _():
        place_rows([(second_ref, out_ref.shape[1] - second_ref.shape[1])], out_ref, sems)


def begin_kernel(out_ref):
    out_ref[...] = jnp.zeros_like(out_ref)


def expert_kernel(mine_ref, other_ref, gate_ref, up_ref, down_ref, keep_ref, give_ref):
    rows, half = mine_ref.shape
    x = jnp.concatenate([mine_ref[...], other_ref[...]], axis=0)
    total = x.shape[0]
    numbers = (((1,), (1,)), ((), ()))

    def project(ref):
        left = lax.dot_general(x, ref[:, :half], numbers, preferred_element_type=F32)
        right = lax.dot_general(x, ref[:, half:], numbers, preferred_element_type=F32)
        return left + jnp.concatenate([right[CAP:], right[:CAP]], axis=0)

    gate_value = project(gate_ref)
    up_value = project(up_ref)
    hidden = (gate_value / (1.0 + jnp.exp(-gate_value)) * up_value).astype(BF16)
    left = jnp.dot(hidden, down_ref[:, :half], preferred_element_type=F32)
    right = jnp.dot(hidden, down_ref[:, half:], preferred_element_type=F32)
    right = jnp.concatenate([right[total - CAP :], right[: total - CAP]], axis=0)
    row = lax.broadcasted_iota(jnp.int32, (total, half), 0)
    partial = jnp.where(row % PACK < CAP, left, right)
    keep_ref[...] = partial[:rows]
    give_ref[...] = partial[rows:].astype(BF16)


def combine_kernel(experts, ids_ref, weight_ref, *refs):
    piece_refs, (out_ref, rows_ref) = refs[:-2], refs[-2:]
    ids = ids_ref[...]
    group = lax.axis_index("expert") // GROUP
    half = out_ref.shape[1] // 2
    each = len(piece_refs) // experts
    place = token_places(ids, group, experts)
    slot = lax.broadcasted_iota(jnp.int32, (STRIDE, ids.shape[1]), 0)
    numbers = (((0,), (0,)), ((), ()))
    rows_ref[...] = jnp.zeros_like(rows_ref)
    for n, ref in enumerate(piece_refs):
        rows_ref[n * STRIDE : n * STRIDE + PACK, :] = ref[...]
    scaled = [[], []]
    for j in range(experts):
        named = ids == lax.rem(group + j, experts)
        weight = jnp.sum(jnp.where(named, weight_ref[...], 0.0), axis=0, keepdims=True)
        for side in range(2):
            chosen = jnp.where(slot == place[j : j + 1, :] + side * CAP, weight, 0.0)
            scaled[side] += [chosen] * each
    for side in range(2):
        chosen = jnp.concatenate(scaled[side], axis=0)
        high = chosen.astype(BF16)
        low = (chosen - high.astype(F32)).astype(BF16)
        mixed = lax.dot_general(high, rows_ref[...], numbers, preferred_element_type=F32)
        mixed = mixed + lax.dot_general(low, rows_ref[...], numbers, preferred_element_type=F32)
        out_ref[:, side * half : (side + 1) * half] = mixed.astype(BF16)


def on_device(tokens, expert_ids, combine, old_gate, old_up, old_down, move_plan):
    devices = lax.axis_size("expert")
    replicas = lax.axis_size("replica")
    experts = move_plan.shape[0]
    most = move_plan.shape[2]
    width = tokens.shape[1]
    plan = jnp.transpose(move_plan, (1, 0, 2))
    weights = (old_gate, old_up, old_down)
    half = most // 2
    lead = most // 6 * 5

    def shape(*dims, dtype=BF16):
        return jax.ShapeDtypeStruct(dims, dtype)

    def send(block, j, k):
        route = []
        for i in range(devices):
            g, p = i // GROUP, i % GROUP
            route.append((i, GROUP * ((g + j) % experts) + (p ^ k)))
        return lax.ppermute(block, "expert", route)

    def migrate(block, survivor):
        route = [(GROUP * e + GROUP - 1, GROUP * e + survivor) for e in range(experts)]
        return lax.ppermute(block, "expert", route)

    def swap(block, survivor):
        route = []
        for r in range(replicas):
            for e in range(experts):
                i = GROUP * e + survivor
                route.append((i * replicas + r, i * replicas + (r ^ 1)))
        return lax.ppermute(block, ("expert", "replica"), route)

    def select(wanted, held):
        return pl.pallas_call(
            functools.partial(select_kernel, wanted),
            out_shape=[shape(3, count, width) for _, count, _ in wanted],
            in_specs=[VMEM] * 4,
            out_specs=[VMEM] * len(wanted),
            compiler_params=params(),
            cost_estimate=cost(2),
            name="select",
        )(plan, *held)

    begun = pl.pallas_call(
        begin_kernel,
        out_shape=shape(8, 128, dtype=F32),
        out_specs=VMEM,
        cost_estimate=cost(5),
        name="begin",
    )()
    parcels = pl.pallas_call(
        functools.partial(dispatch_kernel, experts),
        out_shape=[shape(PACK, width // 2)] * experts,
        in_specs=[VMEM, VMEM, HBM],
        out_specs=[VMEM] * experts,
        compiler_params=params(),
        cost_estimate=cost(2),
        name="dispatch",
    )(expert_ids.T, tokens, begun)

    pairs = [(j, k) for j in range(experts) for k in (0, 2)]
    mine = [parcels[0]] + [send(parcels[j], j, k) for j, k in pairs[1:]]
    held, _ = lax.optimization_barrier((weights, parcels))
    wanted = [(1, half, None), (0, lead, 0), (0, most - lead, lead), (2, most, 0)]
    chosen = select(wanted, held)
    shared = migrate(chosen[0], 1)
    first = migrate(chosen[1], 0)
    near = migrate(chosen[3], 2)
    mine = jnp.concatenate(mine, axis=0)
    other = send(mine, 0, 1)

    total = mine.shape[0]
    step = min(total, 4 * PACK)
    row_spec = pl.BlockSpec((step, width // 2), lambda i: (i, 0))
    whole_spec = pl.BlockSpec(old_gate.shape, lambda i: (0, 0))
    keep, give = pl.pallas_call(
        expert_kernel,
        grid=(total // step,),
        out_shape=[shape(total, width // 2, dtype=F32), shape(total, width // 2)],
        in_specs=[row_spec] * 2 + [whole_spec] * 3,
        out_specs=[row_spec] * 2,
        compiler_params=params(),
        cost_estimate=cost(0),
        name="expert",
    )(mine, other, *weights)
    taken, shared = lax.optimization_barrier((send(give, 0, 1), shared))
    summed = (keep + taken.astype(F32)).astype(BF16)
    pieces = [summed[n * PACK : (n + 1) * PACK] for n in range(len(pairs))]
    back = [pieces[0]] + [
        send(block, -j, k) for (j, k), block in zip(pairs[1:], pieces[1:])
    ]
    swapped = swap(shared, 1)
    beside = len(pairs) // 2
    back[beside], near = lax.optimization_barrier((back[beside], near))
    last, _ = lax.optimization_barrier((chosen[2], summed))
    second = migrate(last, 0)

    early = pl.pallas_call(
        early_kernel,
        out_shape=shape(3, most, width),
        in_specs=[HBM] * 4,
        out_specs=HBM,
        scratch_shapes=[pltpu.SemaphoreType.DMA((6,))],
        compiler_params=params(),
        name="early",
    )(shared, swapped, first, near)
    back, early = lax.optimization_barrier((back, early))

    mixed = pl.pallas_call(
        functools.partial(combine_kernel, experts),
        out_shape=shape(tokens.shape[0], width),
        in_specs=[VMEM, VMEM] + [VMEM] * len(back),
        out_specs=VMEM,
        scratch_shapes=[pltpu.VMEM((len(back) * STRIDE, width // 2), BF16)],
        compiler_params=params(14 + experts),
        cost_estimate=cost(3),
        name="combine",
    )(expert_ids.T, combine.T, *back)

    arrived = pl.pallas_call(
        late_kernel,
        out_shape=shape(3, most, width),
        in_specs=[HBM] * 2,
        out_specs=HBM,
        input_output_aliases={0: 0},
        scratch_shapes=[pltpu.SemaphoreType.DMA((3,))],
        compiler_params=params(),
        name="late",
    )(early, second)
    return mixed, arrived


def solution(mesh):
    placed = (
        P(("replica", "expert"), None),
        P(("replica", "expert"), None),
        P(("replica", "expert"), None),
        P("expert", None),
        P("expert", None),
        P("expert", None),
        P(),
    )
    return jax.shard_map(
        on_device,
        mesh=mesh,
        in_specs=placed,
        out_specs=(P(("replica", "expert"), None), P("replica", "expert", None)),
        check_vma=False,
    )
```

```python
import functools

import jax
import jax.numpy as jnp
from jax import lax
from jax.experimental import pallas as pl
from jax.experimental.pallas import tpu as pltpu
from jax.sharding import PartitionSpec as P

CAP = 12
PACK = 2 * CAP
STRIDE = 32
GROUP = 4
BF16 = jnp.bfloat16
F32 = jnp.float32
VMEM = pl.BlockSpec(memory_space=pltpu.VMEM)
HBM = pl.BlockSpec(memory_space=pltpu.HBM)
ANY = pl.BlockSpec(memory_space=pl.ANY)


def params(megabytes=16):
    return pltpu.CompilerParams(vmem_limit_bytes=megabytes * 1024 * 1024)


def cost(microseconds):
    return pl.CostEstimate(
        flops=microseconds * 10**9, bytes_accessed=10**4, transcendentals=0
    )


def token_places(ids, group, experts):
    tok = ids.shape[1]
    member = []
    for j in range(experts):
        named = jnp.where(ids == lax.rem(group + j, experts), 1.0, 0.0)
        member.append(jnp.sum(named, axis=0, keepdims=True))
    member = jnp.concatenate(member, axis=0)
    row = lax.broadcasted_iota(jnp.int32, (tok, tok), 0)
    col = lax.broadcasted_iota(jnp.int32, (tok, tok), 1)
    upto = jnp.where(row <= col, 1.0, 0.0).astype(BF16)
    rank = jnp.dot(member.astype(BF16), upto, preferred_element_type=F32)
    return jnp.where(member > 0, rank - 1.0, -PACK).astype(jnp.int32)


def dispatch_kernel(experts, ids_ref, tok_ref, begun_hbm, *out_refs):
    group = lax.axis_index("expert") // GROUP
    place = token_places(ids_ref[...], group, experts)
    tok, half = tok_ref.shape[0], tok_ref.shape[1] // 2
    slot = lax.broadcasted_iota(jnp.int32, (PACK, tok), 0)
    for j, ref in enumerate(out_refs):
        spot = place[j : j + 1, :]
        left = jnp.where(jnp.logical_and(slot == spot, spot >= 0), 1.0, 0.0).astype(BF16)
        right = jnp.where(slot == spot + CAP, 1.0, 0.0).astype(BF16)
        rows = jnp.dot(left, tok_ref[:, :half], preferred_element_type=F32)
        rows = rows + jnp.dot(right, tok_ref[:, half:], preferred_element_type=F32)
        ref[...] = rows.astype(BF16)


def select_kernel(wanted, plan_ref, gate_ref, up_ref, down_ref, *out_refs):
    device = lax.axis_index("expert")
    even = lax.axis_index("replica") % 2 == 0
    rows = gate_ref.shape[0]

    @pl.when(device % GROUP == GROUP - 1)
    def _():
        plans = []
        for survivor, count, first in wanted:
            plan = plan_ref[survivor, pl.ds(device // GROUP, 1), :]
            if first is None:
                plan = jnp.where(even, plan[:, :count], plan[:, count : 2 * count])
            else:
                plan = plan[:, first : first + count]
            plans.append(plan)
        total = sum(count for _, count, _ in wanted)
        number = lax.broadcasted_iota(jnp.int32, (rows, total), 0)
        pick = jnp.where(number == jnp.concatenate(plans, axis=1), 1.0, 0.0).astype(BF16)
        for m, held_ref in enumerate((gate_ref, up_ref, down_ref)):
            found = lax.dot_general(
                pick, held_ref[...], (((0,), (0,)), ((), ())), preferred_element_type=F32
            ).astype(BF16)
            start = 0
            for (_, count, _), ref in zip(wanted, out_refs):
                ref[m] = found[start : start + count]
                start += count


def place_rows(pieces, out_ref, sems):
    copies = []
    for ref, first in pieces:
        for m in range(3):
            rows = pl.ds(first, ref.shape[1])
            copies.append(
                pltpu.make_async_copy(ref.at[m], out_ref.at[m, rows], sems.at[len(copies)])
            )
    for copy in copies:
        copy.start()
    for copy in copies:
        copy.wait()


def early_kernel(swapped_ref, near_ref, shared_ref, own_ref, out_ref, sems):
    position = lax.axis_index("expert") % GROUP
    parity = lax.axis_index("replica") % 2
    half, part = shared_ref.shape[1], own_ref.shape[1]
    for even in range(2):

        @pl.when(jnp.logical_and(position == 1, parity == even))
        def _():
            place_rows([(shared_ref, half * even), (swapped_ref, half * (1 - even))], out_ref, sems)

        @pl.when(jnp.logical_and(position % 3 == 0, parity == even))
        def _():
            place_rows([(own_ref, part * even)], out_ref, sems)

    @pl.when(position == 2)
    def _():
        place_rows([(near_ref, 0)], out_ref, sems)


def late_kernel(early_ref, straight_ref, swapped_ref, out_ref, sems):
    position = lax.axis_index("expert") % GROUP
    parity = lax.axis_index("replica") % 2
    part = swapped_ref.shape[1]
    for even in range(2):

        @pl.when(jnp.logical_and(position % 3 == 0, parity == even))
        def _():
            place_rows([(straight_ref, 2 * part), (swapped_ref, part * (1 - even))], out_ref, sems)


def begin_kernel(out_ref):
    out_ref[...] = jnp.zeros_like(out_ref)


def expert_kernel(mine_ref, other_ref, gate_ref, up_ref, down_ref, keep_ref, give_ref):
    rows, half = mine_ref.shape
    x = jnp.concatenate([mine_ref[...], other_ref[...]], axis=0)
    total = x.shape[0]
    numbers = (((1,), (1,)), ((), ()))

    def project(ref):
        left = lax.dot_general(x, ref[:, :half], numbers, preferred_element_type=F32)
        right = lax.dot_general(x, ref[:, half:], numbers, preferred_element_type=F32)
        return left + jnp.concatenate([right[CAP:], right[:CAP]], axis=0)

    gate_value = project(gate_ref)
    up_value = project(up_ref)
    hidden = (gate_value / (1.0 + jnp.exp(-gate_value)) * up_value).astype(BF16)
    left = jnp.dot(hidden, down_ref[:, :half], preferred_element_type=F32)
    right = jnp.dot(hidden, down_ref[:, half:], preferred_element_type=F32)
    right = jnp.concatenate([right[total - CAP :], right[: total - CAP]], axis=0)
    row = lax.broadcasted_iota(jnp.int32, (total, half), 0)
    partial = jnp.where(row % PACK < CAP, left, right)
    keep_ref[...] = partial[:rows]
    give_ref[...] = partial[rows:].astype(BF16)


def combine_kernel(experts, ids_ref, weight_ref, *refs):
    piece_refs, (out_ref, rows_ref) = refs[:-2], refs[-2:]
    ids = ids_ref[...]
    group = lax.axis_index("expert") // GROUP
    half = out_ref.shape[1] // 2
    each = len(piece_refs) // experts
    place = token_places(ids, group, experts)
    slot = lax.broadcasted_iota(jnp.int32, (STRIDE, ids.shape[1]), 0)
    numbers = (((0,), (0,)), ((), ()))
    rows_ref[...] = jnp.zeros_like(rows_ref)
    for n, ref in enumerate(piece_refs):
        rows_ref[n * STRIDE : n * STRIDE + PACK, :] = ref[...]
    scaled = [[], []]
    for j in range(experts):
        named = ids == lax.rem(group + j, experts)
        weight = jnp.sum(jnp.where(named, weight_ref[...], 0.0), axis=0, keepdims=True)
        for side in range(2):
            chosen = jnp.where(slot == place[j : j + 1, :] + side * CAP, weight, 0.0)
            scaled[side] += [chosen] * each
    for side in range(2):
        chosen = jnp.concatenate(scaled[side], axis=0)
        high = chosen.astype(BF16)
        low = (chosen - high.astype(F32)).astype(BF16)
        mixed = lax.dot_general(high, rows_ref[...], numbers, preferred_element_type=F32)
        mixed = mixed + lax.dot_general(low, rows_ref[...], numbers, preferred_element_type=F32)
        out_ref[:, side * half : (side + 1) * half] = mixed.astype(BF16)


def on_device(tokens, expert_ids, combine, old_gate, old_up, old_down, move_plan):
    devices = lax.axis_size("expert")
    replicas = lax.axis_size("replica")
    experts = move_plan.shape[0]
    most = move_plan.shape[2]
    width = tokens.shape[1]
    plan = jnp.transpose(move_plan, (1, 0, 2))
    weights = (old_gate, old_up, old_down)
    half = most // 2
    part = most // 6

    def shape(*dims, dtype=BF16):
        return jax.ShapeDtypeStruct(dims, dtype)

    def send(block, j, k):
        route = []
        for i in range(devices):
            g, p = i // GROUP, i % GROUP
            route.append((i, GROUP * ((g + j) % experts) + (p ^ k)))
        return lax.ppermute(block, "expert", route)

    def migrate(block, survivor):
        route = [(GROUP * e + GROUP - 1, GROUP * e + survivor) for e in range(experts)]
        return lax.ppermute(block, "expert", route)

    def swap(block, survivor):
        route = []
        for r in range(replicas):
            for e in range(experts):
                i = GROUP * e + survivor
                route.append((i * replicas + r, i * replicas + (r ^ 1)))
        return lax.ppermute(block, ("expert", "replica"), route)

    def select(wanted, held):
        return pl.pallas_call(
            functools.partial(select_kernel, wanted),
            out_shape=[shape(3, count, width) for _, count, _ in wanted],
            in_specs=[VMEM] * 4,
            out_specs=[VMEM] * len(wanted),
            compiler_params=params(),
            cost_estimate=cost(2),
            name="select",
        )(plan, *held)

    begun = pl.pallas_call(
        begin_kernel,
        out_shape=shape(8, 128, dtype=F32),
        out_specs=VMEM,
        cost_estimate=cost(5),
        name="begin",
    )()
    parcels = pl.pallas_call(
        functools.partial(dispatch_kernel, experts),
        out_shape=[shape(PACK, width // 2)] * experts,
        in_specs=[VMEM, VMEM, ANY],
        out_specs=[VMEM] * experts,
        compiler_params=params(),
        cost_estimate=cost(2),
        name="dispatch",
    )(expert_ids.T, tokens, begun)

    pairs = [(j, k) for j in range(experts) for k in (0, 2)]
    mine = [parcels[0]] + [send(parcels[j], j, k) for j, k in pairs[1:]]
    held, _ = lax.optimization_barrier((weights, parcels))
    wanted = [(0, part, None), (1, half, None), (0, most - 2 * part, 2 * part), (2, most, 0)]
    chosen = select(wanted, held)
    shared = [migrate(chosen[p], p) for p in range(2)]
    straight = migrate(chosen[2], 0)
    near = migrate(chosen[3], 2)
    mine = jnp.concatenate(mine, axis=0)
    other = send(mine, 0, 1)

    total = mine.shape[0]
    step = min(total, 4 * PACK)
    row_spec = pl.BlockSpec((step, width // 2), lambda i: (i, 0))
    whole_spec = pl.BlockSpec(old_gate.shape, lambda i: (0, 0))
    keep, give = pl.pallas_call(
        expert_kernel,
        grid=(total // step,),
        out_shape=[shape(total, width // 2, dtype=F32), shape(total, width // 2)],
        in_specs=[row_spec] * 2 + [whole_spec] * 3,
        out_specs=[row_spec] * 2,
        compiler_params=params(),
        cost_estimate=cost(0),
        name="expert",
    )(mine, other, *weights)
    taken, shared = lax.optimization_barrier((send(give, 0, 1), shared))
    summed = (keep + taken.astype(F32)).astype(BF16)
    pieces = [summed[n * PACK : (n + 1) * PACK] for n in range(len(pairs))]
    back = [pieces[0]] + [
        send(block, -j, k) for (j, k), block in zip(pairs[1:], pieces[1:])
    ]
    swapped = [swap(shared[p], p) for p in range(2)]
    beside = len(pairs) // 2
    back[beside], near = lax.optimization_barrier((back[beside], near))

    early = pl.pallas_call(
        early_kernel,
        out_shape=shape(3, most, width),
        in_specs=[HBM] * 4,
        out_specs=HBM,
        scratch_shapes=[pltpu.SemaphoreType.DMA((6,))],
        compiler_params=params(),
        name="early",
    )(swapped[1], near, shared[1], shared[0])
    back, early, straight = lax.optimization_barrier((back, early, straight))

    mixed = pl.pallas_call(
        functools.partial(combine_kernel, experts),
        out_shape=shape(tokens.shape[0], width),
        in_specs=[VMEM, VMEM] + [VMEM] * len(back),
        out_specs=VMEM,
        scratch_shapes=[pltpu.VMEM((len(back) * STRIDE, width // 2), BF16)],
        compiler_params=params(14 + experts),
        cost_estimate=cost(3),
        name="combine",
    )(expert_ids.T, combine.T, *back)

    arrived = pl.pallas_call(
        late_kernel,
        out_shape=shape(3, most, width),
        in_specs=[HBM] * 3,
        out_specs=HBM,
        input_output_aliases={0: 0},
        scratch_shapes=[pltpu.SemaphoreType.DMA((6,))],
        compiler_params=params(),
        name="late",
    )(early, straight, swapped[0])
    return mixed, arrived


def solution(mesh):
    placed = (
        P(("replica", "expert"), None),
        P(("replica", "expert"), None),
        P(("replica", "expert"), None),
        P("expert", None),
        P("expert", None),
        P("expert", None),
        P(),
    )
    return jax.shard_map(
        on_device,
        mesh=mesh,
        in_specs=placed,
        out_specs=(P(("replica", "expert"), None), P("replica", "expert", None)),
        check_vma=False,
    )
```

```python
import functools

import jax
import jax.numpy as jnp
from jax import lax
from jax.experimental import pallas as pl
from jax.experimental.pallas import tpu as pltpu
from jax.sharding import PartitionSpec as P

CAP = 12
PACK = 2 * CAP
STRIDE = 32
GROUP = 4
BF16 = jnp.bfloat16
F32 = jnp.float32
VMEM = pl.BlockSpec(memory_space=pltpu.VMEM)
HBM = pl.BlockSpec(memory_space=pltpu.HBM)


def params(megabytes=16):
    return pltpu.CompilerParams(vmem_limit_bytes=megabytes * 1024 * 1024)


def cost(microseconds):
    return pl.CostEstimate(
        flops=microseconds * 10**9, bytes_accessed=10**4, transcendentals=0
    )


def token_places(ids, group, experts):
    tok = ids.shape[1]
    member = []
    for j in range(experts):
        named = jnp.where(ids == lax.rem(group + j, experts), 1.0, 0.0)
        member.append(jnp.sum(named, axis=0, keepdims=True))
    member = jnp.concatenate(member, axis=0)
    row = lax.broadcasted_iota(jnp.int32, (tok, tok), 0)
    col = lax.broadcasted_iota(jnp.int32, (tok, tok), 1)
    upto = jnp.where(row <= col, 1.0, 0.0).astype(BF16)
    rank = jnp.dot(member.astype(BF16), upto, preferred_element_type=F32)
    return jnp.where(member > 0, rank - 1.0, -PACK).astype(jnp.int32)


def dispatch_kernel(experts, ids_ref, tok_ref, *out_refs):
    group = lax.axis_index("expert") // GROUP
    place = token_places(ids_ref[...], group, experts)
    tok, half = tok_ref.shape[0], tok_ref.shape[1] // 2
    slot = lax.broadcasted_iota(jnp.int32, (PACK, tok), 0)
    for j, ref in enumerate(out_refs):
        spot = place[j : j + 1, :]
        left = jnp.where(jnp.logical_and(slot == spot, spot >= 0), 1.0, 0.0).astype(BF16)
        right = jnp.where(slot == spot + CAP, 1.0, 0.0).astype(BF16)
        rows = jnp.dot(left, tok_ref[:, :half], preferred_element_type=F32)
        rows = rows + jnp.dot(right, tok_ref[:, half:], preferred_element_type=F32)
        ref[...] = rows.astype(BF16)


def select_kernel(wanted, plan_ref, gate_ref, up_ref, down_ref, *out_refs):
    device = lax.axis_index("expert")
    even = lax.axis_index("replica") % 2 == 0
    rows = gate_ref.shape[0]

    @pl.when(device % GROUP == GROUP - 1)
    def _():
        plans = []
        for survivor, count, first in wanted:
            plan = plan_ref[survivor, pl.ds(device // GROUP, 1), :]
            if first is None:
                plan = jnp.where(even, plan[:, :count], plan[:, count : 2 * count])
            else:
                plan = plan[:, first : first + count]
            plans.append(plan)
        total = sum(count for _, count, _ in wanted)
        number = lax.broadcasted_iota(jnp.int32, (rows, total), 0)
        pick = jnp.where(number == jnp.concatenate(plans, axis=1), 1.0, 0.0).astype(BF16)
        for m, held_ref in enumerate((gate_ref, up_ref, down_ref)):
            found = lax.dot_general(
                pick, held_ref[...], (((0,), (0,)), ((), ())), preferred_element_type=F32
            ).astype(BF16)
            start = 0
            for (_, count, _), ref in zip(wanted, out_refs):
                ref[m] = found[start : start + count]
                start += count


def place_rows(pieces, out_ref, sems):
    copies = []
    for ref, first in pieces:
        for m in range(3):
            rows = pl.ds(first, ref.shape[1])
            copies.append(
                pltpu.make_async_copy(ref.at[m], out_ref.at[m, rows], sems.at[len(copies)])
            )
    for copy in copies:
        copy.start()
    for copy in copies:
        copy.wait()


def early_kernel(shared_ref, swapped_ref, first_ref, near_ref, out_ref, sems):
    position = lax.axis_index("expert") % GROUP
    parity = lax.axis_index("replica") % 2
    half = shared_ref.shape[1]
    for even in range(2):

        @pl.when(jnp.logical_and(position == 1, parity == even))
        def _():
            place_rows([(shared_ref, half * even), (swapped_ref, half * (1 - even))], out_ref, sems)

    @pl.when(jnp.logical_or(position == 0, position == 3))
    def _():
        place_rows([(first_ref, 0)], out_ref, sems)

    @pl.when(position == 2)
    def _():
        place_rows([(near_ref, 0)], out_ref, sems)


def late_kernel(early_ref, second_ref, begun_ref, out_ref, sems):
    position = lax.axis_index("expert") % GROUP

    @pl.when(jnp.logical_or(position == 0, position == 3))
    def _():
        place_rows([(second_ref, out_ref.shape[1] - second_ref.shape[1])], out_ref, sems)


def begin_kernel(out_ref):
    out_ref[...] = jnp.zeros_like(out_ref)


def expert_kernel(mine_ref, other_ref, gate_ref, up_ref, down_ref, keep_ref, give_ref):
    rows, half = mine_ref.shape
    x = jnp.concatenate([mine_ref[...], other_ref[...]], axis=0)
    total = x.shape[0]
    numbers = (((1,), (1,)), ((), ()))

    def project(ref):
        left = lax.dot_general(x, ref[:, :half], numbers, preferred_element_type=F32)
        right = lax.dot_general(x, ref[:, half:], numbers, preferred_element_type=F32)
        return left + jnp.concatenate([right[CAP:], right[:CAP]], axis=0)

    gate_value = project(gate_ref)
    up_value = project(up_ref)
    hidden = (gate_value / (1.0 + jnp.exp(-gate_value)) * up_value).astype(BF16)
    left = jnp.dot(hidden, down_ref[:, :half], preferred_element_type=F32)
    right = jnp.dot(hidden, down_ref[:, half:], preferred_element_type=F32)
    right = jnp.concatenate([right[total - CAP :], right[: total - CAP]], axis=0)
    row = lax.broadcasted_iota(jnp.int32, (total, half), 0)
    partial = jnp.where(row % PACK < CAP, left, right)
    keep_ref[...] = partial[:rows]
    give_ref[...] = partial[rows:].astype(BF16)


def combine_kernel(experts, ids_ref, weight_ref, *refs):
    piece_refs, (out_ref, rows_ref) = refs[:-2], refs[-2:]
    ids = ids_ref[...]
    group = lax.axis_index("expert") // GROUP
    half = out_ref.shape[1] // 2
    each = len(piece_refs) // experts
    place = token_places(ids, group, experts)
    slot = lax.broadcasted_iota(jnp.int32, (STRIDE, ids.shape[1]), 0)
    numbers = (((0,), (0,)), ((), ()))
    rows_ref[...] = jnp.zeros_like(rows_ref)
    for n, ref in enumerate(piece_refs):
        rows_ref[n * STRIDE : n * STRIDE + PACK, :] = ref[...]
    scaled = [[], []]
    for j in range(experts):
        named = ids == lax.rem(group + j, experts)
        weight = jnp.sum(jnp.where(named, weight_ref[...], 0.0), axis=0, keepdims=True)
        for side in range(2):
            chosen = jnp.where(slot == place[j : j + 1, :] + side * CAP, weight, 0.0)
            scaled[side] += [chosen] * each
    for side in range(2):
        chosen = jnp.concatenate(scaled[side], axis=0)
        high = chosen.astype(BF16)
        low = (chosen - high.astype(F32)).astype(BF16)
        mixed = lax.dot_general(high, rows_ref[...], numbers, preferred_element_type=F32)
        mixed = mixed + lax.dot_general(low, rows_ref[...], numbers, preferred_element_type=F32)
        out_ref[:, side * half : (side + 1) * half] = mixed.astype(BF16)


def on_device(tokens, expert_ids, combine, old_gate, old_up, old_down, move_plan):
    devices = lax.axis_size("expert")
    replicas = lax.axis_size("replica")
    experts = move_plan.shape[0]
    most = move_plan.shape[2]
    width = tokens.shape[1]
    plan = jnp.transpose(move_plan, (1, 0, 2))
    weights = (old_gate, old_up, old_down)
    half = most // 2
    lead = most // 6 * 5

    def shape(*dims, dtype=BF16):
        return jax.ShapeDtypeStruct(dims, dtype)

    def send(block, j, k):
        route = []
        for i in range(devices):
            g, p = i // GROUP, i % GROUP
            route.append((i, GROUP * ((g + j) % experts) + (p ^ k)))
        return lax.ppermute(block, "expert", route)

    def migrate(block, survivor):
        route = [(GROUP * e + GROUP - 1, GROUP * e + survivor) for e in range(experts)]
        return lax.ppermute(block, "expert", route)

    def swap(block, survivor):
        route = []
        for r in range(replicas):
            for e in range(experts):
                i = GROUP * e + survivor
                route.append((i * replicas + r, i * replicas + (r ^ 1)))
        return lax.ppermute(block, ("expert", "replica"), route)

    def select(wanted, held):
        return pl.pallas_call(
            functools.partial(select_kernel, wanted),
            out_shape=[shape(3, count, width) for _, count, _ in wanted],
            in_specs=[VMEM] * 4,
            out_specs=[VMEM] * len(wanted),
            compiler_params=params(),
            cost_estimate=cost(2),
            name="select",
        )(plan, *held)

    begun = pl.pallas_call(
        begin_kernel,
        out_shape=shape(8, 128, dtype=F32),
        out_specs=VMEM,
        cost_estimate=cost(5),
        name="begin",
    )()
    ids, begun = lax.optimization_barrier((expert_ids.T, begun))
    parcels = pl.pallas_call(
        functools.partial(dispatch_kernel, experts),
        out_shape=[shape(PACK, width // 2)] * experts,
        in_specs=[VMEM, VMEM],
        out_specs=[VMEM] * experts,
        compiler_params=params(),
        cost_estimate=cost(2),
        name="dispatch",
    )(ids, tokens)

    pairs = [(j, k) for j in range(experts) for k in (0, 2)]
    held, _ = lax.optimization_barrier((weights, parcels))
    wanted = [(1, half, None), (0, lead, 0), (0, most - lead, lead), (2, most, 0)]
    chosen = select(wanted, held)
    after, _ = lax.optimization_barrier((parcels, chosen))
    mine = [parcels[0]]
    for j, k in pairs[1:]:
        mine.append(send(parcels[j] if k else after[j], j, k))
    shared = migrate(chosen[0], 1)
    first = migrate(chosen[1], 0)
    near = migrate(chosen[3], 2)
    mine = jnp.concatenate(mine, axis=0)
    other = send(mine, 0, 1)

    total = mine.shape[0]
    step = min(total, 4 * PACK)
    row_spec = pl.BlockSpec((step, width // 2), lambda i: (i, 0))
    whole_spec = pl.BlockSpec(old_gate.shape, lambda i: (0, 0))
    keep, give = pl.pallas_call(
        expert_kernel,
        grid=(total // step,),
        out_shape=[shape(total, width // 2, dtype=F32), shape(total, width // 2)],
        in_specs=[row_spec] * 2 + [whole_spec] * 3,
        out_specs=[row_spec] * 2,
        compiler_params=params(),
        cost_estimate=cost(0),
        name="expert",
    )(mine, other, *weights)
    taken, shared = lax.optimization_barrier((send(give, 0, 1), shared))
    summed = (keep + taken.astype(F32)).astype(BF16)
    pieces = [summed[n * PACK : (n + 1) * PACK] for n in range(len(pairs))]
    back = [pieces[0]] + [
        send(block, -j, k) for (j, k), block in zip(pairs[1:], pieces[1:])
    ]
    swapped = swap(shared, 1)
    beside = len(pairs) // 2
    back[beside], near = lax.optimization_barrier((back[beside], near))
    last, _ = lax.optimization_barrier((chosen[2], summed))
    second = migrate(last, 0)

    early = pl.pallas_call(
        early_kernel,
        out_shape=shape(3, most, width),
        in_specs=[HBM] * 4,
        out_specs=HBM,
        scratch_shapes=[pltpu.SemaphoreType.DMA((6,))],
        compiler_params=params(),
        name="early",
    )(shared, swapped, first, near)
    back, early = lax.optimization_barrier((back, early))

    mixed = pl.pallas_call(
        functools.partial(combine_kernel, experts),
        out_shape=shape(tokens.shape[0], width),
        in_specs=[VMEM, VMEM] + [VMEM] * len(back),
        out_specs=VMEM,
        scratch_shapes=[pltpu.VMEM((len(back) * STRIDE, width // 2), BF16)],
        compiler_params=params(14 + experts),
        cost_estimate=cost(3),
        name="combine",
    )(expert_ids.T, combine.T, *back)

    arrived = pl.pallas_call(
        late_kernel,
        out_shape=shape(3, most, width),
        in_specs=[HBM] * 3,
        out_specs=HBM,
        input_output_aliases={0: 0},
        scratch_shapes=[pltpu.SemaphoreType.DMA((3,))],
        compiler_params=params(),
        name="late",
    )(early, second, begun)
    return mixed, arrived


def solution(mesh):
    placed = (
        P(("replica", "expert"), None),
        P(("replica", "expert"), None),
        P(("replica", "expert"), None),
        P("expert", None),
        P("expert", None),
        P("expert", None),
        P(),
    )
    return jax.shard_map(
        on_device,
        mesh=mesh,
        in_specs=placed,
        out_specs=(P(("replica", "expert"), None), P("replica", "expert", None)),
        check_vma=False,
    )
```

```python
import functools

import jax
import jax.numpy as jnp
from jax import lax
from jax.experimental import pallas as pl
from jax.experimental.pallas import tpu as pltpu
from jax.sharding import PartitionSpec as P

CAP = 12
PACK = 2 * CAP
STRIDE = 32
GROUP = 4
BF16 = jnp.bfloat16
F32 = jnp.float32
VMEM = pl.BlockSpec(memory_space=pltpu.VMEM)
HBM = pl.BlockSpec(memory_space=pltpu.HBM)


def params(megabytes=16):
    return pltpu.CompilerParams(vmem_limit_bytes=megabytes * 1024 * 1024)


def cost(microseconds):
    return pl.CostEstimate(
        flops=int(microseconds * 10**9), bytes_accessed=10**4, transcendentals=0
    )


def token_places(ids, group, experts):
    tok = ids.shape[1]
    member = []
    for j in range(experts):
        named = jnp.where(ids == lax.rem(group + j, experts), 1.0, 0.0)
        member.append(jnp.sum(named, axis=0, keepdims=True))
    member = jnp.concatenate(member, axis=0)
    row = lax.broadcasted_iota(jnp.int32, (tok, tok), 0)
    col = lax.broadcasted_iota(jnp.int32, (tok, tok), 1)
    upto = jnp.where(row <= col, 1.0, 0.0).astype(BF16)
    rank = jnp.dot(member.astype(BF16), upto, preferred_element_type=F32)
    return jnp.where(member > 0, rank - 1.0, -PACK).astype(jnp.int32)


def dispatch_kernel(experts, ids_ref, tok_ref, *out_refs):
    group = lax.axis_index("expert") // GROUP
    place = token_places(ids_ref[...], group, experts)
    tok, half = tok_ref.shape[0], tok_ref.shape[1] // 2
    slot = lax.broadcasted_iota(jnp.int32, (PACK, tok), 0)
    for j, ref in enumerate(out_refs):
        spot = place[j : j + 1, :]
        left = jnp.where(jnp.logical_and(slot == spot, spot >= 0), 1.0, 0.0).astype(BF16)
        right = jnp.where(slot == spot + CAP, 1.0, 0.0).astype(BF16)
        rows = jnp.dot(left, tok_ref[:, :half], preferred_element_type=F32)
        rows = rows + jnp.dot(right, tok_ref[:, half:], preferred_element_type=F32)
        ref[...] = rows.astype(BF16)


def select_kernel(wanted, plan_ref, gate_ref, up_ref, down_ref, *out_refs):
    device = lax.axis_index("expert")
    even = lax.axis_index("replica") % 2 == 0
    rows = gate_ref.shape[0]

    @pl.when(device % GROUP == GROUP - 1)
    def _():
        plans = []
        for survivor, count, first in wanted:
            plan = plan_ref[survivor, pl.ds(device // GROUP, 1), :]
            if first is None:
                plan = jnp.where(even, plan[:, :count], plan[:, count : 2 * count])
            else:
                plan = plan[:, first : first + count]
            plans.append(plan)
        total = sum(count for _, count, _ in wanted)
        number = lax.broadcasted_iota(jnp.int32, (rows, total), 0)
        pick = jnp.where(number == jnp.concatenate(plans, axis=1), 1.0, 0.0).astype(BF16)
        for m, held_ref in enumerate((gate_ref, up_ref, down_ref)):
            found = lax.dot_general(
                pick, held_ref[...], (((0,), (0,)), ((), ())), preferred_element_type=F32
            ).astype(BF16)
            start = 0
            for (_, count, _), ref in zip(wanted, out_refs):
                ref[m] = found[start : start + count]
                start += count


def place_rows(pieces, out_ref, sems):
    copies = []
    for ref, first in pieces:
        for m in range(3):
            rows = pl.ds(first, ref.shape[1])
            copies.append(
                pltpu.make_async_copy(ref.at[m], out_ref.at[m, rows], sems.at[len(copies)])
            )
    for copy in copies:
        copy.start()
    for copy in copies:
        copy.wait()


def early_kernel(shared_ref, swapped_ref, out_ref, sems):
    position = lax.axis_index("expert") % GROUP
    parity = lax.axis_index("replica") % 2
    half = shared_ref.shape[1]
    for even in range(2):

        @pl.when(jnp.logical_and(position == 1, parity == even))
        def _():
            place_rows([(shared_ref, half * even), (swapped_ref, half * (1 - even))], out_ref, sems)


def late_kernel(early_ref, straight_ref, near_ref, begun_ref, out_ref, sems):
    position = lax.axis_index("expert") % GROUP

    @pl.when(jnp.logical_or(position == 0, position == 3))
    def _():
        place_rows([(straight_ref, 0)], out_ref, sems)

    @pl.when(position == 2)
    def _():
        place_rows([(near_ref, 0)], out_ref, sems)


def begin_kernel(out_ref):
    out_ref[...] = jnp.zeros_like(out_ref)


def expert_kernel(mine_ref, other_ref, gate_ref, up_ref, down_ref, keep_ref, give_ref):
    rows, half = mine_ref.shape
    x = jnp.concatenate([mine_ref[...], other_ref[...]], axis=0)
    total = x.shape[0]
    numbers = (((1,), (1,)), ((), ()))

    def project(ref):
        left = lax.dot_general(x, ref[:, :half], numbers, preferred_element_type=F32)
        right = lax.dot_general(x, ref[:, half:], numbers, preferred_element_type=F32)
        return left + jnp.concatenate([right[CAP:], right[:CAP]], axis=0)

    gate_value = project(gate_ref)
    up_value = project(up_ref)
    hidden = (gate_value / (1.0 + jnp.exp(-gate_value)) * up_value).astype(BF16)
    left = jnp.dot(hidden, down_ref[:, :half], preferred_element_type=F32)
    right = jnp.dot(hidden, down_ref[:, half:], preferred_element_type=F32)
    right = jnp.concatenate([right[total - CAP :], right[: total - CAP]], axis=0)
    row = lax.broadcasted_iota(jnp.int32, (total, half), 0)
    partial = jnp.where(row % PACK < CAP, left, right)
    keep_ref[...] = partial[:rows]
    give_ref[...] = partial[rows:].astype(BF16)


def weigh_kernel(experts, ids_ref, weight_ref, out_ref):
    ids = ids_ref[...]
    group = lax.axis_index("expert") // GROUP
    place = token_places(ids, group, experts)
    each = out_ref.shape[2] // STRIDE // experts
    slot = lax.broadcasted_iota(jnp.int32, (STRIDE, ids.shape[1]), 0)
    for j in range(experts):
        named = ids == lax.rem(group + j, experts)
        weight = jnp.sum(jnp.where(named, weight_ref[...], 0.0), axis=0, keepdims=True)
        for side in range(2):
            chosen = jnp.where(slot == place[j : j + 1, :] + side * CAP, weight, 0.0)
            high = chosen.astype(BF16)
            low = (chosen - high.astype(F32)).astype(BF16)
            for n in range(j * each, (j + 1) * each):
                out_ref[side, 0, n * STRIDE : (n + 1) * STRIDE, :] = high
                out_ref[side, 1, n * STRIDE : (n + 1) * STRIDE, :] = low


def combine_kernel(scaled_ref, *refs):
    piece_refs, (out_ref, rows_ref) = refs[:-2], refs[-2:]
    half = out_ref.shape[1] // 2
    numbers = (((0,), (0,)), ((), ()))
    for n, ref in enumerate(piece_refs):
        rows_ref[n * STRIDE : n * STRIDE + PACK, :] = ref[...]
        rows_ref[n * STRIDE + PACK : (n + 1) * STRIDE, :] = jnp.zeros((STRIDE - PACK, half), BF16)
    rows = rows_ref[...]
    for side in range(2):
        mixed = lax.dot_general(scaled_ref[side, 0], rows, numbers, preferred_element_type=F32)
        mixed = mixed + lax.dot_general(
            scaled_ref[side, 1], rows, numbers, preferred_element_type=F32
        )
        out_ref[:, side * half : (side + 1) * half] = mixed.astype(BF16)


def on_device(tokens, expert_ids, combine, old_gate, old_up, old_down, move_plan):
    devices = lax.axis_size("expert")
    replicas = lax.axis_size("replica")
    experts = move_plan.shape[0]
    most = move_plan.shape[2]
    width = tokens.shape[1]
    plan = jnp.transpose(move_plan, (1, 0, 2))
    weights = (old_gate, old_up, old_down)
    half = most // 2

    def shape(*dims, dtype=BF16):
        return jax.ShapeDtypeStruct(dims, dtype)

    def send(block, j, k):
        route = []
        for i in range(devices):
            g, p = i // GROUP, i % GROUP
            route.append((i, GROUP * ((g + j) % experts) + (p ^ k)))
        return lax.ppermute(block, "expert", route)

    def migrate(block, survivor):
        route = [(GROUP * e + GROUP - 1, GROUP * e + survivor) for e in range(experts)]
        return lax.ppermute(block, "expert", route)

    def swap(block, survivor):
        route = []
        for r in range(replicas):
            for e in range(experts):
                i = GROUP * e + survivor
                route.append((i * replicas + r, i * replicas + (r ^ 1)))
        return lax.ppermute(block, ("expert", "replica"), route)

    def select(wanted, held):
        return pl.pallas_call(
            functools.partial(select_kernel, wanted),
            out_shape=[shape(3, count, width) for _, count, _ in wanted],
            in_specs=[VMEM] * 4,
            out_specs=[VMEM] * len(wanted),
            compiler_params=params(),
            cost_estimate=cost(2),
            name="select",
        )(plan, *held)

    begun = pl.pallas_call(
        begin_kernel,
        out_shape=shape(8, 128, dtype=F32),
        out_specs=VMEM,
        cost_estimate=cost(5),
        name="begin",
    )()
    ids, begun = lax.optimization_barrier((expert_ids.T, begun))
    parcels = pl.pallas_call(
        functools.partial(dispatch_kernel, experts),
        out_shape=[shape(PACK, width // 2)] * experts,
        in_specs=[VMEM, VMEM],
        out_specs=[VMEM] * experts,
        compiler_params=params(),
        cost_estimate=cost(2),
        name="dispatch",
    )(ids, tokens)

    pairs = [(j, k) for j in range(experts) for k in (0, 2)]
    held, _ = lax.optimization_barrier((weights, parcels))
    wanted = [(1, half, None), (0, most, 0), (2, most, 0)]
    chosen = select(wanted, held)
    after, _ = lax.optimization_barrier((parcels, chosen))
    mine = [parcels[0]]
    for j, k in pairs[1:]:
        mine.append(send(parcels[j] if k else after[j], j, k))
    shared = migrate(chosen[0], 1)
    straight = migrate(chosen[1], 0)
    mine = jnp.concatenate(mine, axis=0)
    other = send(mine, 0, 1)

    total = mine.shape[0]
    step = min(total, 4 * PACK)
    row_spec = pl.BlockSpec((step, width // 2), lambda i: (i, 0))
    whole_spec = pl.BlockSpec(old_gate.shape, lambda i: (0, 0))
    keep, give = pl.pallas_call(
        expert_kernel,
        grid=(total // step,),
        out_shape=[shape(total, width // 2, dtype=F32), shape(total, width // 2)],
        in_specs=[row_spec] * 2 + [whole_spec] * 3,
        out_specs=[row_spec] * 2,
        compiler_params=params(),
        cost_estimate=cost(0),
        name="expert",
    )(mine, other, *weights)
    taken, shared = lax.optimization_barrier((send(give, 0, 1), shared))
    summed = (keep + taken.astype(F32)).astype(BF16)
    pieces = [summed[n * PACK : (n + 1) * PACK] for n in range(len(pairs))]
    back = [pieces[0]] + [
        send(block, -j, k) for (j, k), block in zip(pairs[1:], pieces[1:])
    ]
    swapped = swap(shared, 1)
    swapped, near = lax.optimization_barrier((swapped, chosen[2]))
    near = migrate(near, 2)

    scaled = pl.pallas_call(
        functools.partial(weigh_kernel, experts),
        out_shape=shape(2, 2, len(back) * STRIDE, tokens.shape[0]),
        in_specs=[VMEM, VMEM],
        out_specs=VMEM,
        compiler_params=params(),
        name="weigh",
    )(expert_ids.T, combine.T)
    swapped, scaled = lax.optimization_barrier((swapped, scaled))

    early = pl.pallas_call(
        early_kernel,
        out_shape=shape(3, most, width),
        in_specs=[HBM] * 2,
        out_specs=HBM,
        scratch_shapes=[pltpu.SemaphoreType.DMA((6,))],
        compiler_params=params(),
        name="early",
    )(shared, swapped)
    back, early, straight = lax.optimization_barrier((back, early, straight))

    mixed = pl.pallas_call(
        combine_kernel,
        out_shape=shape(tokens.shape[0], width),
        in_specs=[VMEM] + [VMEM] * len(back),
        out_specs=VMEM,
        scratch_shapes=[pltpu.VMEM((len(back) * STRIDE, width // 2), BF16)],
        compiler_params=params(),
        cost_estimate=cost(12.3),
        name="combine",
    )(scaled, *back)

    arrived = pl.pallas_call(
        late_kernel,
        out_shape=shape(3, most, width),
        in_specs=[HBM] * 4,
        out_specs=HBM,
        input_output_aliases={0: 0},
        scratch_shapes=[pltpu.SemaphoreType.DMA((3,))],
        compiler_params=params(),
        name="late",
    )(early, straight, near, begun)
    return mixed, arrived


def solution(mesh):
    placed = (
        P(("replica", "expert"), None),
        P(("replica", "expert"), None),
        P(("replica", "expert"), None),
        P("expert", None),
        P("expert", None),
        P("expert", None),
        P(),
    )
    return jax.shard_map(
        on_device,
        mesh=mesh,
        in_specs=placed,
        out_specs=(P(("replica", "expert"), None), P("replica", "expert", None)),
        check_vma=False,
    )
```

```python
import functools

import jax
import jax.numpy as jnp
from jax import lax
from jax.experimental import pallas as pl
from jax.experimental.pallas import tpu as pltpu
from jax.sharding import PartitionSpec as P

CAP = 12
PACK = 2 * CAP
STRIDE = 32
GROUP = 4
BF16 = jnp.bfloat16
F32 = jnp.float32
VMEM = pl.BlockSpec(memory_space=pltpu.VMEM)
HBM = pl.BlockSpec(memory_space=pltpu.HBM)


def params(megabytes=16):
    return pltpu.CompilerParams(vmem_limit_bytes=megabytes * 1024 * 1024)


def cost(microseconds):
    return pl.CostEstimate(
        flops=int(microseconds * 10**9), bytes_accessed=10**4, transcendentals=0
    )


def token_places(ids, group, experts):
    tok = ids.shape[1]
    member = []
    for j in range(experts):
        named = jnp.where(ids == lax.rem(group + j, experts), 1.0, 0.0)
        member.append(jnp.sum(named, axis=0, keepdims=True))
    member = jnp.concatenate(member, axis=0)
    row = lax.broadcasted_iota(jnp.int32, (tok, tok), 0)
    col = lax.broadcasted_iota(jnp.int32, (tok, tok), 1)
    upto = jnp.where(row <= col, 1.0, 0.0).astype(BF16)
    rank = jnp.dot(member.astype(BF16), upto, preferred_element_type=F32)
    return jnp.where(member > 0, rank - 1.0, -PACK).astype(jnp.int32)


def dispatch_kernel(experts, ids_ref, tok_ref, *out_refs):
    group = lax.axis_index("expert") // GROUP
    place = token_places(ids_ref[...], group, experts)
    tok, half = tok_ref.shape[0], tok_ref.shape[1] // 2
    slot = lax.broadcasted_iota(jnp.int32, (PACK, tok), 0)
    for j, ref in enumerate(out_refs):
        spot = place[j : j + 1, :]
        left = jnp.where(jnp.logical_and(slot == spot, spot >= 0), 1.0, 0.0).astype(BF16)
        right = jnp.where(slot == spot + CAP, 1.0, 0.0).astype(BF16)
        rows = jnp.dot(left, tok_ref[:, :half], preferred_element_type=F32)
        rows = rows + jnp.dot(right, tok_ref[:, half:], preferred_element_type=F32)
        ref[...] = rows.astype(BF16)


def select_kernel(wanted, plan_ref, gate_ref, up_ref, down_ref, *out_refs):
    device = lax.axis_index("expert")
    even = lax.axis_index("replica") % 2 == 0
    rows = gate_ref.shape[0]

    @pl.when(device % GROUP == GROUP - 1)
    def _():
        plans = []
        for survivor, count, first in wanted:
            plan = plan_ref[survivor, pl.ds(device // GROUP, 1), :]
            if first is None:
                plan = jnp.where(even, plan[:, :count], plan[:, count : 2 * count])
            else:
                plan = plan[:, first : first + count]
            plans.append(plan)
        total = sum(count for _, count, _ in wanted)
        number = lax.broadcasted_iota(jnp.int32, (rows, total), 0)
        pick = jnp.where(number == jnp.concatenate(plans, axis=1), 1.0, 0.0).astype(BF16)
        for m, held_ref in enumerate((gate_ref, up_ref, down_ref)):
            found = lax.dot_general(
                pick, held_ref[...], (((0,), (0,)), ((), ())), preferred_element_type=F32
            ).astype(BF16)
            start = 0
            for (_, count, _), ref in zip(wanted, out_refs):
                ref[m] = found[start : start + count]
                start += count


def place_rows(pieces, out_ref, sems):
    copies = []
    for ref, first in pieces:
        for m in range(3):
            rows = pl.ds(first, ref.shape[1])
            copies.append(
                pltpu.make_async_copy(ref.at[m], out_ref.at[m, rows], sems.at[len(copies)])
            )
    for copy in copies:
        copy.start()
    for copy in copies:
        copy.wait()


def early_kernel(shared_ref, swapped_ref, out_ref, sems):
    position = lax.axis_index("expert") % GROUP
    parity = lax.axis_index("replica") % 2
    half = shared_ref.shape[1]
    for even in range(2):

        @pl.when(jnp.logical_and(position == 1, parity == even))
        def _():
            place_rows([(shared_ref, half * even), (swapped_ref, half * (1 - even))], out_ref, sems)


def late_kernel(filled_ref, near_ref, begun_ref, out_ref, sems):
    @pl.when(lax.axis_index("expert") % GROUP == 2)
    def _():
        place_rows([(near_ref, 0)], out_ref, sems)


def begin_kernel(out_ref):
    out_ref[...] = jnp.zeros_like(out_ref)


def expert_kernel(mine_ref, other_ref, gate_ref, up_ref, down_ref, keep_ref, give_ref):
    rows, half = mine_ref.shape
    x = jnp.concatenate([mine_ref[...], other_ref[...]], axis=0)
    total = x.shape[0]
    numbers = (((1,), (1,)), ((), ()))

    def project(ref):
        left = lax.dot_general(x, ref[:, :half], numbers, preferred_element_type=F32)
        right = lax.dot_general(x, ref[:, half:], numbers, preferred_element_type=F32)
        return left + jnp.concatenate([right[CAP:], right[:CAP]], axis=0)

    gate_value = project(gate_ref)
    up_value = project(up_ref)
    hidden = (gate_value / (1.0 + jnp.exp(-gate_value)) * up_value).astype(BF16)
    left = jnp.dot(hidden, down_ref[:, :half], preferred_element_type=F32)
    right = jnp.dot(hidden, down_ref[:, half:], preferred_element_type=F32)
    right = jnp.concatenate([right[total - CAP :], right[: total - CAP]], axis=0)
    row = lax.broadcasted_iota(jnp.int32, (total, half), 0)
    partial = jnp.where(row % PACK < CAP, left, right)
    keep_ref[...] = partial[:rows]
    give_ref[...] = partial[rows:].astype(BF16)


def weigh_kernel(experts, ids_ref, weight_ref, out_ref):
    ids = ids_ref[...]
    group = lax.axis_index("expert") // GROUP
    place = token_places(ids, group, experts)
    each = out_ref.shape[2] // STRIDE // experts
    slot = lax.broadcasted_iota(jnp.int32, (STRIDE, ids.shape[1]), 0)
    for j in range(experts):
        named = ids == lax.rem(group + j, experts)
        weight = jnp.sum(jnp.where(named, weight_ref[...], 0.0), axis=0, keepdims=True)
        for side in range(2):
            chosen = jnp.where(slot == place[j : j + 1, :] + side * CAP, weight, 0.0)
            high = chosen.astype(BF16)
            low = (chosen - high.astype(F32)).astype(BF16)
            for n in range(j * each, (j + 1) * each):
                out_ref[side, 0, n * STRIDE : (n + 1) * STRIDE, :] = high
                out_ref[side, 1, n * STRIDE : (n + 1) * STRIDE, :] = low


def combine_kernel(scaled_ref, *refs):
    piece_refs, (straight_ref, early_ref, out_ref, arrived_ref) = refs[:-7], refs[-7:-3]
    rows_ref, mixed_ref, sems = refs[-3:]
    half = out_ref.shape[1] // 2
    numbers = (((0,), (0,)), ((), ()))
    direct = lax.axis_index("expert") % GROUP % 3 == 0
    fill = pltpu.make_async_copy(straight_ref, arrived_ref, sems.at[2])

    @pl.when(direct)
    def _():
        fill.start()

    for n, ref in enumerate(piece_refs):
        rows_ref[n * STRIDE : n * STRIDE + PACK, :] = ref[...]
        rows_ref[n * STRIDE + PACK : (n + 1) * STRIDE, :] = jnp.zeros((STRIDE - PACK, half), BF16)
    rows = rows_ref[...]
    copies = []
    for side in range(2):
        mixed = lax.dot_general(scaled_ref[side, 0], rows, numbers, preferred_element_type=F32)
        mixed = mixed + lax.dot_general(
            scaled_ref[side, 1], rows, numbers, preferred_element_type=F32
        )
        columns = pl.ds(side * half, half)
        mixed_ref[:, columns] = mixed.astype(BF16)
        copy = pltpu.make_async_copy(mixed_ref.at[:, columns], out_ref.at[:, columns], sems.at[side])
        copy.start()
        copies.append(copy)
    for copy in copies:
        copy.wait()

    @pl.when(direct)
    def _():
        fill.wait()


def on_device(tokens, expert_ids, combine, old_gate, old_up, old_down, move_plan):
    devices = lax.axis_size("expert")
    replicas = lax.axis_size("replica")
    experts = move_plan.shape[0]
    most = move_plan.shape[2]
    width = tokens.shape[1]
    plan = jnp.transpose(move_plan, (1, 0, 2))
    weights = (old_gate, old_up, old_down)
    half = most // 2

    def shape(*dims, dtype=BF16):
        return jax.ShapeDtypeStruct(dims, dtype)

    def send(block, j, k):
        route = []
        for i in range(devices):
            g, p = i // GROUP, i % GROUP
            route.append((i, GROUP * ((g + j) % experts) + (p ^ k)))
        return lax.ppermute(block, "expert", route)

    def migrate(block, survivor):
        route = [(GROUP * e + GROUP - 1, GROUP * e + survivor) for e in range(experts)]
        return lax.ppermute(block, "expert", route)

    def swap(block, survivor):
        route = []
        for r in range(replicas):
            for e in range(experts):
                i = GROUP * e + survivor
                route.append((i * replicas + r, i * replicas + (r ^ 1)))
        return lax.ppermute(block, ("expert", "replica"), route)

    def select(wanted, held):
        return pl.pallas_call(
            functools.partial(select_kernel, wanted),
            out_shape=[shape(3, count, width) for _, count, _ in wanted],
            in_specs=[VMEM] * 4,
            out_specs=[VMEM] * len(wanted),
            compiler_params=params(),
            cost_estimate=cost(2),
            name="select",
        )(plan, *held)

    begun = pl.pallas_call(
        begin_kernel,
        out_shape=shape(8, 128, dtype=F32),
        out_specs=VMEM,
        cost_estimate=cost(5),
        name="begin",
    )()
    ids, begun = lax.optimization_barrier((expert_ids.T, begun))
    parcels = pl.pallas_call(
        functools.partial(dispatch_kernel, experts),
        out_shape=[shape(PACK, width // 2)] * experts,
        in_specs=[VMEM, VMEM],
        out_specs=[VMEM] * experts,
        compiler_params=params(),
        cost_estimate=cost(2),
        name="dispatch",
    )(ids, tokens)

    pairs = [(j, k) for j in range(experts) for k in (0, 2)]
    held, _ = lax.optimization_barrier((weights, parcels))
    wanted = [(1, half, None), (0, most, 0), (2, most, 0)]
    chosen = select(wanted, held)
    after, _ = lax.optimization_barrier((parcels, chosen))
    mine = [parcels[0]]
    for j, k in pairs[1:]:
        mine.append(send(parcels[j] if k else after[j], j, k))
    shared = migrate(chosen[0], 1)
    straight = migrate(chosen[1], 0)
    mine = jnp.concatenate(mine, axis=0)
    other = send(mine, 0, 1)

    total = mine.shape[0]
    step = min(total, 4 * PACK)
    row_spec = pl.BlockSpec((step, width // 2), lambda i: (i, 0))
    whole_spec = pl.BlockSpec(old_gate.shape, lambda i: (0, 0))
    keep, give = pl.pallas_call(
        expert_kernel,
        grid=(total // step,),
        out_shape=[shape(total, width // 2, dtype=F32), shape(total, width // 2)],
        in_specs=[row_spec] * 2 + [whole_spec] * 3,
        out_specs=[row_spec] * 2,
        compiler_params=params(),
        cost_estimate=cost(0),
        name="expert",
    )(mine, other, *weights)
    taken, shared = lax.optimization_barrier((send(give, 0, 1), shared))
    summed = (keep + taken.astype(F32)).astype(BF16)
    pieces = [summed[n * PACK : (n + 1) * PACK] for n in range(len(pairs))]
    back = [pieces[0]] + [
        send(block, -j, k) for (j, k), block in zip(pairs[1:], pieces[1:])
    ]
    swapped = swap(shared, 1)
    swapped, near = lax.optimization_barrier((swapped, chosen[2]))
    near = migrate(near, 2)

    scaled = pl.pallas_call(
        functools.partial(weigh_kernel, experts),
        out_shape=shape(2, 2, len(back) * STRIDE, tokens.shape[0]),
        in_specs=[VMEM, VMEM],
        out_specs=VMEM,
        compiler_params=params(),
        name="weigh",
    )(expert_ids.T, combine.T)
    swapped, scaled = lax.optimization_barrier((swapped, scaled))

    early = pl.pallas_call(
        early_kernel,
        out_shape=shape(3, most, width),
        in_specs=[HBM] * 2,
        out_specs=HBM,
        scratch_shapes=[pltpu.SemaphoreType.DMA((6,))],
        compiler_params=params(),
        name="early",
    )(shared, swapped)
    back, early, straight = lax.optimization_barrier((back, early, straight))

    mixed, filled = pl.pallas_call(
        combine_kernel,
        out_shape=[shape(tokens.shape[0], width), shape(3, most, width)],
        in_specs=[VMEM] * (len(back) + 1) + [HBM] * 2,
        out_specs=[HBM] * 2,
        input_output_aliases={len(back) + 2: 1},
        scratch_shapes=[
            pltpu.VMEM((len(back) * STRIDE, width // 2), BF16),
            pltpu.VMEM((tokens.shape[0], width), BF16),
            pltpu.SemaphoreType.DMA((3,)),
        ],
        compiler_params=params(),
        cost_estimate=cost(12.3),
        name="combine",
    )(scaled, *back, straight, early)

    arrived = pl.pallas_call(
        late_kernel,
        out_shape=shape(3, most, width),
        in_specs=[HBM] * 3,
        out_specs=HBM,
        input_output_aliases={0: 0},
        scratch_shapes=[pltpu.SemaphoreType.DMA((3,))],
        compiler_params=params(),
        name="late",
    )(filled, near, begun)
    return mixed, arrived


def solution(mesh):
    placed = (
        P(("replica", "expert"), None),
        P(("replica", "expert"), None),
        P(("replica", "expert"), None),
        P("expert", None),
        P("expert", None),
        P("expert", None),
        P(),
    )
    return jax.shard_map(
        on_device,
        mesh=mesh,
        in_specs=placed,
        out_specs=(P(("replica", "expert"), None), P("replica", "expert", None)),
        check_vma=False,
    )
```

```python
import functools

import jax
import jax.numpy as jnp
from jax import lax
from jax.experimental import pallas as pl
from jax.experimental.pallas import tpu as pltpu
from jax.sharding import PartitionSpec as P

CAP = 12
PACK = 2 * CAP
STRIDE = 32
GROUP = 4
BF16 = jnp.bfloat16
F32 = jnp.float32
VMEM = pl.BlockSpec(memory_space=pltpu.VMEM)
HBM = pl.BlockSpec(memory_space=pltpu.HBM)


def params(megabytes=16):
    return pltpu.CompilerParams(vmem_limit_bytes=megabytes * 1024 * 1024)


def cost(microseconds):
    return pl.CostEstimate(
        flops=int(microseconds * 10**9), bytes_accessed=10**4, transcendentals=0
    )


def token_places(ids, group, experts):
    tok = ids.shape[1]
    member = []
    for j in range(experts):
        named = jnp.where(ids == lax.rem(group + j, experts), 1.0, 0.0)
        member.append(jnp.sum(named, axis=0, keepdims=True))
    member = jnp.concatenate(member, axis=0)
    row = lax.broadcasted_iota(jnp.int32, (tok, tok), 0)
    col = lax.broadcasted_iota(jnp.int32, (tok, tok), 1)
    upto = jnp.where(row <= col, 1.0, 0.0).astype(BF16)
    rank = jnp.dot(member.astype(BF16), upto, preferred_element_type=F32)
    return jnp.where(member > 0, rank - 1.0, -PACK).astype(jnp.int32)


def dispatch_kernel(experts, ids_ref, tok_ref, *out_refs):
    group = lax.axis_index("expert") // GROUP
    place = token_places(ids_ref[...], group, experts)
    tok, half = tok_ref.shape[0], tok_ref.shape[1] // 2
    slot = lax.broadcasted_iota(jnp.int32, (PACK, tok), 0)
    for j, ref in enumerate(out_refs):
        spot = place[j : j + 1, :]
        left = jnp.where(jnp.logical_and(slot == spot, spot >= 0), 1.0, 0.0).astype(BF16)
        right = jnp.where(slot == spot + CAP, 1.0, 0.0).astype(BF16)
        rows = jnp.dot(left, tok_ref[:, :half], preferred_element_type=F32)
        rows = rows + jnp.dot(right, tok_ref[:, half:], preferred_element_type=F32)
        ref[...] = rows.astype(BF16)


def select_kernel(wanted, plan_ref, gate_ref, up_ref, down_ref, *out_refs):
    device = lax.axis_index("expert")
    even = lax.axis_index("replica") % 2 == 0
    rows = gate_ref.shape[0]

    @pl.when(device % GROUP == GROUP - 1)
    def _():
        plans = []
        for survivor, count, first in sum(wanted, []):
            plan = plan_ref[survivor, pl.ds(device // GROUP, 1), :]
            if first is None:
                plan = jnp.where(even, plan[:, :count], plan[:, count : 2 * count])
            else:
                plan = plan[:, first : first + count]
            plans.append(plan)
        plan = jnp.concatenate(plans, axis=1)
        number = lax.broadcasted_iota(jnp.int32, (rows, plan.shape[1]), 0)
        pick = jnp.where(number == plan, 1.0, 0.0).astype(BF16)
        for m, held_ref in enumerate((gate_ref, up_ref, down_ref)):
            found = lax.dot_general(
                pick, held_ref[...], (((0,), (0,)), ((), ())), preferred_element_type=F32
            ).astype(BF16)
            start = 0
            for ref in out_refs:
                ref[m] = found[start : start + ref.shape[1]]
                start += ref.shape[1]


def place_rows(pieces, out_ref, sems):
    copies = []
    for ref, first in pieces:
        for m in range(3):
            rows = pl.ds(first, ref.shape[1])
            copies.append(
                pltpu.make_async_copy(ref.at[m], out_ref.at[m, rows], sems.at[len(copies)])
            )
    for copy in copies:
        copy.start()
    for copy in copies:
        copy.wait()


def early_kernel(shared_ref, swapped_ref, beside_ref, relayed_ref, out_ref, sems):
    position = lax.axis_index("expert") % GROUP
    parity = lax.axis_index("replica") % 2
    half = shared_ref.shape[1]
    for even in range(2):

        @pl.when(jnp.logical_and(position == 1, parity == even))
        def _():
            place_rows([(shared_ref, half * even), (swapped_ref, half * (1 - even))], out_ref, sems)

    @pl.when(position == 2)
    def _():
        rows = beside_ref.shape[1] - relayed_ref.shape[1]
        place_rows([(beside_ref.at[:, pl.ds(0, rows)], 0)], out_ref, sems)

    @pl.when(position % 3 == 0)
    def _():
        place_rows([(relayed_ref, out_ref.shape[1] - relayed_ref.shape[1])], out_ref, sems)


def late_kernel(filled_ref, near_ref, begun_ref, out_ref, sems):
    @pl.when(lax.axis_index("expert") % GROUP == 2)
    def _():
        place_rows([(near_ref, out_ref.shape[1] - near_ref.shape[1])], out_ref, sems)


def begin_kernel(out_ref):
    out_ref[...] = jnp.zeros_like(out_ref)


def expert_kernel(mine_ref, other_ref, gate_ref, up_ref, down_ref, keep_ref, give_ref):
    rows, half = mine_ref.shape
    x = jnp.concatenate([mine_ref[...], other_ref[...]], axis=0)
    total = x.shape[0]
    numbers = (((1,), (1,)), ((), ()))

    def project(ref):
        left = lax.dot_general(x, ref[:, :half], numbers, preferred_element_type=F32)
        right = lax.dot_general(x, ref[:, half:], numbers, preferred_element_type=F32)
        return left + jnp.concatenate([right[CAP:], right[:CAP]], axis=0)

    gate_value = project(gate_ref)
    up_value = project(up_ref)
    hidden = (gate_value / (1.0 + jnp.exp(-gate_value)) * up_value).astype(BF16)
    left = jnp.dot(hidden, down_ref[:, :half], preferred_element_type=F32)
    right = jnp.dot(hidden, down_ref[:, half:], preferred_element_type=F32)
    right = jnp.concatenate([right[total - CAP :], right[: total - CAP]], axis=0)
    row = lax.broadcasted_iota(jnp.int32, (total, half), 0)
    partial = jnp.where(row % PACK < CAP, left, right)
    keep_ref[...] = partial[:rows]
    give_ref[...] = partial[rows:].astype(BF16)


def weigh_kernel(experts, ids_ref, weight_ref, out_ref):
    ids = ids_ref[...]
    group = lax.axis_index("expert") // GROUP
    place = token_places(ids, group, experts)
    each = out_ref.shape[2] // STRIDE // experts
    slot = lax.broadcasted_iota(jnp.int32, (STRIDE, ids.shape[1]), 0)
    for j in range(experts):
        named = ids == lax.rem(group + j, experts)
        weight = jnp.sum(jnp.where(named, weight_ref[...], 0.0), axis=0, keepdims=True)
        for side in range(2):
            chosen = jnp.where(slot == place[j : j + 1, :] + side * CAP, weight, 0.0)
            high = chosen.astype(BF16)
            low = (chosen - high.astype(F32)).astype(BF16)
            for n in range(j * each, (j + 1) * each):
                out_ref[side, 0, n * STRIDE : (n + 1) * STRIDE, :] = high
                out_ref[side, 1, n * STRIDE : (n + 1) * STRIDE, :] = low


def combine_kernel(scaled_ref, *refs):
    piece_refs, (straight_ref, early_ref, out_ref, arrived_ref) = refs[:-7], refs[-7:-3]
    rows_ref, mixed_ref, sems = refs[-3:]
    half = out_ref.shape[1] // 2
    numbers = (((0,), (0,)), ((), ()))
    direct = lax.axis_index("expert") % GROUP % 3 == 0
    rows_at = pl.ds(0, straight_ref.shape[1])
    fill = pltpu.make_async_copy(straight_ref, arrived_ref.at[:, rows_at], sems.at[2])

    @pl.when(direct)
    def _():
        fill.start()

    for n, ref in enumerate(piece_refs):
        rows_ref[n * STRIDE : n * STRIDE + PACK, :] = ref[...]
        rows_ref[n * STRIDE + PACK : (n + 1) * STRIDE, :] = jnp.zeros((STRIDE - PACK, half), BF16)
    rows = rows_ref[...]
    copies = []
    for side in range(2):
        mixed = lax.dot_general(scaled_ref[side, 0], rows, numbers, preferred_element_type=F32)
        mixed = mixed + lax.dot_general(
            scaled_ref[side, 1], rows, numbers, preferred_element_type=F32
        )
        columns = pl.ds(side * half, half)
        mixed_ref[:, columns] = mixed.astype(BF16)
        copy = pltpu.make_async_copy(mixed_ref.at[:, columns], out_ref.at[:, columns], sems.at[side])
        copy.start()
        copies.append(copy)
    for copy in copies:
        copy.wait()

    @pl.when(direct)
    def _():
        fill.wait()


def on_device(tokens, expert_ids, combine, old_gate, old_up, old_down, move_plan):
    devices = lax.axis_size("expert")
    replicas = lax.axis_size("replica")
    experts = move_plan.shape[0]
    most = move_plan.shape[2]
    width = tokens.shape[1]
    plan = jnp.transpose(move_plan, (1, 0, 2))
    weights = (old_gate, old_up, old_down)
    half = most // 2
    lead = most // 6 * 5
    ahead = half - (most - lead)

    def shape(*dims, dtype=BF16):
        return jax.ShapeDtypeStruct(dims, dtype)

    def send(block, j, k):
        route = []
        for i in range(devices):
            g, p = i // GROUP, i % GROUP
            route.append((i, GROUP * ((g + j) % experts) + (p ^ k)))
        return lax.ppermute(block, "expert", route)

    def migrate(block, survivor, source=GROUP - 1):
        route = [(GROUP * e + source, GROUP * e + survivor) for e in range(experts)]
        return lax.ppermute(block, "expert", route)

    def swap(block, survivor):
        route = []
        for r in range(replicas):
            for e in range(experts):
                i = GROUP * e + survivor
                route.append((i * replicas + r, i * replicas + (r ^ 1)))
        return lax.ppermute(block, ("expert", "replica"), route)

    def select(wanted, held):
        return pl.pallas_call(
            functools.partial(select_kernel, wanted),
            out_shape=[shape(3, sum(piece[1] for piece in part), width) for part in wanted],
            in_specs=[VMEM] * 4,
            out_specs=[VMEM] * len(wanted),
            compiler_params=params(),
            cost_estimate=cost(2),
            name="select",
        )(plan, *held)

    begun = pl.pallas_call(
        begin_kernel,
        out_shape=shape(8, 128, dtype=F32),
        out_specs=VMEM,
        cost_estimate=cost(5),
        name="begin",
    )()
    ids, begun = lax.optimization_barrier((expert_ids.T, begun))
    parcels = pl.pallas_call(
        functools.partial(dispatch_kernel, experts),
        out_shape=[shape(PACK, width // 2)] * experts,
        in_specs=[VMEM, VMEM],
        out_specs=[VMEM] * experts,
        compiler_params=params(),
        cost_estimate=cost(2),
        name="dispatch",
    )(ids, tokens)

    pairs = [(j, k) for j in range(experts) for k in (0, 2)]
    held, _ = lax.optimization_barrier((weights, parcels))
    wanted = [
        [(1, half, None)],
        [(0, lead, 0)],
        [(2, ahead, 0), (0, most - lead, lead)],
        [(2, most - ahead, ahead)],
    ]
    chosen = select(wanted, held)
    after, _ = lax.optimization_barrier((parcels, chosen))
    mine = [parcels[0]]
    for j, k in pairs[1:]:
        mine.append(send(parcels[j] if k else after[j], j, k))
    shared = migrate(chosen[0], 1)
    straight = migrate(chosen[1], 0)
    beside = migrate(chosen[2], 2)
    mine = jnp.concatenate(mine, axis=0)
    other = send(mine, 0, 1)

    total = mine.shape[0]
    step = min(total, 4 * PACK)
    row_spec = pl.BlockSpec((step, width // 2), lambda i: (i, 0))
    whole_spec = pl.BlockSpec(old_gate.shape, lambda i: (0, 0))
    keep, give = pl.pallas_call(
        expert_kernel,
        grid=(total // step,),
        out_shape=[shape(total, width // 2, dtype=F32), shape(total, width // 2)],
        in_specs=[row_spec] * 2 + [whole_spec] * 3,
        out_specs=[row_spec] * 2,
        compiler_params=params(),
        cost_estimate=cost(0),
        name="expert",
    )(mine, other, *weights)
    taken, shared, beside = lax.optimization_barrier((send(give, 0, 1), shared, beside))
    summed = (keep + taken.astype(F32)).astype(BF16)
    pieces = [summed[n * PACK : (n + 1) * PACK] for n in range(len(pairs))]
    back = [send(block, -j, k) for (j, k), block in zip(pairs[2:], pieces[2:])]
    back[0], across = lax.optimization_barrier((back[0], pieces[1]))
    back = [pieces[0], send(across, 0, 2)] + back
    swapped = swap(shared, 1)
    relayed = migrate(beside[:, ahead:], 0, GROUP - 2)
    swapped, near = lax.optimization_barrier((swapped, chosen[3]))
    near = migrate(near, 2)

    scaled = pl.pallas_call(
        functools.partial(weigh_kernel, experts),
        out_shape=shape(2, 2, len(back) * STRIDE, tokens.shape[0]),
        in_specs=[VMEM, VMEM],
        out_specs=VMEM,
        compiler_params=params(),
        name="weigh",
    )(expert_ids.T, combine.T)
    swapped, scaled = lax.optimization_barrier((swapped, scaled))

    early = pl.pallas_call(
        early_kernel,
        out_shape=shape(3, most, width),
        in_specs=[HBM] * 4,
        out_specs=HBM,
        scratch_shapes=[pltpu.SemaphoreType.DMA((6,))],
        compiler_params=params(),
        name="early",
    )(shared, swapped, beside, relayed)
    back, early, straight = lax.optimization_barrier((back, early, straight))

    mixed, filled = pl.pallas_call(
        combine_kernel,
        out_shape=[shape(tokens.shape[0], width), shape(3, most, width)],
        in_specs=[VMEM] * (len(back) + 1) + [HBM] * 2,
        out_specs=[HBM] * 2,
        input_output_aliases={len(back) + 2: 1},
        scratch_shapes=[
            pltpu.VMEM((len(back) * STRIDE, width // 2), BF16),
            pltpu.VMEM((tokens.shape[0], width), BF16),
            pltpu.SemaphoreType.DMA((3,)),
        ],
        compiler_params=params(),
        cost_estimate=cost(8.7),
        name="combine",
    )(scaled, *back, straight, early)

    arrived = pl.pallas_call(
        late_kernel,
        out_shape=shape(3, most, width),
        in_specs=[HBM] * 3,
        out_specs=HBM,
        input_output_aliases={0: 0},
        scratch_shapes=[pltpu.SemaphoreType.DMA((3,))],
        compiler_params=params(),
        name="late",
    )(filled, near, begun)
    return mixed, arrived


def solution(mesh):
    placed = (
        P(("replica", "expert"), None),
        P(("replica", "expert"), None),
        P(("replica", "expert"), None),
        P("expert", None),
        P("expert", None),
        P("expert", None),
        P(),
    )
    return jax.shard_map(
        on_device,
        mesh=mesh,
        in_specs=placed,
        out_specs=(P(("replica", "expert"), None), P("replica", "expert", None)),
        check_vma=False,
    )
```

```python
import functools

import jax
import jax.numpy as jnp
from jax import lax
from jax.experimental import pallas as pl
from jax.experimental.pallas import tpu as pltpu
from jax.sharding import PartitionSpec as P

CAP = 12
PACK = 2 * CAP
STRIDE = 32
GROUP = 4
BF16 = jnp.bfloat16
F32 = jnp.float32
VMEM = pl.BlockSpec(memory_space=pltpu.VMEM)
HBM = pl.BlockSpec(memory_space=pltpu.HBM)


def params(megabytes=16):
    return pltpu.CompilerParams(vmem_limit_bytes=megabytes * 1024 * 1024)


def cost(microseconds):
    return pl.CostEstimate(
        flops=int(microseconds * 10**9), bytes_accessed=10**4, transcendentals=0
    )


def token_places(ids, group, experts):
    tok = ids.shape[1]
    member = []
    for j in range(experts):
        named = jnp.where(ids == lax.rem(group + j, experts), 1.0, 0.0)
        member.append(jnp.sum(named, axis=0, keepdims=True))
    member = jnp.concatenate(member, axis=0)
    row = lax.broadcasted_iota(jnp.int32, (tok, tok), 0)
    col = lax.broadcasted_iota(jnp.int32, (tok, tok), 1)
    upto = jnp.where(row <= col, 1.0, 0.0).astype(BF16)
    rank = jnp.dot(member.astype(BF16), upto, preferred_element_type=F32)
    return jnp.where(member > 0, rank - 1.0, -PACK).astype(jnp.int32)


def dispatch_kernel(experts, ids_ref, tok_ref, *out_refs):
    group = lax.axis_index("expert") // GROUP
    place = token_places(ids_ref[...], group, experts)
    tok, half = tok_ref.shape[0], tok_ref.shape[1] // 2
    slot = lax.broadcasted_iota(jnp.int32, (PACK, tok), 0)
    for j, ref in enumerate(out_refs):
        spot = place[j : j + 1, :]
        left = jnp.where(jnp.logical_and(slot == spot, spot >= 0), 1.0, 0.0).astype(BF16)
        right = jnp.where(slot == spot + CAP, 1.0, 0.0).astype(BF16)
        rows = jnp.dot(left, tok_ref[:, :half], preferred_element_type=F32)
        rows = rows + jnp.dot(right, tok_ref[:, half:], preferred_element_type=F32)
        ref[...] = rows.astype(BF16)


def select_kernel(wanted, plan_ref, gate_ref, up_ref, down_ref, *out_refs):
    device = lax.axis_index("expert")
    even = lax.axis_index("replica") % 2 == 0
    rows = gate_ref.shape[0]

    @pl.when(device % GROUP == GROUP - 1)
    def _():
        plans = []
        for survivor, count, first in wanted:
            plan = plan_ref[survivor, pl.ds(device // GROUP, 1), :]
            if first is None:
                plan = jnp.where(even, plan[:, :count], plan[:, count : 2 * count])
            else:
                plan = plan[:, first : first + count]
            plans.append(plan)
        total = sum(count for _, count, _ in wanted)
        number = lax.broadcasted_iota(jnp.int32, (rows, total), 0)
        pick = jnp.where(number == jnp.concatenate(plans, axis=1), 1.0, 0.0).astype(BF16)
        for m, held_ref in enumerate((gate_ref, up_ref, down_ref)):
            found = lax.dot_general(
                pick, held_ref[...], (((0,), (0,)), ((), ())), preferred_element_type=F32
            ).astype(BF16)
            start = 0
            for (_, count, _), ref in zip(wanted, out_refs):
                ref[m] = found[start : start + count]
                start += count


def place_rows(pieces, out_ref, sems):
    copies = []
    for ref, first in pieces:
        for m in range(3):
            rows = pl.ds(first, ref.shape[1])
            copies.append(
                pltpu.make_async_copy(ref.at[m], out_ref.at[m, rows], sems.at[len(copies)])
            )
    for copy in copies:
        copy.start()
    for copy in copies:
        copy.wait()


def early_kernel(shared_ref, swapped_ref, out_ref, sems):
    position = lax.axis_index("expert") % GROUP
    parity = lax.axis_index("replica") % 2
    half = shared_ref.shape[1]
    for even in range(2):

        @pl.when(jnp.logical_and(position == 1, parity == even))
        def _():
            place_rows([(shared_ref, half * even), (swapped_ref, half * (1 - even))], out_ref, sems)


def late_kernel(filled_ref, near_ref, begun_ref, out_ref, sems):
    @pl.when(lax.axis_index("expert") % GROUP == 2)
    def _():
        place_rows([(near_ref, 0)], out_ref, sems)


def begin_kernel(out_ref):
    out_ref[...] = jnp.zeros_like(out_ref)


def expert_kernel(mine_ref, other_ref, gate_ref, up_ref, down_ref, keep_ref, give_ref):
    rows, half = mine_ref.shape
    x = jnp.concatenate([mine_ref[...], other_ref[...]], axis=0)
    total = x.shape[0]
    numbers = (((1,), (1,)), ((), ()))

    def project(ref):
        left = lax.dot_general(x, ref[:, :half], numbers, preferred_element_type=F32)
        right = lax.dot_general(x, ref[:, half:], numbers, preferred_element_type=F32)
        return left + jnp.concatenate([right[CAP:], right[:CAP]], axis=0)

    gate_value = project(gate_ref)
    up_value = project(up_ref)
    hidden = (gate_value / (1.0 + jnp.exp(-gate_value)) * up_value).astype(BF16)
    left = jnp.dot(hidden, down_ref[:, :half], preferred_element_type=F32)
    right = jnp.dot(hidden, down_ref[:, half:], preferred_element_type=F32)
    right = jnp.concatenate([right[total - CAP :], right[: total - CAP]], axis=0)
    row = lax.broadcasted_iota(jnp.int32, (total, half), 0)
    partial = jnp.where(row % PACK < CAP, left, right)
    keep_ref[...] = partial[:rows]
    give_ref[...] = partial[rows:].astype(BF16)


def weigh_kernel(experts, ids_ref, weight_ref, out_ref):
    ids = ids_ref[...]
    group = lax.axis_index("expert") // GROUP
    place = token_places(ids, group, experts)
    each = out_ref.shape[3] // STRIDE // experts
    slot = lax.broadcasted_iota(jnp.int32, (STRIDE, ids.shape[1]), 0)
    chosen = [[], []]
    for j in range(experts):
        named = ids == lax.rem(group + j, experts)
        weight = jnp.sum(jnp.where(named, weight_ref[...], 0.0), axis=0, keepdims=True)
        for side in range(2):
            block = jnp.where(slot == place[j : j + 1, :] + side * CAP, weight, 0.0)
            chosen[side] += [block] * each
    for side in range(2):
        scaled = jnp.concatenate(chosen[side], axis=0).T
        high = scaled.astype(BF16)
        out_ref[side, 0] = high
        out_ref[side, 1] = (scaled - high.astype(F32)).astype(BF16)


def combine_kernel(scaled_ref, *refs):
    piece_refs, (straight_ref, early_ref, out_ref, arrived_ref) = refs[:-6], refs[-6:-2]
    mixed_ref, sems = refs[-2:]
    half = out_ref.shape[1] // 2
    direct = lax.axis_index("expert") % GROUP % 3 == 0
    fill = pltpu.make_async_copy(straight_ref, arrived_ref, sems.at[2])

    @pl.when(direct)
    def _():
        fill.start()

    blank = jnp.zeros((STRIDE - PACK, half), F32)
    rows = []
    for ref in piece_refs:
        rows += [ref[...].astype(F32), blank]
    rows = jnp.concatenate(rows, axis=0).astype(BF16)
    copies = []
    for side in range(2):
        mixed = jnp.dot(scaled_ref[side, 0], rows, preferred_element_type=F32)
        mixed = mixed + jnp.dot(scaled_ref[side, 1], rows, preferred_element_type=F32)
        columns = pl.ds(side * half, half)
        mixed_ref[:, columns] = mixed.astype(BF16)
        copy = pltpu.make_async_copy(mixed_ref.at[:, columns], out_ref.at[:, columns], sems.at[side])
        copy.start()
        copies.append(copy)
    for copy in copies:
        copy.wait()

    @pl.when(direct)
    def _():
        fill.wait()


def on_device(tokens, expert_ids, combine, old_gate, old_up, old_down, move_plan):
    devices = lax.axis_size("expert")
    replicas = lax.axis_size("replica")
    experts = move_plan.shape[0]
    most = move_plan.shape[2]
    width = tokens.shape[1]
    plan = jnp.transpose(move_plan, (1, 0, 2))
    weights = (old_gate, old_up, old_down)
    half = most // 2

    def shape(*dims, dtype=BF16):
        return jax.ShapeDtypeStruct(dims, dtype)

    def send(block, j, k):
        route = []
        for i in range(devices):
            g, p = i // GROUP, i % GROUP
            route.append((i, GROUP * ((g + j) % experts) + (p ^ k)))
        return lax.ppermute(block, "expert", route)

    def migrate(block, survivor):
        route = [(GROUP * e + GROUP - 1, GROUP * e + survivor) for e in range(experts)]
        return lax.ppermute(block, "expert", route)

    def swap(block, survivor):
        route = []
        for r in range(replicas):
            for e in range(experts):
                i = GROUP * e + survivor
                route.append((i * replicas + r, i * replicas + (r ^ 1)))
        return lax.ppermute(block, ("expert", "replica"), route)

    def select(wanted, held):
        return pl.pallas_call(
            functools.partial(select_kernel, wanted),
            out_shape=[shape(3, count, width) for _, count, _ in wanted],
            in_specs=[VMEM] * 4,
            out_specs=[VMEM] * len(wanted),
            compiler_params=params(),
            cost_estimate=cost(2),
            name="select",
        )(plan, *held)

    begun = pl.pallas_call(
        begin_kernel,
        out_shape=shape(8, 128, dtype=F32),
        out_specs=VMEM,
        cost_estimate=cost(5),
        name="begin",
    )()
    ids, begun = lax.optimization_barrier((expert_ids.T, begun))
    parcels = pl.pallas_call(
        functools.partial(dispatch_kernel, experts),
        out_shape=[shape(PACK, width // 2)] * experts,
        in_specs=[VMEM, VMEM],
        out_specs=[VMEM] * experts,
        compiler_params=params(),
        cost_estimate=cost(2),
        name="dispatch",
    )(ids, tokens)

    pairs = [(j, k) for j in range(experts) for k in (0, 2)]
    held, _ = lax.optimization_barrier((weights, parcels))
    wanted = [(1, half, None), (0, most, 0), (2, most, 0)]
    chosen = select(wanted, held)
    after, _ = lax.optimization_barrier((parcels, chosen))
    mine = [parcels[0]]
    for j, k in pairs[1:]:
        mine.append(send(parcels[j] if k else after[j], j, k))
    shared = migrate(chosen[0], 1)
    straight = migrate(chosen[1], 0)
    mine = jnp.concatenate(mine, axis=0)
    other = send(mine, 0, 1)

    total = mine.shape[0]
    step = min(total, 4 * PACK)
    row_spec = pl.BlockSpec((step, width // 2), lambda i: (i, 0))
    whole_spec = pl.BlockSpec(old_gate.shape, lambda i: (0, 0))
    keep, give = pl.pallas_call(
        expert_kernel,
        grid=(total // step,),
        out_shape=[shape(total, width // 2, dtype=F32), shape(total, width // 2)],
        in_specs=[row_spec] * 2 + [whole_spec] * 3,
        out_specs=[row_spec] * 2,
        compiler_params=params(),
        cost_estimate=cost(0),
        name="expert",
    )(mine, other, *weights)
    taken, shared = lax.optimization_barrier((send(give, 0, 1), shared))
    summed = (keep + taken.astype(F32)).astype(BF16)
    pieces = [summed[n * PACK : (n + 1) * PACK] for n in range(len(pairs))]
    back = [pieces[0]] + [
        send(block, -j, k) for (j, k), block in zip(pairs[1:], pieces[1:])
    ]
    swapped = swap(shared, 1)
    swapped, near = lax.optimization_barrier((swapped, chosen[2]))
    near = migrate(near, 2)

    scaled = pl.pallas_call(
        functools.partial(weigh_kernel, experts),
        out_shape=shape(2, 2, tokens.shape[0], len(back) * STRIDE),
        in_specs=[VMEM, VMEM],
        out_specs=VMEM,
        compiler_params=params(),
        name="weigh",
    )(expert_ids.T, combine.T)
    swapped, scaled = lax.optimization_barrier((swapped, scaled))

    early = pl.pallas_call(
        early_kernel,
        out_shape=shape(3, most, width),
        in_specs=[HBM] * 2,
        out_specs=HBM,
        scratch_shapes=[pltpu.SemaphoreType.DMA((6,))],
        compiler_params=params(),
        name="early",
    )(shared, swapped)
    back, early, straight = lax.optimization_barrier((back, early, straight))

    mixed, filled = pl.pallas_call(
        combine_kernel,
        out_shape=[shape(tokens.shape[0], width), shape(3, most, width)],
        in_specs=[VMEM] * (len(back) + 1) + [HBM] * 2,
        out_specs=[HBM] * 2,
        input_output_aliases={len(back) + 2: 1},
        scratch_shapes=[
            pltpu.VMEM((tokens.shape[0], width), BF16),
            pltpu.SemaphoreType.DMA((3,)),
        ],
        compiler_params=params(),
        cost_estimate=cost(12.3),
        name="combine",
    )(scaled, *back, straight, early)

    arrived = pl.pallas_call(
        late_kernel,
        out_shape=shape(3, most, width),
        in_specs=[HBM] * 3,
        out_specs=HBM,
        input_output_aliases={0: 0},
        scratch_shapes=[pltpu.SemaphoreType.DMA((3,))],
        compiler_params=params(),
        name="late",
    )(filled, near, begun)
    return mixed, arrived


def solution(mesh):
    placed = (
        P(("replica", "expert"), None),
        P(("replica", "expert"), None),
        P(("replica", "expert"), None),
        P("expert", None),
        P("expert", None),
        P("expert", None),
        P(),
    )
    return jax.shard_map(
        on_device,
        mesh=mesh,
        in_specs=placed,
        out_specs=(P(("replica", "expert"), None), P("replica", "expert", None)),
        check_vma=False,
    )
```

```python
import functools

import jax
import jax.numpy as jnp
from jax import lax
from jax.experimental import pallas as pl
from jax.experimental.pallas import tpu as pltpu
from jax.sharding import PartitionSpec as P

CAP = 12
PACK = 2 * CAP
STRIDE = 32
GROUP = 4
BF16 = jnp.bfloat16
F32 = jnp.float32
VMEM = pl.BlockSpec(memory_space=pltpu.VMEM)
HBM = pl.BlockSpec(memory_space=pltpu.HBM)


def params(megabytes=16):
    return pltpu.CompilerParams(vmem_limit_bytes=megabytes * 1024 * 1024)


def cost(microseconds):
    return pl.CostEstimate(
        flops=int(microseconds * 10**9), bytes_accessed=10**4, transcendentals=0
    )


def token_places(ids, group, experts):
    tok = ids.shape[1]
    member = []
    for j in range(experts):
        named = jnp.where(ids == lax.rem(group + j, experts), 1.0, 0.0)
        member.append(jnp.sum(named, axis=0, keepdims=True))
    member = jnp.concatenate(member, axis=0)
    row = lax.broadcasted_iota(jnp.int32, (tok, tok), 0)
    col = lax.broadcasted_iota(jnp.int32, (tok, tok), 1)
    upto = jnp.where(row <= col, 1.0, 0.0).astype(BF16)
    rank = jnp.dot(member.astype(BF16), upto, preferred_element_type=F32)
    return jnp.where(member > 0, rank - 1.0, -PACK).astype(jnp.int32)


def dispatch_kernel(experts, ids_ref, tok_ref, *out_refs):
    group = lax.axis_index("expert") // GROUP
    place = token_places(ids_ref[...], group, experts)
    tok, half = tok_ref.shape[0], tok_ref.shape[1] // 2
    slot = lax.broadcasted_iota(jnp.int32, (PACK, tok), 0)
    for j, ref in enumerate(out_refs):
        spot = place[j : j + 1, :]
        left = jnp.where(jnp.logical_and(slot == spot, spot >= 0), 1.0, 0.0).astype(BF16)
        right = jnp.where(slot == spot + CAP, 1.0, 0.0).astype(BF16)
        rows = jnp.dot(left, tok_ref[:, :half], preferred_element_type=F32)
        rows = rows + jnp.dot(right, tok_ref[:, half:], preferred_element_type=F32)
        ref[...] = rows.astype(BF16)


def select_kernel(wanted, plan_ref, gate_ref, up_ref, down_ref, *out_refs):
    device = lax.axis_index("expert")
    even = lax.axis_index("replica") % 2 == 0
    rows = gate_ref.shape[0]

    @pl.when(device % GROUP == GROUP - 1)
    def _():
        plans = []
        for survivor, count, first in wanted:
            plan = plan_ref[survivor, pl.ds(device // GROUP, 1), :]
            if first is None:
                plan = jnp.where(even, plan[:, :count], plan[:, count : 2 * count])
            else:
                plan = plan[:, first : first + count]
            plans.append(plan)
        total = sum(count for _, count, _ in wanted)
        number = lax.broadcasted_iota(jnp.int32, (rows, total), 0)
        pick = jnp.where(number == jnp.concatenate(plans, axis=1), 1.0, 0.0).astype(BF16)
        for m, held_ref in enumerate((gate_ref, up_ref, down_ref)):
            found = lax.dot_general(
                pick, held_ref[...], (((0,), (0,)), ((), ())), preferred_element_type=F32
            ).astype(BF16)
            start = 0
            for (_, count, _), ref in zip(wanted, out_refs):
                ref[m] = found[start : start + count]
                start += count


def place_rows(pieces, out_ref, sems):
    copies = []
    for ref, first in pieces:
        for m in range(3):
            rows = pl.ds(first, ref.shape[1])
            copies.append(
                pltpu.make_async_copy(ref.at[m], out_ref.at[m, rows], sems.at[len(copies)])
            )
    for copy in copies:
        copy.start()
    for copy in copies:
        copy.wait()


def early_kernel(shared_ref, swapped_ref, out_ref, sems):
    position = lax.axis_index("expert") % GROUP
    parity = lax.axis_index("replica") % 2
    half = shared_ref.shape[1]
    for even in range(2):

        @pl.when(jnp.logical_and(position == 1, parity == even))
        def _():
            place_rows([(shared_ref, half * even), (swapped_ref, half * (1 - even))], out_ref, sems)


def late_kernel(filled_ref, near_ref, begun_ref, out_ref, sems):
    @pl.when(lax.axis_index("expert") % GROUP == 2)
    def _():
        place_rows([(near_ref, 0)], out_ref, sems)


def begin_kernel(out_ref):
    out_ref[...] = jnp.zeros_like(out_ref)


def expert_kernel(mine_ref, other_ref, gate_ref, up_ref, down_ref, keep_ref, give_ref):
    rows, half = mine_ref.shape
    x = jnp.concatenate([mine_ref[...], other_ref[...]], axis=0)
    total = x.shape[0]
    numbers = (((1,), (1,)), ((), ()))

    def project(ref):
        left = lax.dot_general(x, ref[:, :half], numbers, preferred_element_type=F32)
        right = lax.dot_general(x, ref[:, half:], numbers, preferred_element_type=F32)
        return left + jnp.concatenate([right[CAP:], right[:CAP]], axis=0)

    gate_value = project(gate_ref)
    up_value = project(up_ref)
    hidden = (gate_value / (1.0 + jnp.exp(-gate_value)) * up_value).astype(BF16)
    left = jnp.dot(hidden, down_ref[:, :half], preferred_element_type=F32)
    right = jnp.dot(hidden, down_ref[:, half:], preferred_element_type=F32)
    right = jnp.concatenate([right[total - CAP :], right[: total - CAP]], axis=0)
    row = lax.broadcasted_iota(jnp.int32, (total, half), 0)
    partial = jnp.where(row % PACK < CAP, left, right)
    keep_ref[...] = partial[:rows]
    give_ref[...] = partial[rows:].astype(BF16)


def weigh_kernel(experts, ids_ref, weight_ref, out_ref):
    ids = ids_ref[...]
    group = lax.axis_index("expert") // GROUP
    place = token_places(ids, group, experts)
    each = out_ref.shape[3] // STRIDE // experts
    slot = lax.broadcasted_iota(jnp.int32, (STRIDE, ids.shape[1]), 0)
    chosen = [[], []]
    for j in range(experts):
        named = ids == lax.rem(group + j, experts)
        weight = jnp.sum(jnp.where(named, weight_ref[...], 0.0), axis=0, keepdims=True)
        for side in range(2):
            block = jnp.where(slot == place[j : j + 1, :] + side * CAP, weight, 0.0)
            chosen[side] += [block] * each
    for side in range(2):
        scaled = jnp.concatenate(chosen[side], axis=0).T
        high = scaled.astype(BF16)
        out_ref[side, 0] = high
        out_ref[side, 1] = (scaled - high.astype(F32)).astype(BF16)


def combine_kernel(scaled_ref, *refs):
    piece_refs, (straight_ref, early_ref, out_ref, arrived_ref) = refs[:-6], refs[-6:-2]
    mixed_ref, sems = refs[-2:]
    half = out_ref.shape[1] // 2
    direct = lax.axis_index("expert") % GROUP % 3 == 0
    fill = pltpu.make_async_copy(straight_ref, arrived_ref, sems.at[2])

    @pl.when(direct)
    def _():
        fill.start()

    blank = jnp.zeros((STRIDE - PACK, half), F32)
    rows = []
    for ref in piece_refs:
        rows += [ref[...].astype(F32), blank]
    rows = jnp.concatenate(rows, axis=0).astype(BF16)
    copies = []
    for side in range(2):
        mixed = jnp.dot(scaled_ref[side, 0], rows, preferred_element_type=F32)
        mixed = mixed + jnp.dot(scaled_ref[side, 1], rows, preferred_element_type=F32)
        columns = pl.ds(side * half, half)
        mixed_ref[:, columns] = mixed.astype(BF16)
        copy = pltpu.make_async_copy(mixed_ref.at[:, columns], out_ref.at[:, columns], sems.at[side])
        copy.start()
        copies.append(copy)
    for copy in copies:
        copy.wait()

    @pl.when(direct)
    def _():
        fill.wait()


def on_device(tokens, expert_ids, combine, old_gate, old_up, old_down, move_plan):
    devices = lax.axis_size("expert")
    replicas = lax.axis_size("replica")
    experts = move_plan.shape[0]
    most = move_plan.shape[2]
    width = tokens.shape[1]
    plan = jnp.transpose(move_plan, (1, 0, 2))
    weights = (old_gate, old_up, old_down)
    half = most // 2

    def shape(*dims, dtype=BF16):
        return jax.ShapeDtypeStruct(dims, dtype)

    def send(block, j, k):
        route = []
        for i in range(devices):
            g, p = i // GROUP, i % GROUP
            route.append((i, GROUP * ((g + j) % experts) + (p ^ k)))
        return lax.ppermute(block, "expert", route)

    def migrate(block, survivor):
        route = [(GROUP * e + GROUP - 1, GROUP * e + survivor) for e in range(experts)]
        return lax.ppermute(block, "expert", route)

    def swap(block, survivor):
        route = []
        for r in range(replicas):
            for e in range(experts):
                i = GROUP * e + survivor
                route.append((i * replicas + r, i * replicas + (r ^ 1)))
        return lax.ppermute(block, ("expert", "replica"), route)

    def select(wanted, held):
        return pl.pallas_call(
            functools.partial(select_kernel, wanted),
            out_shape=[shape(3, count, width) for _, count, _ in wanted],
            in_specs=[VMEM] * 4,
            out_specs=[VMEM] * len(wanted),
            compiler_params=params(),
            cost_estimate=cost(2),
            name="select",
        )(plan, *held)

    begun = pl.pallas_call(
        begin_kernel,
        out_shape=shape(8, 128, dtype=F32),
        out_specs=VMEM,
        cost_estimate=cost(5),
        name="begin",
    )()
    ids, begun = lax.optimization_barrier((expert_ids.T, begun))
    parcels = pl.pallas_call(
        functools.partial(dispatch_kernel, experts),
        out_shape=[shape(PACK, width // 2)] * experts,
        in_specs=[VMEM, VMEM],
        out_specs=[VMEM] * experts,
        compiler_params=params(),
        cost_estimate=cost(2),
        name="dispatch",
    )(ids, tokens)

    pairs = [(j, k) for j in range(experts) for k in (0, 2)]
    held, _ = lax.optimization_barrier((weights, parcels))
    chosen = list(select([(1, half, None)], held))
    held, _ = lax.optimization_barrier((weights, chosen))
    chosen += select([(0, most, 0), (2, most, 0)], held)
    after, _ = lax.optimization_barrier((parcels, chosen[0]))
    mine = [parcels[0]]
    for j, k in pairs[1:]:
        mine.append(send(parcels[j] if k else after[j], j, k))
    shared = migrate(chosen[0], 1)
    straight = migrate(chosen[1], 0)
    mine = jnp.concatenate(mine, axis=0)
    other = send(mine, 0, 1)

    total = mine.shape[0]
    step = min(total, 4 * PACK)
    row_spec = pl.BlockSpec((step, width // 2), lambda i: (i, 0))
    whole_spec = pl.BlockSpec(old_gate.shape, lambda i: (0, 0))
    keep, give = pl.pallas_call(
        expert_kernel,
        grid=(total // step,),
        out_shape=[shape(total, width // 2, dtype=F32), shape(total, width // 2)],
        in_specs=[row_spec] * 2 + [whole_spec] * 3,
        out_specs=[row_spec] * 2,
        compiler_params=params(),
        cost_estimate=cost(0),
        name="expert",
    )(mine, other, *weights)
    taken, shared = lax.optimization_barrier((send(give, 0, 1), shared))
    summed = (keep + taken.astype(F32)).astype(BF16)
    pieces = [summed[n * PACK : (n + 1) * PACK] for n in range(len(pairs))]
    back = [pieces[0]] + [
        send(block, -j, k) for (j, k), block in zip(pairs[1:], pieces[1:])
    ]
    swapped = swap(shared, 1)
    swapped, near = lax.optimization_barrier((swapped, chosen[2]))
    near = migrate(near, 2)

    scaled = pl.pallas_call(
        functools.partial(weigh_kernel, experts),
        out_shape=shape(2, 2, tokens.shape[0], len(back) * STRIDE),
        in_specs=[VMEM, VMEM],
        out_specs=VMEM,
        compiler_params=params(),
        name="weigh",
    )(expert_ids.T, combine.T)
    swapped, scaled = lax.optimization_barrier((swapped, scaled))

    early = pl.pallas_call(
        early_kernel,
        out_shape=shape(3, most, width),
        in_specs=[HBM] * 2,
        out_specs=HBM,
        scratch_shapes=[pltpu.SemaphoreType.DMA((6,))],
        compiler_params=params(),
        name="early",
    )(shared, swapped)
    back, early, straight = lax.optimization_barrier((back, early, straight))

    mixed, filled = pl.pallas_call(
        combine_kernel,
        out_shape=[shape(tokens.shape[0], width), shape(3, most, width)],
        in_specs=[VMEM] * (len(back) + 1) + [HBM] * 2,
        out_specs=[HBM] * 2,
        input_output_aliases={len(back) + 2: 1},
        scratch_shapes=[
            pltpu.VMEM((tokens.shape[0], width), BF16),
            pltpu.SemaphoreType.DMA((3,)),
        ],
        compiler_params=params(),
        cost_estimate=cost(12.3),
        name="combine",
    )(scaled, *back, straight, early)

    arrived = pl.pallas_call(
        late_kernel,
        out_shape=shape(3, most, width),
        in_specs=[HBM] * 3,
        out_specs=HBM,
        input_output_aliases={0: 0},
        scratch_shapes=[pltpu.SemaphoreType.DMA((3,))],
        compiler_params=params(),
        name="late",
    )(filled, near, begun)
    return mixed, arrived


def solution(mesh):
    placed = (
        P(("replica", "expert"), None),
        P(("replica", "expert"), None),
        P(("replica", "expert"), None),
        P("expert", None),
        P("expert", None),
        P("expert", None),
        P(),
    )
    return jax.shard_map(
        on_device,
        mesh=mesh,
        in_specs=placed,
        out_specs=(P(("replica", "expert"), None), P("replica", "expert", None)),
        check_vma=False,
    )
```

```python
import functools

import jax
import jax.numpy as jnp
from jax import lax
from jax.experimental import pallas as pl
from jax.experimental.pallas import tpu as pltpu
from jax.sharding import PartitionSpec as P

CAP = 12
PACK = 2 * CAP
STRIDE = 32
GROUP = 4
BF16 = jnp.bfloat16
F32 = jnp.float32
VMEM = pl.BlockSpec(memory_space=pltpu.VMEM)
HBM = pl.BlockSpec(memory_space=pltpu.HBM)


def params(megabytes=16):
    return pltpu.CompilerParams(vmem_limit_bytes=megabytes * 1024 * 1024)


def cost(microseconds):
    return pl.CostEstimate(
        flops=int(microseconds * 10**9), bytes_accessed=10**4, transcendentals=0
    )


def token_places(ids, group, experts):
    tok = ids.shape[1]
    member = []
    for j in range(experts):
        named = jnp.where(ids == lax.rem(group + j, experts), 1.0, 0.0)
        member.append(jnp.sum(named, axis=0, keepdims=True))
    member = jnp.concatenate(member, axis=0)
    row = lax.broadcasted_iota(jnp.int32, (tok, tok), 0)
    col = lax.broadcasted_iota(jnp.int32, (tok, tok), 1)
    upto = jnp.where(row <= col, 1.0, 0.0).astype(BF16)
    rank = jnp.dot(member.astype(BF16), upto, preferred_element_type=F32)
    return jnp.where(member > 0, rank - 1.0, -PACK).astype(jnp.int32)


def dispatch_kernel(experts, ids_ref, tok_ref, *out_refs):
    group = lax.axis_index("expert") // GROUP
    place = token_places(ids_ref[...], group, experts)
    tok, half = tok_ref.shape[0], tok_ref.shape[1] // 2
    slot = lax.broadcasted_iota(jnp.int32, (PACK, tok), 0)
    for j, ref in enumerate(out_refs):
        spot = place[j : j + 1, :]
        left = jnp.where(jnp.logical_and(slot == spot, spot >= 0), 1.0, 0.0).astype(BF16)
        right = jnp.where(slot == spot + CAP, 1.0, 0.0).astype(BF16)
        rows = jnp.dot(left, tok_ref[:, :half], preferred_element_type=F32)
        rows = rows + jnp.dot(right, tok_ref[:, half:], preferred_element_type=F32)
        ref[...] = rows.astype(BF16)


def select_kernel(wanted, plan_ref, gate_ref, up_ref, down_ref, *out_refs):
    device = lax.axis_index("expert")
    even = lax.axis_index("replica") % 2 == 0
    rows = gate_ref.shape[0]

    @pl.when(device % GROUP == GROUP - 1)
    def _():
        plans = []
        for survivor, count, first in wanted:
            plan = plan_ref[survivor, pl.ds(device // GROUP, 1), :]
            if first is None:
                plan = jnp.where(even, plan[:, :count], plan[:, count : 2 * count])
            else:
                plan = plan[:, first : first + count]
            plans.append(plan)
        total = sum(count for _, count, _ in wanted)
        number = lax.broadcasted_iota(jnp.int32, (rows, total), 0)
        pick = jnp.where(number == jnp.concatenate(plans, axis=1), 1.0, 0.0).astype(BF16)
        for m, held_ref in enumerate((gate_ref, up_ref, down_ref)):
            found = lax.dot_general(
                pick, held_ref[...], (((0,), (0,)), ((), ())), preferred_element_type=F32
            ).astype(BF16)
            start = 0
            for (_, count, _), ref in zip(wanted, out_refs):
                ref[m] = found[start : start + count]
                start += count


def place_rows(pieces, out_ref, sems):
    copies = []
    for ref, first in pieces:
        for m in range(3):
            rows = pl.ds(first, ref.shape[1])
            copies.append(
                pltpu.make_async_copy(ref.at[m], out_ref.at[m, rows], sems.at[len(copies)])
            )
    for copy in copies:
        copy.start()
    for copy in copies:
        copy.wait()


def early_kernel(shared_ref, swapped_ref, out_ref, sems):
    position = lax.axis_index("expert") % GROUP
    parity = lax.axis_index("replica") % 2
    half = shared_ref.shape[1]
    for even in range(2):

        @pl.when(jnp.logical_and(position == 1, parity == even))
        def _():
            place_rows([(shared_ref, half * even), (swapped_ref, half * (1 - even))], out_ref, sems)


def late_kernel(filled_ref, near_ref, begun_ref, out_ref, sems):
    @pl.when(lax.axis_index("expert") % GROUP == 2)
    def _():
        place_rows([(near_ref, 0)], out_ref, sems)


def begin_kernel(out_ref):
    out_ref[...] = jnp.zeros_like(out_ref)


def expert_kernel(mine_ref, other_ref, gate_ref, up_ref, down_ref, keep_ref, give_ref):
    rows, half = mine_ref.shape
    x = jnp.concatenate([mine_ref[...], other_ref[...]], axis=0)
    total = x.shape[0]
    numbers = (((1,), (1,)), ((), ()))

    def project(ref):
        left = lax.dot_general(x, ref[:, :half], numbers, preferred_element_type=F32)
        right = lax.dot_general(x, ref[:, half:], numbers, preferred_element_type=F32)
        return left + jnp.concatenate([right[CAP:], right[:CAP]], axis=0)

    gate_value = project(gate_ref)
    up_value = project(up_ref)
    hidden = (gate_value / (1.0 + jnp.exp(-gate_value)) * up_value).astype(BF16)
    left = jnp.dot(hidden, down_ref[:, :half], preferred_element_type=F32)
    right = jnp.dot(hidden, down_ref[:, half:], preferred_element_type=F32)
    right = jnp.concatenate([right[total - CAP :], right[: total - CAP]], axis=0)
    row = lax.broadcasted_iota(jnp.int32, (total, half), 0)
    partial = jnp.where(row % PACK < CAP, left, right)
    keep_ref[...] = partial[:rows]
    give_ref[...] = partial[rows:].astype(BF16)


def weigh_kernel(experts, ids_ref, weight_ref, out_ref):
    ids = ids_ref[...]
    group = lax.axis_index("expert") // GROUP
    place = token_places(ids, group, experts)
    each = out_ref.shape[2] // 2 // STRIDE // experts
    slot = lax.broadcasted_iota(jnp.int32, (STRIDE, ids.shape[1]), 0)
    chosen = [[], []]
    for j in range(experts):
        named = ids == lax.rem(group + j, experts)
        weight = jnp.sum(jnp.where(named, weight_ref[...], 0.0), axis=0, keepdims=True)
        for side in range(2):
            block = jnp.where(slot == place[j : j + 1, :] + side * CAP, weight, 0.0)
            chosen[side] += [block] * each
    for side in range(2):
        scaled = jnp.concatenate(chosen[side], axis=0).T
        high = scaled.astype(BF16)
        low = (scaled - high.astype(F32)).astype(BF16)
        out_ref[side] = jnp.concatenate([high, low], axis=1)


def combine_kernel(scaled_ref, *refs):
    piece_refs, (straight_ref, early_ref, out_ref, arrived_ref) = refs[:-6], refs[-6:-2]
    mixed_ref, sems = refs[-2:]
    half = out_ref.shape[1] // 2
    direct = lax.axis_index("expert") % GROUP % 3 == 0
    fills = [
        pltpu.make_async_copy(straight_ref.at[m], arrived_ref.at[m], sems.at[2 + m])
        for m in range(3)
    ]

    @pl.when(direct)
    def _():
        for fill in fills:
            fill.start()

    blank = jnp.zeros((STRIDE - PACK, half), F32)
    rows = []
    for ref in piece_refs:
        rows += [ref[...].astype(F32), blank]
    rows = jnp.concatenate(rows, axis=0).astype(BF16)
    rows = jnp.concatenate([rows, rows], axis=0)
    copies = []
    for side in range(2):
        mixed = jnp.dot(scaled_ref[side], rows, preferred_element_type=F32)
        columns = pl.ds(side * half, half)
        mixed_ref[:, columns] = mixed.astype(BF16)
        copy = pltpu.make_async_copy(mixed_ref.at[:, columns], out_ref.at[:, columns], sems.at[side])
        copy.start()
        copies.append(copy)
    for copy in copies:
        copy.wait()

    @pl.when(direct)
    def _():
        for fill in fills:
            fill.wait()


def on_device(tokens, expert_ids, combine, old_gate, old_up, old_down, move_plan):
    devices = lax.axis_size("expert")
    replicas = lax.axis_size("replica")
    experts = move_plan.shape[0]
    most = move_plan.shape[2]
    width = tokens.shape[1]
    plan = jnp.transpose(move_plan, (1, 0, 2))
    weights = (old_gate, old_up, old_down)
    half = most // 2

    def shape(*dims, dtype=BF16):
        return jax.ShapeDtypeStruct(dims, dtype)

    def send(block, j, k):
        route = []
        for i in range(devices):
            g, p = i // GROUP, i % GROUP
            route.append((i, GROUP * ((g + j) % experts) + (p ^ k)))
        return lax.ppermute(block, "expert", route)

    def migrate(block, survivor):
        route = [(GROUP * e + GROUP - 1, GROUP * e + survivor) for e in range(experts)]
        return lax.ppermute(block, "expert", route)

    def swap(block, survivor):
        route = []
        for r in range(replicas):
            for e in range(experts):
                i = GROUP * e + survivor
                route.append((i * replicas + r, i * replicas + (r ^ 1)))
        return lax.ppermute(block, ("expert", "replica"), route)

    def select(wanted, held):
        return pl.pallas_call(
            functools.partial(select_kernel, wanted),
            out_shape=[shape(3, count, width) for _, count, _ in wanted],
            in_specs=[VMEM] * 4,
            out_specs=[VMEM] * len(wanted),
            compiler_params=params(),
            cost_estimate=cost(2),
            name="select",
        )(plan, *held)

    begun = pl.pallas_call(
        begin_kernel,
        out_shape=shape(8, 128, dtype=F32),
        out_specs=VMEM,
        cost_estimate=cost(5),
        name="begin",
    )()
    ids, begun = lax.optimization_barrier((expert_ids.T, begun))
    parcels = pl.pallas_call(
        functools.partial(dispatch_kernel, experts),
        out_shape=[shape(PACK, width // 2)] * experts,
        in_specs=[VMEM, VMEM],
        out_specs=[VMEM] * experts,
        compiler_params=params(),
        cost_estimate=cost(2),
        name="dispatch",
    )(ids, tokens)

    pairs = [(j, k) for j in range(experts) for k in (0, 2)]
    held, _ = lax.optimization_barrier((weights, parcels))
    chosen = list(select([(1, half, None)], held))
    held, _ = lax.optimization_barrier((weights, chosen))
    chosen += select([(0, most, 0), (2, most, 0)], held)
    after, _ = lax.optimization_barrier((parcels, chosen[0]))
    mine = [parcels[0]]
    for j, k in pairs[1:]:
        mine.append(send(parcels[j] if k else after[j], j, k))
    shared = migrate(chosen[0], 1)
    straight = migrate(chosen[1], 0)
    mine = jnp.concatenate(mine, axis=0)
    other = send(mine, 0, 1)

    total = mine.shape[0]
    step = min(total, 4 * PACK)
    row_spec = pl.BlockSpec((step, width // 2), lambda i: (i, 0))
    whole_spec = pl.BlockSpec(old_gate.shape, lambda i: (0, 0))
    keep, give = pl.pallas_call(
        expert_kernel,
        grid=(total // step,),
        out_shape=[shape(total, width // 2, dtype=F32), shape(total, width // 2)],
        in_specs=[row_spec] * 2 + [whole_spec] * 3,
        out_specs=[row_spec] * 2,
        compiler_params=params(),
        cost_estimate=cost(0),
        name="expert",
    )(mine, other, *weights)
    taken, shared = lax.optimization_barrier((send(give, 0, 1), shared))
    summed = (keep + taken.astype(F32)).astype(BF16)
    pieces = [summed[n * PACK : (n + 1) * PACK] for n in range(len(pairs))]
    back = [pieces[0]] + [
        send(block, -j, k) for (j, k), block in zip(pairs[1:], pieces[1:])
    ]
    swapped = swap(shared, 1)
    swapped, near = lax.optimization_barrier((swapped, chosen[2]))
    near = migrate(near, 2)

    scaled = pl.pallas_call(
        functools.partial(weigh_kernel, experts),
        out_shape=shape(2, tokens.shape[0], 2 * len(back) * STRIDE),
        in_specs=[VMEM, VMEM],
        out_specs=VMEM,
        compiler_params=params(),
        name="weigh",
    )(expert_ids.T, combine.T)
    swapped, scaled = lax.optimization_barrier((swapped, scaled))

    early = pl.pallas_call(
        early_kernel,
        out_shape=shape(3, most, width),
        in_specs=[HBM] * 2,
        out_specs=HBM,
        scratch_shapes=[pltpu.SemaphoreType.DMA((6,))],
        compiler_params=params(),
        name="early",
    )(shared, swapped)
    back, early, straight = lax.optimization_barrier((back, early, straight))

    mixed, filled = pl.pallas_call(
        combine_kernel,
        out_shape=[shape(tokens.shape[0], width), shape(3, most, width)],
        in_specs=[VMEM] * (len(back) + 1) + [HBM] * 2,
        out_specs=[HBM] * 2,
        input_output_aliases={len(back) + 2: 1},
        scratch_shapes=[
            pltpu.VMEM((tokens.shape[0], width), BF16),
            pltpu.SemaphoreType.DMA((5,)),
        ],
        compiler_params=params(),
        cost_estimate=cost(12.3),
        name="combine",
    )(scaled, *back, straight, early)

    arrived = pl.pallas_call(
        late_kernel,
        out_shape=shape(3, most, width),
        in_specs=[HBM] * 3,
        out_specs=HBM,
        input_output_aliases={0: 0},
        scratch_shapes=[pltpu.SemaphoreType.DMA((3,))],
        compiler_params=params(),
        name="late",
    )(filled, near, begun)
    return mixed, arrived


def solution(mesh):
    placed = (
        P(("replica", "expert"), None),
        P(("replica", "expert"), None),
        P(("replica", "expert"), None),
        P("expert", None),
        P("expert", None),
        P("expert", None),
        P(),
    )
    return jax.shard_map(
        on_device,
        mesh=mesh,
        in_specs=placed,
        out_specs=(P(("replica", "expert"), None), P("replica", "expert", None)),
        check_vma=False,
    )
```

```python
import functools

import jax
import jax.numpy as jnp
from jax import lax
from jax.experimental import pallas as pl
from jax.experimental.pallas import tpu as pltpu
from jax.sharding import PartitionSpec as P

CAP = 12
PACK = 2 * CAP
STRIDE = 32
GROUP = 4
BF16 = jnp.bfloat16
F32 = jnp.float32
VMEM = pl.BlockSpec(memory_space=pltpu.VMEM)
HBM = pl.BlockSpec(memory_space=pltpu.HBM)


def params(megabytes=16):
    return pltpu.CompilerParams(vmem_limit_bytes=megabytes * 1024 * 1024)


def cost(microseconds):
    return pl.CostEstimate(
        flops=int(microseconds * 10**9), bytes_accessed=10**4, transcendentals=0
    )


def token_places(ids, group, experts):
    tok = ids.shape[1]
    member = []
    for j in range(experts):
        named = jnp.where(ids == lax.rem(group + j, experts), 1.0, 0.0)
        member.append(jnp.sum(named, axis=0, keepdims=True))
    member = jnp.concatenate(member, axis=0)
    row = lax.broadcasted_iota(jnp.int32, (tok, tok), 0)
    col = lax.broadcasted_iota(jnp.int32, (tok, tok), 1)
    upto = jnp.where(row <= col, 1.0, 0.0).astype(BF16)
    rank = jnp.dot(member.astype(BF16), upto, preferred_element_type=F32)
    return jnp.where(member > 0, rank - 1.0, -PACK).astype(jnp.int32)


def dispatch_kernel(experts, ids_ref, tok_ref, *out_refs):
    group = lax.axis_index("expert") // GROUP
    place = token_places(ids_ref[...], group, experts)
    tok, half = tok_ref.shape[0], tok_ref.shape[1] // 2
    slot = lax.broadcasted_iota(jnp.int32, (PACK, tok), 0)
    for j, ref in enumerate(out_refs):
        spot = place[j : j + 1, :]
        left = jnp.where(jnp.logical_and(slot == spot, spot >= 0), 1.0, 0.0).astype(BF16)
        right = jnp.where(slot == spot + CAP, 1.0, 0.0).astype(BF16)
        rows = jnp.dot(left, tok_ref[:, :half], preferred_element_type=F32)
        rows = rows + jnp.dot(right, tok_ref[:, half:], preferred_element_type=F32)
        ref[...] = rows.astype(BF16)


def select_kernel(wanted, plan_ref, gate_ref, up_ref, down_ref, *out_refs):
    device = lax.axis_index("expert")
    even = lax.axis_index("replica") % 2 == 0
    rows = gate_ref.shape[0]

    @pl.when(device % GROUP == GROUP - 1)
    def _():
        plans = []
        for survivor, count, first in wanted:
            plan = plan_ref[survivor, pl.ds(device // GROUP, 1), :]
            if first is None:
                plan = jnp.where(even, plan[:, :count], plan[:, count : 2 * count])
            else:
                plan = plan[:, first : first + count]
            plans.append(plan)
        total = sum(count for _, count, _ in wanted)
        number = lax.broadcasted_iota(jnp.int32, (rows, total), 0)
        pick = jnp.where(number == jnp.concatenate(plans, axis=1), 1.0, 0.0).astype(BF16)
        for m, held_ref in enumerate((gate_ref, up_ref, down_ref)):
            found = lax.dot_general(
                pick, held_ref[...], (((0,), (0,)), ((), ())), preferred_element_type=F32
            ).astype(BF16)
            start = 0
            for (_, count, _), ref in zip(wanted, out_refs):
                ref[m] = found[start : start + count]
                start += count


def place_rows(pieces, out_ref, sems):
    copies = []
    for ref, first in pieces:
        for m in range(3):
            rows = pl.ds(first, ref.shape[1])
            copies.append(
                pltpu.make_async_copy(ref.at[m], out_ref.at[m, rows], sems.at[len(copies)])
            )
    for copy in copies:
        copy.start()
    for copy in copies:
        copy.wait()


def early_kernel(shared_ref, swapped_ref, out_ref, sems):
    position = lax.axis_index("expert") % GROUP
    parity = lax.axis_index("replica") % 2
    half = shared_ref.shape[1]
    for even in range(2):

        @pl.when(jnp.logical_and(position == 1, parity == even))
        def _():
            place_rows([(shared_ref, half * even), (swapped_ref, half * (1 - even))], out_ref, sems)


def late_kernel(filled_ref, near_ref, begun_ref, out_ref, sems):
    @pl.when(lax.axis_index("expert") % GROUP == 2)
    def _():
        place_rows([(near_ref, 0)], out_ref, sems)


def begin_kernel(out_ref):
    out_ref[...] = jnp.zeros_like(out_ref)


def expert_kernel(mine_ref, other_ref, gate_ref, up_ref, down_ref, keep_ref, give_ref):
    rows, half = mine_ref.shape
    x = jnp.concatenate([mine_ref[...], other_ref[...]], axis=0)
    total = x.shape[0]
    numbers = (((1,), (1,)), ((), ()))

    def project(ref):
        left = lax.dot_general(x, ref[:, :half], numbers, preferred_element_type=F32)
        right = lax.dot_general(x, ref[:, half:], numbers, preferred_element_type=F32)
        return left + jnp.concatenate([right[CAP:], right[:CAP]], axis=0)

    gate_value = project(gate_ref)
    up_value = project(up_ref)
    hidden = (gate_value / (1.0 + jnp.exp(-gate_value)) * up_value).astype(BF16)
    left = jnp.dot(hidden, down_ref[:, :half], preferred_element_type=F32)
    right = jnp.dot(hidden, down_ref[:, half:], preferred_element_type=F32)
    right = jnp.concatenate([right[total - CAP :], right[: total - CAP]], axis=0)
    row = lax.broadcasted_iota(jnp.int32, (total, half), 0)
    partial = jnp.where(row % PACK < CAP, left, right)
    keep_ref[...] = partial[:rows]
    give_ref[...] = partial[rows:].astype(BF16)


def weigh_kernel(experts, ids_ref, weight_ref, out_ref):
    ids = ids_ref[...]
    group = lax.axis_index("expert") // GROUP
    place = token_places(ids, group, experts)
    each = out_ref.shape[2] // 2 // STRIDE // experts
    slot = lax.broadcasted_iota(jnp.int32, (STRIDE, ids.shape[1]), 0)
    chosen = [[], []]
    for j in range(experts):
        named = ids == lax.rem(group + j, experts)
        weight = jnp.sum(jnp.where(named, weight_ref[...], 0.0), axis=0, keepdims=True)
        for side in range(2):
            block = jnp.where(slot == place[j : j + 1, :] + side * CAP, weight, 0.0)
            chosen[side] += [block] * each
    for side in range(2):
        scaled = jnp.concatenate(chosen[side], axis=0).T
        high = scaled.astype(BF16)
        low = (scaled - high.astype(F32)).astype(BF16)
        out_ref[side] = jnp.concatenate([high, low], axis=1)


def combine_kernel(scaled_ref, *refs):
    piece_refs, (straight_ref, early_ref, out_ref, arrived_ref) = refs[:-6], refs[-6:-2]
    mixed_ref, sems = refs[-2:]
    half = out_ref.shape[1] // 2
    direct = lax.axis_index("expert") % GROUP % 3 == 0
    fills = [
        pltpu.make_async_copy(straight_ref.at[m], arrived_ref.at[m], sems.at[2 + m])
        for m in range(3)
    ]

    @pl.when(direct)
    def _():
        for fill in fills:
            fill.start()

    blank = jnp.zeros((STRIDE - PACK, half), F32)
    rows = []
    for ref in piece_refs:
        rows += [ref[...].astype(F32), blank]
    rows = jnp.concatenate(rows, axis=0).astype(BF16)
    rows = jnp.concatenate([rows, rows], axis=0)
    copies = []
    tok = out_ref.shape[0] // 2
    for n in range(2):
        span = pl.ds(n * tok, tok)
        for side in range(2):
            mixed = jnp.dot(scaled_ref[side, span], rows, preferred_element_type=F32)
            mixed_ref[span, side * half : (side + 1) * half] = mixed.astype(BF16)
        copy = pltpu.make_async_copy(mixed_ref.at[span], out_ref.at[span], sems.at[n])
        copy.start()
        copies.append(copy)
    for copy in copies:
        copy.wait()

    @pl.when(direct)
    def _():
        for fill in fills:
            fill.wait()


def on_device(tokens, expert_ids, combine, old_gate, old_up, old_down, move_plan):
    devices = lax.axis_size("expert")
    replicas = lax.axis_size("replica")
    experts = move_plan.shape[0]
    most = move_plan.shape[2]
    width = tokens.shape[1]
    plan = jnp.transpose(move_plan, (1, 0, 2))
    weights = (old_gate, old_up, old_down)
    half = most // 2

    def shape(*dims, dtype=BF16):
        return jax.ShapeDtypeStruct(dims, dtype)

    def send(block, j, k):
        route = []
        for i in range(devices):
            g, p = i // GROUP, i % GROUP
            route.append((i, GROUP * ((g + j) % experts) + (p ^ k)))
        return lax.ppermute(block, "expert", route)

    def migrate(block, survivor):
        route = [(GROUP * e + GROUP - 1, GROUP * e + survivor) for e in range(experts)]
        return lax.ppermute(block, "expert", route)

    def swap(block, survivor):
        route = []
        for r in range(replicas):
            for e in range(experts):
                i = GROUP * e + survivor
                route.append((i * replicas + r, i * replicas + (r ^ 1)))
        return lax.ppermute(block, ("expert", "replica"), route)

    def select(wanted, held):
        return pl.pallas_call(
            functools.partial(select_kernel, wanted),
            out_shape=[shape(3, count, width) for _, count, _ in wanted],
            in_specs=[VMEM] * 4,
            out_specs=[VMEM] * len(wanted),
            compiler_params=params(),
            cost_estimate=cost(2),
            name="select",
        )(plan, *held)

    begun = pl.pallas_call(
        begin_kernel,
        out_shape=shape(8, 128, dtype=F32),
        out_specs=VMEM,
        cost_estimate=cost(5),
        name="begin",
    )()
    ids, begun = lax.optimization_barrier((expert_ids.T, begun))
    parcels = pl.pallas_call(
        functools.partial(dispatch_kernel, experts),
        out_shape=[shape(PACK, width // 2)] * experts,
        in_specs=[VMEM, VMEM],
        out_specs=[VMEM] * experts,
        compiler_params=params(),
        cost_estimate=cost(2),
        name="dispatch",
    )(ids, tokens)

    pairs = [(j, k) for j in range(experts) for k in (0, 2)]
    held, _ = lax.optimization_barrier((weights, parcels))
    chosen = list(select([(1, half, None)], held))
    held, _ = lax.optimization_barrier((weights, chosen))
    chosen += select([(0, most, 0), (2, most, 0)], held)
    after, _ = lax.optimization_barrier((parcels, chosen[0]))
    mine = [parcels[0]]
    for j, k in pairs[1:]:
        mine.append(send(parcels[j] if k else after[j], j, k))
    shared = migrate(chosen[0], 1)
    straight = migrate(chosen[1], 0)
    mine = jnp.concatenate(mine, axis=0)
    other = send(mine, 0, 1)

    total = mine.shape[0]
    step = min(total, 4 * PACK)
    row_spec = pl.BlockSpec((step, width // 2), lambda i: (i, 0))
    whole_spec = pl.BlockSpec(old_gate.shape, lambda i: (0, 0))
    keep, give = pl.pallas_call(
        expert_kernel,
        grid=(total // step,),
        out_shape=[shape(total, width // 2, dtype=F32), shape(total, width // 2)],
        in_specs=[row_spec] * 2 + [whole_spec] * 3,
        out_specs=[row_spec] * 2,
        compiler_params=params(),
        cost_estimate=cost(0),
        name="expert",
    )(mine, other, *weights)
    taken, shared = lax.optimization_barrier((send(give, 0, 1), shared))
    summed = (keep + taken.astype(F32)).astype(BF16)
    pieces = [summed[n * PACK : (n + 1) * PACK] for n in range(len(pairs))]
    back = [pieces[0]] + [
        send(block, -j, k) for (j, k), block in zip(pairs[1:], pieces[1:])
    ]
    swapped = swap(shared, 1)
    swapped, near = lax.optimization_barrier((swapped, chosen[2]))
    near = migrate(near, 2)

    scaled = pl.pallas_call(
        functools.partial(weigh_kernel, experts),
        out_shape=shape(2, tokens.shape[0], 2 * len(back) * STRIDE),
        in_specs=[VMEM, VMEM],
        out_specs=VMEM,
        compiler_params=params(),
        name="weigh",
    )(expert_ids.T, combine.T)
    swapped, scaled = lax.optimization_barrier((swapped, scaled))

    early = pl.pallas_call(
        early_kernel,
        out_shape=shape(3, most, width),
        in_specs=[HBM] * 2,
        out_specs=HBM,
        scratch_shapes=[pltpu.SemaphoreType.DMA((6,))],
        compiler_params=params(),
        name="early",
    )(shared, swapped)
    back, early, straight = lax.optimization_barrier((back, early, straight))

    mixed, filled = pl.pallas_call(
        combine_kernel,
        out_shape=[shape(tokens.shape[0], width), shape(3, most, width)],
        in_specs=[VMEM] * (len(back) + 1) + [HBM] * 2,
        out_specs=[HBM] * 2,
        input_output_aliases={len(back) + 2: 1},
        scratch_shapes=[
            pltpu.VMEM((tokens.shape[0], width), BF16),
            pltpu.SemaphoreType.DMA((5,)),
        ],
        compiler_params=params(),
        cost_estimate=cost(12.3),
        name="combine",
    )(scaled, *back, straight, early)

    arrived = pl.pallas_call(
        late_kernel,
        out_shape=shape(3, most, width),
        in_specs=[HBM] * 3,
        out_specs=HBM,
        input_output_aliases={0: 0},
        scratch_shapes=[pltpu.SemaphoreType.DMA((3,))],
        compiler_params=params(),
        name="late",
    )(filled, near, begun)
    return mixed, arrived


def solution(mesh):
    placed = (
        P(("replica", "expert"), None),
        P(("replica", "expert"), None),
        P(("replica", "expert"), None),
        P("expert", None),
        P("expert", None),
        P("expert", None),
        P(),
    )
    return jax.shard_map(
        on_device,
        mesh=mesh,
        in_specs=placed,
        out_specs=(P(("replica", "expert"), None), P("replica", "expert", None)),
        check_vma=False,
    )
```

```python
import functools

import jax
import jax.numpy as jnp
from jax import lax
from jax.experimental import pallas as pl
from jax.experimental.pallas import tpu as pltpu
from jax.sharding import PartitionSpec as P

CAP = 12
PACK = 2 * CAP
STRIDE = 32
GROUP = 4
BF16 = jnp.bfloat16
F32 = jnp.float32
VMEM = pl.BlockSpec(memory_space=pltpu.VMEM)
HBM = pl.BlockSpec(memory_space=pltpu.HBM)


def params(megabytes=16):
    return pltpu.CompilerParams(vmem_limit_bytes=megabytes * 1024 * 1024)


def cost(microseconds):
    return pl.CostEstimate(
        flops=int(microseconds * 10**9), bytes_accessed=10**4, transcendentals=0
    )


def token_places(ids, group, experts):
    tok = ids.shape[1]
    member = []
    for j in range(experts):
        named = jnp.where(ids == lax.rem(group + j, experts), 1.0, 0.0)
        member.append(jnp.sum(named, axis=0, keepdims=True))
    member = jnp.concatenate(member, axis=0)
    row = lax.broadcasted_iota(jnp.int32, (tok, tok), 0)
    col = lax.broadcasted_iota(jnp.int32, (tok, tok), 1)
    upto = jnp.where(row <= col, 1.0, 0.0).astype(BF16)
    rank = jnp.dot(member.astype(BF16), upto, preferred_element_type=F32)
    return jnp.where(member > 0, rank - 1.0, -PACK).astype(jnp.int32)


def dispatch_kernel(experts, ids_ref, tok_ref, *out_refs):
    group = lax.axis_index("expert") // GROUP
    place = token_places(ids_ref[...], group, experts)
    tok, half = tok_ref.shape[0], tok_ref.shape[1] // 2
    slot = lax.broadcasted_iota(jnp.int32, (PACK, tok), 0)
    for j, ref in enumerate(out_refs):
        spot = place[j : j + 1, :]
        left = jnp.where(jnp.logical_and(slot == spot, spot >= 0), 1.0, 0.0).astype(BF16)
        right = jnp.where(slot == spot + CAP, 1.0, 0.0).astype(BF16)
        rows = jnp.dot(left, tok_ref[:, :half], preferred_element_type=F32)
        rows = rows + jnp.dot(right, tok_ref[:, half:], preferred_element_type=F32)
        ref[...] = rows.astype(BF16)


def select_kernel(wanted, plan_ref, gate_ref, up_ref, down_ref, *out_refs):
    device = lax.axis_index("expert")
    even = lax.axis_index("replica") % 2 == 0
    rows = gate_ref.shape[0]

    @pl.when(device % GROUP == GROUP - 1)
    def _():
        plans = []
        for survivor, count, first in wanted:
            plan = plan_ref[survivor, pl.ds(device // GROUP, 1), :]
            if first is None:
                plan = jnp.where(even, plan[:, :count], plan[:, count : 2 * count])
            else:
                plan = plan[:, first : first + count]
            plans.append(plan)
        total = sum(count for _, count, _ in wanted)
        number = lax.broadcasted_iota(jnp.int32, (rows, total), 0)
        pick = jnp.where(number == jnp.concatenate(plans, axis=1), 1.0, 0.0).astype(BF16)
        for m, held_ref in enumerate((gate_ref, up_ref, down_ref)):
            found = lax.dot_general(
                pick, held_ref[...], (((0,), (0,)), ((), ())), preferred_element_type=F32
            ).astype(BF16)
            start = 0
            for (_, count, _), ref in zip(wanted, out_refs):
                ref[m] = found[start : start + count]
                start += count


def place_rows(pieces, out_ref, sems):
    copies = []
    for ref, first in pieces:
        for m in range(3):
            rows = pl.ds(first, ref.shape[1])
            copies.append(
                pltpu.make_async_copy(ref.at[m], out_ref.at[m, rows], sems.at[len(copies)])
            )
    for copy in copies:
        copy.start()
    for copy in copies:
        copy.wait()


def early_kernel(shared_ref, swapped_ref, out_ref, sems):
    position = lax.axis_index("expert") % GROUP
    parity = lax.axis_index("replica") % 2
    half = shared_ref.shape[1]
    for even in range(2):

        @pl.when(jnp.logical_and(position == 1, parity == even))
        def _():
            place_rows([(shared_ref, half * even), (swapped_ref, half * (1 - even))], out_ref, sems)


def late_kernel(filled_ref, near_ref, begun_ref, out_ref, sems):
    @pl.when(lax.axis_index("expert") % GROUP == 2)
    def _():
        place_rows([(near_ref, 0)], out_ref, sems)


def begin_kernel(out_ref):
    out_ref[...] = jnp.zeros_like(out_ref)


def expert_kernel(mine_ref, other_ref, gate_ref, up_ref, down_ref, keep_ref, give_ref):
    rows, half = mine_ref.shape
    x = jnp.concatenate([mine_ref[...], other_ref[...]], axis=0)
    total = x.shape[0]
    numbers = (((1,), (1,)), ((), ()))

    def project(ref):
        left = lax.dot_general(x, ref[:, :half], numbers, preferred_element_type=F32)
        right = lax.dot_general(x, ref[:, half:], numbers, preferred_element_type=F32)
        return left + jnp.concatenate([right[CAP:], right[:CAP]], axis=0)

    gate_value = project(gate_ref)
    up_value = project(up_ref)
    hidden = (gate_value / (1.0 + jnp.exp(-gate_value)) * up_value).astype(BF16)
    left = jnp.dot(hidden, down_ref[:, :half], preferred_element_type=F32)
    right = jnp.dot(hidden, down_ref[:, half:], preferred_element_type=F32)
    right = jnp.concatenate([right[total - CAP :], right[: total - CAP]], axis=0)
    row = lax.broadcasted_iota(jnp.int32, (total, half), 0)
    partial = jnp.where(row % PACK < CAP, left, right)
    keep_ref[...] = partial[:rows]
    give_ref[...] = partial[rows:].astype(BF16)


def weigh_kernel(experts, ids_ref, weight_ref, out_ref):
    ids = ids_ref[...]
    group = lax.axis_index("expert") // GROUP
    place = token_places(ids, group, experts)
    each = out_ref.shape[2] // 2 // STRIDE // experts
    slot = lax.broadcasted_iota(jnp.int32, (STRIDE, ids.shape[1]), 0)
    chosen = [[], []]
    for j in range(experts):
        named = ids == lax.rem(group + j, experts)
        weight = jnp.sum(jnp.where(named, weight_ref[...], 0.0), axis=0, keepdims=True)
        for side in range(2):
            block = jnp.where(slot == place[j : j + 1, :] + side * CAP, weight, 0.0)
            chosen[side] += [block] * each
    for side in range(2):
        scaled = jnp.concatenate(chosen[side], axis=0).T
        high = scaled.astype(BF16)
        low = (scaled - high.astype(F32)).astype(BF16)
        out_ref[side] = jnp.concatenate([high, low], axis=1)


def combine_kernel(scaled_ref, *refs):
    piece_refs, (straight_ref, early_ref, out_ref, arrived_ref) = refs[:-6], refs[-6:-2]
    mixed_ref, sems = refs[-2:]
    half = out_ref.shape[1] // 2
    direct = lax.axis_index("expert") % GROUP % 3 == 0
    fills = [
        pltpu.make_async_copy(straight_ref.at[m], arrived_ref.at[m], sems.at[2 + m])
        for m in range(3)
    ]

    @pl.when(direct)
    def _():
        for fill in fills:
            fill.start()

    blank = jnp.zeros((STRIDE - PACK, half), F32)
    rows = []
    for ref in piece_refs:
        rows += [ref[...].astype(F32), blank]
    rows = jnp.concatenate(rows, axis=0).astype(BF16)
    rows = jnp.concatenate([rows, rows], axis=0)
    copies = []
    for side in range(2):
        mixed = jnp.dot(scaled_ref[side], rows, preferred_element_type=F32)
        columns = pl.ds(side * half, half)
        mixed_ref[:, columns] = mixed.astype(BF16)
        copy = pltpu.make_async_copy(mixed_ref.at[:, columns], out_ref.at[:, columns], sems.at[side])
        copy.start()
        copies.append(copy)
    for copy in copies:
        copy.wait()

    @pl.when(direct)
    def _():
        for fill in fills:
            fill.wait()


def on_device(tokens, expert_ids, combine, old_gate, old_up, old_down, move_plan):
    devices = lax.axis_size("expert")
    replicas = lax.axis_size("replica")
    experts = move_plan.shape[0]
    most = move_plan.shape[2]
    width = tokens.shape[1]
    plan = jnp.transpose(move_plan, (1, 0, 2))
    weights = (old_gate, old_up, old_down)
    half = most // 2

    def shape(*dims, dtype=BF16):
        return jax.ShapeDtypeStruct(dims, dtype)

    def send(block, j, k):
        route = []
        for i in range(devices):
            g, p = i // GROUP, i % GROUP
            route.append((i, GROUP * ((g + j) % experts) + (p ^ k)))
        return lax.ppermute(block, "expert", route)

    def migrate(block, survivor):
        route = [(GROUP * e + GROUP - 1, GROUP * e + survivor) for e in range(experts)]
        return lax.ppermute(block, "expert", route)

    def swap(block, survivor):
        route = []
        for r in range(replicas):
            for e in range(experts):
                i = GROUP * e + survivor
                route.append((i * replicas + r, i * replicas + (r ^ 1)))
        return lax.ppermute(block, ("expert", "replica"), route)

    def select(wanted, held):
        return pl.pallas_call(
            functools.partial(select_kernel, wanted),
            out_shape=[shape(3, count, width) for _, count, _ in wanted],
            in_specs=[VMEM] * 4,
            out_specs=[VMEM] * len(wanted),
            compiler_params=params(),
            cost_estimate=cost(2),
            name="select",
        )(plan, *held)

    begun = pl.pallas_call(
        begin_kernel,
        out_shape=shape(8, 128, dtype=F32),
        out_specs=VMEM,
        cost_estimate=cost(5),
        name="begin",
    )()
    ids, begun = lax.optimization_barrier((expert_ids.T, begun))
    parcels = pl.pallas_call(
        functools.partial(dispatch_kernel, experts),
        out_shape=[shape(PACK, width // 2)] * experts,
        in_specs=[VMEM, VMEM],
        out_specs=[VMEM] * experts,
        compiler_params=params(),
        cost_estimate=cost(2),
        name="dispatch",
    )(ids, tokens)

    pairs = [(j, k) for j in range(experts) for k in (0, 2)]
    held, _ = lax.optimization_barrier((weights, parcels))
    chosen = list(select([(1, half, None)], held))
    held, _ = lax.optimization_barrier((weights, chosen))
    chosen += select([(0, most, 0), (2, most, 0)], held)
    after, _ = lax.optimization_barrier((parcels, chosen[0]))
    mine = [parcels[0]]
    for j, k in pairs[1:]:
        mine.append(send(after[j] if j else parcels[j], j, k))
    shared = migrate(chosen[0], 1)
    straight = migrate(chosen[1], 0)
    mine = jnp.concatenate(mine, axis=0)
    other = send(mine, 0, 1)

    total = mine.shape[0]
    step = min(total, 4 * PACK)
    row_spec = pl.BlockSpec((step, width // 2), lambda i: (i, 0))
    whole_spec = pl.BlockSpec(old_gate.shape, lambda i: (0, 0))
    keep, give = pl.pallas_call(
        expert_kernel,
        grid=(total // step,),
        out_shape=[shape(total, width // 2, dtype=F32), shape(total, width // 2)],
        in_specs=[row_spec] * 2 + [whole_spec] * 3,
        out_specs=[row_spec] * 2,
        compiler_params=params(),
        cost_estimate=cost(0),
        name="expert",
    )(mine, other, *weights)
    taken, shared = lax.optimization_barrier((send(give, 0, 1), shared))
    summed = (keep + taken.astype(F32)).astype(BF16)
    pieces = [summed[n * PACK : (n + 1) * PACK] for n in range(len(pairs))]
    back = [pieces[0]] + [
        send(block, -j, k) for (j, k), block in zip(pairs[1:], pieces[1:])
    ]
    swapped = swap(shared, 1)
    swapped, near = lax.optimization_barrier((swapped, chosen[2]))
    near = migrate(near, 2)

    scaled = pl.pallas_call(
        functools.partial(weigh_kernel, experts),
        out_shape=shape(2, tokens.shape[0], 2 * len(back) * STRIDE),
        in_specs=[VMEM, VMEM],
        out_specs=VMEM,
        compiler_params=params(),
        name="weigh",
    )(expert_ids.T, combine.T)
    swapped, scaled = lax.optimization_barrier((swapped, scaled))

    early = pl.pallas_call(
        early_kernel,
        out_shape=shape(3, most, width),
        in_specs=[HBM] * 2,
        out_specs=HBM,
        scratch_shapes=[pltpu.SemaphoreType.DMA((6,))],
        compiler_params=params(),
        name="early",
    )(shared, swapped)
    back, early, straight = lax.optimization_barrier((back, early, straight))

    mixed, filled = pl.pallas_call(
        combine_kernel,
        out_shape=[shape(tokens.shape[0], width), shape(3, most, width)],
        in_specs=[VMEM] * (len(back) + 1) + [HBM] * 2,
        out_specs=[HBM] * 2,
        input_output_aliases={len(back) + 2: 1},
        scratch_shapes=[
            pltpu.VMEM((tokens.shape[0], width), BF16),
            pltpu.SemaphoreType.DMA((5,)),
        ],
        compiler_params=params(),
        cost_estimate=cost(12.3),
        name="combine",
    )(scaled, *back, straight, early)

    arrived = pl.pallas_call(
        late_kernel,
        out_shape=shape(3, most, width),
        in_specs=[HBM] * 3,
        out_specs=HBM,
        input_output_aliases={0: 0},
        scratch_shapes=[pltpu.SemaphoreType.DMA((3,))],
        compiler_params=params(),
        name="late",
    )(filled, near, begun)
    return mixed, arrived


def solution(mesh):
    placed = (
        P(("replica", "expert"), None),
        P(("replica", "expert"), None),
        P(("replica", "expert"), None),
        P("expert", None),
        P("expert", None),
        P("expert", None),
        P(),
    )
    return jax.shard_map(
        on_device,
        mesh=mesh,
        in_specs=placed,
        out_specs=(P(("replica", "expert"), None), P("replica", "expert", None)),
        check_vma=False,
    )
```
